32 devices in a mesh: dp: 2 (over y), expert: 16 (over z, x, core).
Axes of the slice: x: 2, y: 2, z: 4, core: 2. Of those that a mesh axis runs over, the one named last changes fastest.
Arguments:
- activations: bfloat16 [4096, 4096], P(('dp', 'expert')), may hold values from -6 to 6
- cotangent: bfloat16 [4096, 4096], P(('dp', 'expert')), may hold values from -6 to 6
- expert_ids: int32 [4096, 1], P(('dp', 'expert')), may hold values from 0 to 127; in each aligned block of 128 rows (0 to 127, 128 to 255, ...) at most 2 rows name the same one
- gate_probs: float32 [4096, 1], P(('dp', 'expert')), may hold values from 0.2 to 1
- gate_up: bfloat16 [16, 2, 4096, 1536], P('expert', None, None, 'dp'), may hold values from -0.09375 to 0.09375
- down_proj: bfloat16 [16, 1536, 4096], P('expert', 'dp'), may hold values from -0.15625 to 0.15625
Outputs:
- input_grad: bfloat16 [4096, 4096], P(('dp', 'expert'))
- grad_gate_up: bfloat16 [16, 2, 4096, 1536], P('expert', None, None, 'dp')
- grad_down: bfloat16 [16, 1536, 4096], P('expert', 'dp')
The draws below stay inside these ranges and needn't reach their ends.
Inputs may be any that keep to these rules, and one draw needn't show every extreme that they name: `expert_ids`: expert e < 16 is held by index e of the expert axis. Among the 128 tokens of one device no expert is named more than 2 times, a bound that some block reaches.
All inputs are finite; a program needn't handle non-finite values.
Results may differ from the reference program's by a relative error of at most 0.0058.
Values may be sent and summed in bfloat16 or wider, within the bound.
No kernel may reach another device: no remote copies, remote signals or barrier semaphores. Data moves between devices by JAX's collectives and lax.ppermute only.
A program may use at most 128 MiB of HBM per device.

```python
import math
import jax
import jax.numpy as jnp
import numpy as np
from jax import lax

D = 4096
F = 1536
EXPERTS_ALL = 128
TOPK = 1
TOK_DEV = 128
EXPERTS = 16
CAP = 2
TOKENS = 4096
N_DP = 2
N_EXPERT = 16


def block_scale(stream_key, dims, pieces, least, top_value):
    factor_of = 1.0
    for position, shards_of in pieces:
        draws = jax.random.uniform(jax.random.fold_in(jax.random.fold_in(stream_key, 6), position), (shards_of,), jnp.float32, least / len(pieces), top_value / len(pieces))
        factor_of = factor_of * jnp.repeat(jnp.exp(draws), dims[position] // shards_of).reshape((-1,) + (1,) * (len(dims) - 1 - position))
    return factor_of


def deal_out(rng, own, number, rows, amount, top, reach, slope):
    ranking = jax.random.permutation(rng, amount)
    crowded, usual = shares(amount, rows * top, reach, slope, True), shares(amount, rows * top, reach, slope, False)
    places = jnp.arange(amount)

    def named(sizes, turn):
        used = int((sizes > 0).sum())
        fixed = max(1, used // 4)
        moved = fixed + (places - fixed + turn * (used - fixed)) % max(1, amount - fixed)
        return jnp.zeros((amount,), jnp.int32).at[ranking[jnp.where(places < fixed, places, moved)]].set(jnp.asarray(sizes, jnp.int32))

    sizes = jnp.where(number % 4 == 0, named(crowded, number // 4), named(usual, number - number // 4 - 1))
    mixed = jax.random.permutation(jax.random.fold_in(own, 3), amount)
    giver, taker = mixed[0:amount // 2 * 2:2], mixed[1:amount // 2 * 2:2]
    slack = jnp.minimum(sizes[giver] - 1, reach - sizes[taker]) // 2
    slack = jnp.where((giver == ranking[0]) | (taker == ranking[0]) | (sizes[taker] == 0), 0, jnp.maximum(slack, 0))
    moved = jax.random.randint(jax.random.fold_in(own, 4), (amount // 2,), 0, 1 << 20) % (slack + 1)
    sizes = sizes.at[giver].add(-moved).at[taker].add(moved)
    members = jnp.searchsorted(jnp.cumsum(sizes), jnp.arange(rows * top), side="right").astype(jnp.int32)
    table = members.reshape(top, rows).T
    table = table[jax.random.permutation(jax.random.fold_in(own, 1), rows)]
    turn = jax.random.randint(jax.random.fold_in(own, 2), (rows, 1), 0, top)
    return jnp.take_along_axis(table, (jnp.arange(top)[None, :] + turn) % top, axis=1)


def shares(number_of, total, limit, slope, full):
    loads = [(1 << 20) // math.isqrt(grade ** slope) + 1 for grade in range(1, number_of + 1)]
    largest = limit if full else min(limit, max(-(-total // number_of), total * loads[0] // sum(loads)))
    least = 1 if total - largest >= number_of - 1 else 0
    counts, surplus = [largest] + [least] * (number_of - 1), total - largest - least * (number_of - 1)
    while surplus > 0:
        candidates = [i for i in range(1, number_of) if counts[i] < largest] or [i for i in range(1, number_of) if counts[i] < limit]
        whole, left = sum([loads[i] for i in candidates]), surplus
        for i in candidates:
            extra = min(limit - counts[i], max(1, left * loads[i] // whole), surplus)
            counts[i] = counts[i] + extra
            surplus = surplus - extra
    return np.array(counts)


def bell_draw(key, dims, scale, bound, shards=(), held_as=jnp.bfloat16):
    array = jax.random.normal(key, dims, jnp.float32) * scale
    if len(shards) > 0:
        array = block_scale(key, dims, shards, -0.22, 0.18) * array
    return jnp.clip(array, min=-bound, max=bound).astype(held_as)


def setup_inputs(seed: int = 0) -> dict:
    key_of = jax.random.split(jax.random.key(seed), 7)
    activations = bell_draw(key_of[0], (TOKENS, D), 1.0, 6.0, ((0, 32),))
    cotangent = bell_draw(key_of[1], (TOKENS, D), 1.0, 6.0, ((0, 32),))
    expert_ids_keys = jax.random.split(jax.random.fold_in(key_of[2], 1), TOKENS // TOK_DEV)
    expert_ids_turns = jax.random.permutation(jax.random.fold_in(key_of[2], 3), TOKENS // TOK_DEV)
    expert_ids = jax.vmap(lambda own, number: deal_out(jax.random.fold_in(key_of[2], 2), own, number, TOK_DEV, EXPERTS_ALL, TOPK, CAP, 2))(expert_ids_keys, expert_ids_turns).reshape((TOKENS, TOPK))
    gate_probs = jnp.clip(0.2 + 0.8 * jax.random.uniform(key_of[3], (TOKENS, TOPK), jnp.float32) ** block_scale(key_of[3], (TOKENS, TOPK), ((0, 32),), -0.2, 0.2), 0.2, 1.0)
    gate_up = bell_draw(key_of[4], (EXPERTS, 2, D, F), D ** -0.5, 0.09375, ((0, 16), (3, 2)))
    down_proj = bell_draw(key_of[5], (EXPERTS, F, D), F ** -0.5, 0.15625, ((0, 16), (1, 2)))
    return {"activations": activations, "cotangent": cotangent, "expert_ids": expert_ids, "gate_probs": gate_probs, "gate_up": gate_up, "down_proj": down_proj}


def expert_backward(rows_tok, rows_cot, pair_weights, down_weights):
    pre_gate = jnp.dot(rows_tok, pair_weights[0], preferred_element_type=jnp.float32)
    pre_up = jnp.dot(rows_tok, pair_weights[1], preferred_element_type=jnp.float32)
    sigmoid_gate = jax.nn.sigmoid(pre_gate)
    activated = pre_gate * sigmoid_gate
    hidden = (activated * pre_up).astype(jnp.bfloat16)
    hidden_grad = jnp.dot(rows_cot, down_weights.T, preferred_element_type=jnp.float32)
    gate_grad = (hidden_grad * pre_up * sigmoid_gate * (1.0 + pre_gate * (1.0 - sigmoid_gate))).astype(jnp.bfloat16)
    up_grad = (hidden_grad * activated).astype(jnp.bfloat16)
    total_down = jnp.dot(hidden.T, rows_cot, preferred_element_type=jnp.float32)
    total_gate = jnp.dot(rows_tok.T, gate_grad, preferred_element_type=jnp.float32)
    total_up = jnp.dot(rows_tok.T, up_grad, preferred_element_type=jnp.float32)
    input_rows = jnp.dot(gate_grad, pair_weights[0].T, preferred_element_type=jnp.float32)
    input_rows = input_rows + jnp.dot(up_grad, pair_weights[1].T, preferred_element_type=jnp.float32)
    grads_pair = jnp.stack([total_gate, total_up]).astype(jnp.bfloat16)
    return input_rows.astype(jnp.bfloat16), grads_pair, total_down.astype(jnp.bfloat16)


def reference(activations, cotangent, expert_ids, gate_probs, gate_up, down_proj):
    identity = expert_ids[:, 0].astype(jnp.int32)
    rows_most = N_DP * N_EXPERT * CAP
    scaled = (gate_probs * cotangent.astype(jnp.float32)).astype(jnp.bfloat16)

    def one_expert(number):
        ordering = jnp.argsort((identity != number).astype(jnp.int32), stable=True)[:rows_most].astype(jnp.int32)
        chosen = identity[ordering] == number
        rows_tok = activations[ordering]
        rows_cot = jnp.where(chosen[:, None], scaled[ordering], jnp.zeros((), jnp.bfloat16))
        input_rows, grads_pair, grads_down = expert_backward(rows_tok, rows_cot, gate_up[number], down_proj[number])
        return ordering, input_rows, grads_pair, grads_down

    orderings, input_rows, grad_gate_up, grad_down = lax.map(one_expert, jnp.arange(EXPERTS, dtype=jnp.int32))
    input_grad = jnp.zeros((TOKENS, D), jnp.bfloat16).at[orderings.reshape(-1)].add(input_rows.reshape(-1, D))
    return input_grad, grad_gate_up, grad_down
```

```python
import functools

import jax
import jax.numpy as jnp
from jax import lax
from jax.experimental import pallas as pl
from jax.experimental.pallas import tpu as pltpu
from jax.sharding import PartitionSpec as P

CAP = 2
MIB = 1024 * 1024


def dot_nn(a, b):
    return lax.dot_general(a, b, (((1,), (0,)), ((), ())), preferred_element_type=jnp.float32)


def dot_nt(a, b):
    return lax.dot_general(a, b, (((1,), (1,)), ((), ())), preferred_element_type=jnp.float32)


def dot_tn(a, b):
    return lax.dot_general(a, b, (((0,), (0,)), ((), ())), preferred_element_type=jnp.float32)


def cost(flops, moved):
    return pl.CostEstimate(flops=int(flops), bytes_accessed=int(moved), transcendentals=0)


def route_kernel(experts, ids_ref, probs_ref, act_ref, cot_ref, send_ref, place_ref):
    ids = ids_ref[...]
    tokens = ids.shape[1]
    units = lax.broadcasted_iota(jnp.int32, (experts, tokens), 0)
    onehot = jnp.where(units == ids, 1.0, 0.0)
    earlier = lax.broadcasted_iota(jnp.int32, (tokens, tokens), 0) < lax.broadcasted_iota(
        jnp.int32, (tokens, tokens), 1
    )
    before = dot_nn(onehot.astype(jnp.bfloat16), jnp.where(earlier, 1.0, 0.0).astype(jnp.bfloat16))
    rank = jnp.sum(before * onehot, axis=0, keepdims=True).astype(jnp.int32)
    inside = ids < experts
    slot = jnp.where(inside, ids * CAP + rank, -1)
    slots = lax.broadcasted_iota(jnp.int32, (experts * CAP, tokens), 0)
    place_ref[...] = jnp.where(slots == slot, 1.0, 0.0).astype(jnp.bfloat16)
    wide = lax.broadcasted_iota(jnp.int32, (experts * 2 * CAP, tokens), 0)
    row = jnp.where(inside, ids * (2 * CAP) + rank, -2 * CAP)
    pick_tok = jnp.where(wide == row, 1.0, 0.0)
    pick_cot = jnp.where(wide == row + CAP, 1.0, 0.0)
    weight = jnp.sum(pick_cot * probs_ref[...], axis=1, keepdims=True)
    rows = dot_nn(pick_tok.astype(jnp.bfloat16), act_ref[...])
    rows = rows + weight * dot_nn(pick_cot.astype(jnp.bfloat16), cot_ref[...])
    rows = rows.astype(jnp.bfloat16)
    for unit in range(experts):
        send_ref[unit] = rows[unit * 2 * CAP : (unit + 1) * 2 * CAP]


def route(ids, probs, act, cot, experts):
    tokens, width = act.shape
    tile = min(1024, width)
    return pl.pallas_call(
        functools.partial(route_kernel, experts),
        grid=(width // tile,),
        in_specs=[
            pl.BlockSpec((1, tokens), lambda c: (0, 0)),
            pl.BlockSpec((1, tokens), lambda c: (0, 0)),
            pl.BlockSpec((tokens, tile), lambda c: (0, c)),
            pl.BlockSpec((tokens, tile), lambda c: (0, c)),
        ],
        out_specs=[
            pl.BlockSpec((experts, 2 * CAP, tile), lambda c: (0, 0, c)),
            pl.BlockSpec((experts * CAP, tokens), lambda c: (0, 0)),
        ],
        out_shape=[
            jax.ShapeDtypeStruct((experts, 2 * CAP, width), jnp.bfloat16),
            jax.ShapeDtypeStruct((experts * CAP, tokens), jnp.bfloat16),
        ],
        compiler_params=pltpu.CompilerParams(vmem_limit_bytes=16 * MIB),
        cost_estimate=cost(4 * experts * CAP * tokens * width, 4 * tokens * width),
        name="route_rows",
    )(ids, probs, act, cot)


def expert_kernel(groups, chunk, *refs):
    toks, cots = refs[:groups], refs[groups : 2 * groups]
    pair_hbm, down_hbm = refs[2 * groups : 2 * groups + 2]
    gate_out, up_out, hidden_out = refs[2 * groups + 2 : 2 * groups + 5]
    parts = refs[2 * groups + 5 : 3 * groups + 5]
    pair, down, tok_all, cot_all, acc_gate, acc_up, acc_hid, sems = refs[3 * groups + 5 :]
    rows, width = toks[0].shape
    steps = width // chunk

    def copies(step):
        at = pl.ds(step * chunk, chunk)
        return (
            pltpu.make_async_copy(pair_hbm.at[:, at, :], pair.at[:, at, :], sems.at[0, step]),
            pltpu.make_async_copy(down_hbm.at[:, at], down.at[:, at], sems.at[1, step]),
        )

    for step in range(steps):
        for one in copies(step):
            one.start()
    for group in range(groups):
        tok_all[group * rows : (group + 1) * rows, :] = toks[group][...]
        cot_all[group * rows : (group + 1) * rows, :] = cots[group][...]
    acc_gate[...] = jnp.zeros_like(acc_gate)
    acc_up[...] = jnp.zeros_like(acc_up)
    acc_hid[...] = jnp.zeros_like(acc_hid)

    for step in range(steps):
        at = slice(step * chunk, (step + 1) * chunk)
        for one in copies(step):
            one.wait()
        acc_gate[...] += dot_nn(tok_all[:, at], pair[0, at, :])
        acc_up[...] += dot_nn(tok_all[:, at], pair[1, at, :])
        acc_hid[...] += dot_nt(cot_all[:, at], down[:, at])

    pre_gate, pre_up, hidden_grad = acc_gate[...], acc_up[...], acc_hid[...]
    sigmoid_gate = jax.nn.sigmoid(pre_gate)
    activated = pre_gate * sigmoid_gate
    hidden_out[...] = (activated * pre_up).astype(jnp.bfloat16)
    gate_grad = (
        hidden_grad * pre_up * sigmoid_gate * (1.0 + pre_gate * (1.0 - sigmoid_gate))
    ).astype(jnp.bfloat16)
    up_grad = (hidden_grad * activated).astype(jnp.bfloat16)
    gate_out[...] = gate_grad
    up_out[...] = up_grad
    for step in range(steps):
        at = slice(step * chunk, (step + 1) * chunk)
        value = dot_nt(gate_grad, pair[0, at, :]) + dot_nt(up_grad, pair[1, at, :])
        for group in range(groups):
            parts[group][:, at] = value[group * rows : (group + 1) * rows].astype(
                parts[group].dtype
            )


def expert_rows(toks, cots, pair, down):
    groups = len(toks)
    rows, width = toks[0].shape
    units = down.shape[0]
    chunk = min(512, width)
    total = groups * rows
    whole = pl.BlockSpec(memory_space=pltpu.VMEM)
    out_shape = [jax.ShapeDtypeStruct((total, units), jnp.bfloat16)] * 3
    out_shape += [
        jax.ShapeDtypeStruct((rows, width), jnp.float32 if group == 0 else jnp.bfloat16)
        for group in range(groups)
    ]
    out = pl.pallas_call(
        functools.partial(expert_kernel, groups, chunk),
        in_specs=[whole] * (2 * groups) + [pl.BlockSpec(memory_space=pl.ANY)] * 2,
        out_specs=[whole] * len(out_shape),
        out_shape=out_shape,
        scratch_shapes=[
            pltpu.VMEM(pair.shape, jnp.bfloat16),
            pltpu.VMEM(down.shape, jnp.bfloat16),
            pltpu.VMEM((total, width), jnp.bfloat16),
            pltpu.VMEM((total, width), jnp.bfloat16),
            pltpu.VMEM((total, units), jnp.float32),
            pltpu.VMEM((total, units), jnp.float32),
            pltpu.VMEM((total, units), jnp.float32),
            pltpu.SemaphoreType.DMA((2, width // chunk)),
        ],
        compiler_params=pltpu.CompilerParams(vmem_limit_bytes=48 * MIB),
        cost_estimate=cost(10 * total * width * units, 6 * width * units),
        name="expert_rows",
    )(*toks, *cots, pair, down)
    return out[0], out[1], out[2], out[3:]


def pair_grad_kernel(groups, *refs):
    gate_ref, up_ref = refs[groups : groups + 2]
    out_ref = refs[groups + 2]
    tok = jnp.concatenate([ref[...] for ref in refs[:groups]], axis=0)
    out_ref[0, 0] = dot_tn(tok, gate_ref[...]).astype(jnp.bfloat16)
    out_ref[0, 1] = dot_tn(tok, up_ref[...]).astype(jnp.bfloat16)


def pair_grad(toks, gate_grad, up_grad):
    groups = len(toks)
    rows, width = toks[0].shape
    total, units = gate_grad.shape
    tile = min(512, width)
    return pl.pallas_call(
        functools.partial(pair_grad_kernel, groups),
        grid=(width // tile,),
        in_specs=[pl.BlockSpec((rows, tile), lambda c: (0, c))] * groups
        + [pl.BlockSpec((total, units), lambda c: (0, 0))] * 2,
        out_specs=pl.BlockSpec((1, 2, tile, units), lambda c: (0, 0, c, 0)),
        out_shape=jax.ShapeDtypeStruct((1, 2, width, units), jnp.bfloat16),
        compiler_params=pltpu.CompilerParams(vmem_limit_bytes=24 * MIB),
        cost_estimate=cost(4 * total * width * units, 4 * width * units),
        name="pair_grad",
    )(*toks, gate_grad, up_grad)


def down_grad_kernel(groups, *refs):
    hidden_ref, out_ref = refs[groups], refs[groups + 1]
    cot = jnp.concatenate([ref[...] for ref in refs[:groups]], axis=0)
    out_ref[0] = dot_tn(hidden_ref[...], cot).astype(jnp.bfloat16)


def down_grad(cots, hidden):
    groups = len(cots)
    rows, width = cots[0].shape
    total, units = hidden.shape
    tile = min(512, width)
    return pl.pallas_call(
        functools.partial(down_grad_kernel, groups),
        grid=(width // tile,),
        in_specs=[pl.BlockSpec((rows, tile), lambda c: (0, c))] * groups
        + [pl.BlockSpec((total, units), lambda c: (0, 0))],
        out_specs=pl.BlockSpec((1, units, tile), lambda c: (0, 0, c)),
        out_shape=jax.ShapeDtypeStruct((1, units, width), jnp.bfloat16),
        compiler_params=pltpu.CompilerParams(vmem_limit_bytes=24 * MIB),
        cost_estimate=cost(2 * total * width * units, 2 * width * units),
        name="down_grad",
    )(*cots, hidden)


def per_device(activations, cotangent, expert_ids, gate_probs, gate_up, down_proj):
    experts = lax.axis_size("expert")
    groups = lax.axis_size("dp")
    tokens, width = activations.shape
    send, place = route(
        expert_ids.reshape(1, tokens), gate_probs.reshape(1, tokens), activations, cotangent, experts
    )
    got = lax.all_to_all(send, "expert", split_axis=0, concat_axis=0, tiled=True)
    own_tok = got[:, :CAP].reshape(experts * CAP, width)
    own_cot = got[:, CAP:].reshape(experts * CAP, width)

    def shift(value, by):
        return lax.ppermute(value, "dp", [(i, (i + by) % groups) for i in range(groups)])

    toks = [own_tok] + [shift(own_tok, by) for by in range(1, groups)]
    cots = [own_cot] + [shift(own_cot, by) for by in range(1, groups)]
    gate_grad, up_grad, hidden, parts = expert_rows(toks, cots, gate_up[0], down_proj[0])
    summed = parts[0]
    for by in range(1, groups):
        summed = summed + shift(parts[by], -by).astype(jnp.float32)
    rounded = summed.astype(jnp.bfloat16).reshape(experts, CAP, width)
    returned = lax.all_to_all(rounded, "expert", split_axis=0, concat_axis=0, tiled=True)
    pair_total = pair_grad(toks, gate_grad, up_grad)
    down_total = down_grad(cots, hidden)
    input_grad = dot_tn(place, returned.reshape(experts * CAP, width)).astype(jnp.bfloat16)
    return input_grad, pair_total, down_total


def solution(mesh):
    rows = P(("dp", "expert"), None)
    pair, down = P("expert", None, None, "dp"), P("expert", "dp", None)
    return jax.shard_map(
        per_device,
        mesh=mesh,
        in_specs=(rows, rows, rows, rows, pair, down),
        out_specs=(rows, pair, down),
        check_vma=False,
    )
```

```python
import functools

import jax
import jax.numpy as jnp
from jax import lax
from jax.experimental import pallas as pl
from jax.experimental.pallas import tpu as pltpu
from jax.sharding import PartitionSpec as P

CAP = 2
MIB = 1024 * 1024
VMEM = pl.BlockSpec(memory_space=pltpu.VMEM)
HBM = pl.BlockSpec(memory_space=pltpu.HBM)


def dot_nn(a, b):
    return lax.dot_general(a, b, (((1,), (0,)), ((), ())), preferred_element_type=jnp.float32)


def dot_nt(a, b):
    return lax.dot_general(a, b, (((1,), (1,)), ((), ())), preferred_element_type=jnp.float32)


def dot_tn(a, b):
    return lax.dot_general(a, b, (((0,), (0,)), ((), ())), preferred_element_type=jnp.float32)


def cost(flops, moved):
    return pl.CostEstimate(flops=int(flops), bytes_accessed=int(moved), transcendentals=0)


def params(mib):
    return pltpu.CompilerParams(vmem_limit_bytes=mib * MIB)


def bf16(*shape):
    return jax.ShapeDtypeStruct(shape, jnp.bfloat16)


def route_kernel(experts, chunk, ids_hbm, probs_hbm, act_hbm, cot_hbm, *refs):
    pieces, place_ref = refs[:experts], refs[experts]
    ids_ref, probs_ref, act, cot, sems = refs[experts + 1 :]
    tokens, width = act.shape
    steps = width // chunk
    small = (
        pltpu.make_async_copy(ids_hbm, ids_ref, sems.at[2 * steps]),
        pltpu.make_async_copy(probs_hbm, probs_ref, sems.at[2 * steps + 1]),
    )
    large = []
    for step in range(steps):
        at = pl.ds(step * chunk, chunk)
        large.append(
            (
                pltpu.make_async_copy(act_hbm.at[:, at], act.at[:, at], sems.at[2 * step]),
                pltpu.make_async_copy(cot_hbm.at[:, at], cot.at[:, at], sems.at[2 * step + 1]),
            )
        )
    for one in small:
        one.start()
    for pair in large:
        for one in pair:
            one.start()
    for one in small:
        one.wait()

    me = lax.axis_index("expert")
    ids = ids_ref[...]
    inside = ids < experts
    near = jnp.where(inside, ids ^ me, -CAP)
    units = lax.broadcasted_iota(jnp.int32, (experts, tokens), 0)
    onehot = jnp.where(units == near, 1.0, 0.0)
    earlier = lax.broadcasted_iota(jnp.int32, (tokens, tokens), 0) < lax.broadcasted_iota(
        jnp.int32, (tokens, tokens), 1
    )
    before = dot_nn(onehot.astype(jnp.bfloat16), jnp.where(earlier, 1.0, 0.0).astype(jnp.bfloat16))
    rank = jnp.sum(before * onehot, axis=0, keepdims=True).astype(jnp.int32)
    slots = lax.broadcasted_iota(jnp.int32, (experts * CAP, tokens), 0)
    place_ref[...] = jnp.where(slots == near * CAP + rank, 1.0, 0.0).astype(jnp.bfloat16)
    wide = lax.broadcasted_iota(jnp.int32, (experts * 2 * CAP, tokens), 0)
    row = near * (2 * CAP) + rank
    pick_tok = jnp.where(wide == row, 1.0, 0.0)
    pick_cot = jnp.where(wide == row + CAP, 1.0, 0.0)
    pick_cot = jnp.where(inside, pick_cot, 0.0)
    weight = jnp.sum(pick_cot * probs_ref[...], axis=1, keepdims=True)
    pick_tok, pick_cot = pick_tok.astype(jnp.bfloat16), pick_cot.astype(jnp.bfloat16)
    for step in range(steps):
        at = slice(step * chunk, (step + 1) * chunk)
        for one in large[step]:
            one.wait()
        rows = dot_nn(pick_tok, act[:, at]) + weight * dot_nn(pick_cot, cot[:, at])
        rows = rows.astype(jnp.bfloat16)
        for unit in range(experts):
            pieces[unit][:, at] = rows[unit * 2 * CAP : (unit + 1) * 2 * CAP]


def route(ids, probs, act, cot, experts):
    tokens, width = act.shape
    chunk = min(1024, width)
    out = pl.pallas_call(
        functools.partial(route_kernel, experts, chunk),
        in_specs=[HBM] * 4,
        out_specs=[VMEM] * (experts + 1),
        out_shape=[bf16(2 * CAP, width)] * experts + [bf16(experts * CAP, tokens)],
        scratch_shapes=[
            pltpu.VMEM((1, tokens), jnp.int32),
            pltpu.VMEM((1, tokens), jnp.float32),
            pltpu.VMEM((tokens, width), jnp.bfloat16),
            pltpu.VMEM((tokens, width), jnp.bfloat16),
            pltpu.SemaphoreType.DMA((2 * (width // chunk) + 2,)),
        ],
        compiler_params=params(16),
        cost_estimate=cost(4 * experts * CAP * tokens * width, 4 * tokens * width),
        name="route_rows",
    )(ids, probs, act, cot)
    return out[:experts], out[experts]


def merge_kernel(number, *refs):
    pieces, tok, cot = refs[:number], refs[number], refs[number + 1]
    tok[...] = jnp.concatenate([piece[:CAP, :] for piece in pieces], axis=0)
    cot[...] = jnp.concatenate([piece[CAP:, :] for piece in pieces], axis=0)


def merge(pieces):
    number, width = len(pieces), pieces[0].shape[1]
    return pl.pallas_call(
        functools.partial(merge_kernel, number),
        in_specs=[VMEM] * number,
        out_specs=[VMEM] * 2,
        out_shape=[bf16(number * CAP, width)] * 2,
        compiler_params=params(16),
        cost_estimate=cost(0, 8 * number * CAP * width),
        name="merge_rows",
    )(*pieces)


def expert_kernel(blocks, groups, chunk, *refs):
    toks, cots = refs[:blocks], refs[blocks : 2 * blocks]
    pair_hbm, down_hbm = refs[2 * blocks : 2 * blocks + 2]
    gate_out, up_out, hidden_out = refs[2 * blocks + 2 : 2 * blocks + 5]
    parts = refs[2 * blocks + 5 : 3 * blocks + 5]
    pair, down, tok_all, cot_all, acc_gate, acc_up, acc_hid, sems = refs[3 * blocks + 5 :]
    rows, width = toks[0].shape
    steps = width // chunk

    def copies(step):
        at = pl.ds(step * chunk, chunk)
        return (
            pltpu.make_async_copy(pair_hbm.at[:, at, :], pair.at[:, at, :], sems.at[0, step]),
            pltpu.make_async_copy(down_hbm.at[:, at], down.at[:, at], sems.at[1, step]),
        )

    for step in range(steps):
        for one in copies(step):
            one.start()
    for block in range(blocks):
        tok_all[block * rows : (block + 1) * rows, :] = toks[block][...]
        cot_all[block * rows : (block + 1) * rows, :] = cots[block][...]
    acc_gate[...] = jnp.zeros_like(acc_gate)
    acc_up[...] = jnp.zeros_like(acc_up)
    acc_hid[...] = jnp.zeros_like(acc_hid)

    for step in range(steps):
        at = slice(step * chunk, (step + 1) * chunk)
        for one in copies(step):
            one.wait()
        acc_gate[...] += dot_nn(tok_all[:, at], pair[0, at, :])
        acc_up[...] += dot_nn(tok_all[:, at], pair[1, at, :])
        acc_hid[...] += dot_nt(cot_all[:, at], down[:, at])

    pre_gate, pre_up, hidden_grad = acc_gate[...], acc_up[...], acc_hid[...]
    sigmoid_gate = jax.nn.sigmoid(pre_gate)
    activated = pre_gate * sigmoid_gate
    hidden_out[...] = (activated * pre_up).astype(jnp.bfloat16)
    gate_grad = (
        hidden_grad * pre_up * sigmoid_gate * (1.0 + pre_gate * (1.0 - sigmoid_gate))
    ).astype(jnp.bfloat16)
    up_grad = (hidden_grad * activated).astype(jnp.bfloat16)
    gate_out[...] = gate_grad
    up_out[...] = up_grad
    for step in range(steps):
        at = slice(step * chunk, (step + 1) * chunk)
        value = dot_nt(gate_grad, pair[0, at, :]) + dot_nt(up_grad, pair[1, at, :])
        for block in range(blocks):
            parts[block][:, at] = value[block * rows : (block + 1) * rows].astype(
                parts[block].dtype
            )


def expert_rows(toks, cots, pair, down, groups):
    blocks = len(toks)
    rows, width = toks[0].shape
    units = down.shape[0]
    chunk = min(512, width)
    total = blocks * rows
    out_shape = [bf16(total, units)] * 3
    out_shape += [
        jax.ShapeDtypeStruct((rows, width), jnp.float32 if block < blocks // groups else jnp.bfloat16)
        for block in range(blocks)
    ]
    out = pl.pallas_call(
        functools.partial(expert_kernel, blocks, groups, chunk),
        in_specs=[VMEM] * (2 * blocks) + [HBM] * 2,
        out_specs=[VMEM] * len(out_shape),
        out_shape=out_shape,
        scratch_shapes=[
            pltpu.VMEM(pair.shape, jnp.bfloat16),
            pltpu.VMEM(down.shape, jnp.bfloat16),
            pltpu.VMEM((total, width), jnp.bfloat16),
            pltpu.VMEM((total, width), jnp.bfloat16),
            pltpu.VMEM((total, units), jnp.float32),
            pltpu.VMEM((total, units), jnp.float32),
            pltpu.VMEM((total, units), jnp.float32),
            pltpu.SemaphoreType.DMA((2, width // chunk)),
        ],
        compiler_params=params(44),
        cost_estimate=cost(10 * total * width * units, 6 * width * units),
        name="expert_rows",
    )(*toks, *cots, pair, down)
    return out[0], out[1], out[2], out[3:]


def add_kernel(own, other_refs, pieces):
    total = own[...]
    for other in other_refs:
        total = total + other[...].astype(jnp.float32)
    total = total.astype(jnp.bfloat16)
    for index, piece in enumerate(pieces):
        piece[...] = total[index * CAP : (index + 1) * CAP]


def add_parts(own, others):
    rows, width = own.shape
    number = rows // CAP
    count = len(others)

    def body(*refs):
        add_kernel(refs[0], refs[1 : 1 + count], refs[1 + count :])

    return pl.pallas_call(
        body,
        in_specs=[VMEM] * (1 + count),
        out_specs=[VMEM] * number,
        out_shape=[bf16(CAP, width)] * number,
        compiler_params=params(16),
        cost_estimate=cost(rows * width, 8 * rows * width),
        name="add_parts",
    )(own, *others)


def pair_grad_kernel(blocks, chunk, *refs):
    toks, gate_ref, up_ref, out_hbm = refs[:blocks], refs[blocks], refs[blocks + 1], refs[blocks + 2]
    buffer, sems = refs[blocks + 3 :]
    width = toks[0].shape[1]
    copies = []
    for step in range(width // chunk):
        at = slice(step * chunk, (step + 1) * chunk)
        tok = jnp.concatenate([ref[:, at] for ref in toks], axis=0)
        for side, ref in enumerate((gate_ref, up_ref)):
            buffer[side, at, :] = dot_tn(tok, ref[...]).astype(jnp.bfloat16)
        where = pl.ds(step * chunk, chunk)
        one = pltpu.make_async_copy(
            buffer.at[:, where, :], out_hbm.at[0, :, where, :], sems.at[step]
        )
        one.start()
        copies.append(one)
    for one in copies:
        one.wait()


def pair_grad(toks, gate_grad, up_grad):
    blocks = len(toks)
    width = toks[0].shape[1]
    total, units = gate_grad.shape
    chunk = min(512, width)
    return pl.pallas_call(
        functools.partial(pair_grad_kernel, blocks, chunk),
        in_specs=[VMEM] * (blocks + 2),
        out_specs=HBM,
        out_shape=bf16(1, 2, width, units),
        scratch_shapes=[
            pltpu.VMEM((2, width, units), jnp.bfloat16),
            pltpu.SemaphoreType.DMA((width // chunk,)),
        ],
        compiler_params=params(32),
        cost_estimate=cost(4 * total * width * units, 4 * width * units),
        name="pair_grad",
    )(*toks, gate_grad, up_grad)


def down_grad_kernel(blocks, chunk, *refs):
    cots, hidden_ref, out_hbm = refs[:blocks], refs[blocks], refs[blocks + 1]
    buffer, sems = refs[blocks + 2 :]
    width = cots[0].shape[1]
    copies = []
    for step in range(width // chunk):
        at = slice(step * chunk, (step + 1) * chunk)
        cot = jnp.concatenate([ref[:, at] for ref in cots], axis=0)
        buffer[:, at] = dot_tn(hidden_ref[...], cot).astype(jnp.bfloat16)
        where = pl.ds(step * chunk, chunk)
        one = pltpu.make_async_copy(buffer.at[:, where], out_hbm.at[0, :, where], sems.at[step])
        one.start()
        copies.append(one)
    for one in copies:
        one.wait()


def down_grad(cots, hidden):
    blocks = len(cots)
    width = cots[0].shape[1]
    total, units = hidden.shape
    chunk = min(1024, width)
    return pl.pallas_call(
        functools.partial(down_grad_kernel, blocks, chunk),
        in_specs=[VMEM] * (blocks + 1),
        out_specs=HBM,
        out_shape=bf16(1, units, width),
        scratch_shapes=[
            pltpu.VMEM((units, width), jnp.bfloat16),
            pltpu.SemaphoreType.DMA((width // chunk,)),
        ],
        compiler_params=params(24),
        cost_estimate=cost(2 * total * width * units, 2 * width * units),
        name="down_grad",
    )(*cots, hidden)


def spread_kernel(number, chunk, *refs):
    pieces, place_ref, out_hbm = refs[:number], refs[number], refs[number + 1]
    buffer, sems = refs[number + 2 :]
    width = pieces[0].shape[1]
    place = place_ref[...]
    copies = []
    for step in range(width // chunk):
        at = slice(step * chunk, (step + 1) * chunk)
        rows = jnp.concatenate([piece[:, at] for piece in pieces], axis=0)
        buffer[:, at] = dot_tn(place, rows).astype(jnp.bfloat16)
        where = pl.ds(step * chunk, chunk)
        one = pltpu.make_async_copy(buffer.at[:, where], out_hbm.at[:, where], sems.at[step])
        one.start()
        copies.append(one)
    for one in copies:
        one.wait()


def spread(pieces, place):
    number, width = len(pieces), pieces[0].shape[1]
    tokens = place.shape[1]
    chunk = min(1024, width)
    return pl.pallas_call(
        functools.partial(spread_kernel, number, chunk),
        in_specs=[VMEM] * (number + 1),
        out_specs=HBM,
        out_shape=bf16(tokens, width),
        scratch_shapes=[
            pltpu.VMEM((tokens, width), jnp.bfloat16),
            pltpu.SemaphoreType.DMA((width // chunk,)),
        ],
        compiler_params=params(16),
        cost_estimate=cost(2 * number * CAP * tokens * width, 2 * tokens * width),
        name="spread_rows",
    )(*pieces, place)


def per_device(activations, cotangent, expert_ids, gate_probs, gate_up, down_proj):
    experts = lax.axis_size("expert")
    groups = lax.axis_size("dp")
    tokens = activations.shape[0]
    batch = min(8, experts)
    batches = experts // batch

    def swap(value, by):
        if by == 0:
            return value
        return lax.ppermute(value, "expert", [(i, i ^ by) for i in range(experts)])

    def shift(value, by):
        return lax.ppermute(value, "dp", [(i, (i + by) % groups) for i in range(groups)])

    pieces, place = route(
        expert_ids.reshape(1, tokens), gate_probs.reshape(1, tokens), activations, cotangent, experts
    )
    got = [swap(pieces[by], by) for by in range(experts)]
    own = [merge(got[batch * i : batch * (i + 1)]) for i in range(batches)]
    toks, cots = [one[0] for one in own], [one[1] for one in own]
    for by in range(1, groups):
        toks = toks + [shift(own[i][0], by) for i in range(batches)]
        cots = cots + [shift(own[i][1], by) for i in range(batches)]
    gate_grad, up_grad, hidden, parts = expert_rows(toks, cots, gate_up[0], down_proj[0], groups)
    others = [
        [shift(parts[by * batches + i], -by) for by in range(1, groups)] for i in range(batches)
    ]
    down_total = down_grad(cots, hidden)
    back = []
    for i in range(batches):
        back += add_parts(parts[i], others[i])
    returned = [swap(back[by], by) for by in range(experts)]
    pair_total = pair_grad(toks, gate_grad, up_grad)
    input_grad = spread(returned, place)
    return input_grad, pair_total, down_total


def solution(mesh):
    rows = P(("dp", "expert"), None)
    pair, down = P("expert", None, None, "dp"), P("expert", "dp", None)
    return jax.shard_map(
        per_device,
        mesh=mesh,
        in_specs=(rows, rows, rows, rows, pair, down),
        out_specs=(rows, pair, down),
        check_vma=False,
    )
```

```python
import functools

import jax
import jax.numpy as jnp
from jax import lax
from jax.experimental import pallas as pl
from jax.experimental.pallas import tpu as pltpu
from jax.sharding import PartitionSpec as P

CAP = 2
MIB = 1024 * 1024
VMEM = pl.BlockSpec(memory_space=pltpu.VMEM)
HBM = pl.BlockSpec(memory_space=pltpu.HBM)


def dot_nn(a, b):
    return lax.dot_general(a, b, (((1,), (0,)), ((), ())), preferred_element_type=jnp.float32)


def dot_nt(a, b):
    return lax.dot_general(a, b, (((1,), (1,)), ((), ())), preferred_element_type=jnp.float32)


def dot_tn(a, b):
    return lax.dot_general(a, b, (((0,), (0,)), ((), ())), preferred_element_type=jnp.float32)


def cost(flops, moved):
    return pl.CostEstimate(flops=int(flops), bytes_accessed=int(moved), transcendentals=0)


def params(mib):
    return pltpu.CompilerParams(vmem_limit_bytes=mib * MIB)


def in_hbm(value):
    return pltpu.with_memory_space_constraint(value, pltpu.HBM)


def bf16(*shape):
    return jax.ShapeDtypeStruct(shape, jnp.bfloat16)


def route_kernel(experts, chunk, ids_hbm, probs_hbm, act_hbm, cot_hbm, *refs):
    send_tok, send_cot, place_ref, ids_ref, probs_ref, act, cot, sems = refs
    tokens, width = act.shape
    steps = width // chunk
    small = (
        pltpu.make_async_copy(ids_hbm, ids_ref, sems.at[2 * steps]),
        pltpu.make_async_copy(probs_hbm, probs_ref, sems.at[2 * steps + 1]),
    )
    large = []
    for step in range(steps):
        at = pl.ds(step * chunk, chunk)
        large.append(
            (
                pltpu.make_async_copy(act_hbm.at[:, at], act.at[:, at], sems.at[2 * step]),
                pltpu.make_async_copy(cot_hbm.at[:, at], cot.at[:, at], sems.at[2 * step + 1]),
            )
        )
    for one in small:
        one.start()
    for pair in large:
        for one in pair:
            one.start()
    for one in small:
        one.wait()

    ids = ids_ref[...]
    inside = ids < experts
    near = jnp.where(inside, ids, -CAP)
    units = lax.broadcasted_iota(jnp.int32, (experts, tokens), 0)
    onehot = jnp.where(units == near, 1.0, 0.0)
    earlier = lax.broadcasted_iota(jnp.int32, (tokens, tokens), 0) < lax.broadcasted_iota(
        jnp.int32, (tokens, tokens), 1
    )
    before = dot_nn(onehot.astype(jnp.bfloat16), jnp.where(earlier, 1.0, 0.0).astype(jnp.bfloat16))
    rank = jnp.sum(before * onehot, axis=0, keepdims=True).astype(jnp.int32)
    slots = lax.broadcasted_iota(jnp.int32, (experts * CAP, tokens), 0)
    place = jnp.where(slots == near * CAP + rank, 1.0, 0.0)
    weight = jnp.sum(place * probs_ref[...], axis=1, keepdims=True)
    place = place.astype(jnp.bfloat16)
    place_ref[...] = place
    for step in range(steps):
        at = slice(step * chunk, (step + 1) * chunk)
        for one in large[step]:
            one.wait()
        rows_tok = dot_nn(place, act[:, at]).astype(jnp.bfloat16)
        rows_cot = (weight * dot_nn(place, cot[:, at])).astype(jnp.bfloat16)
        for unit in range(experts):
            send_tok[unit, :, at] = rows_tok[unit * CAP : (unit + 1) * CAP]
            send_cot[unit, :, at] = rows_cot[unit * CAP : (unit + 1) * CAP]


def route(ids, probs, act, cot, experts):
    tokens, width = act.shape
    chunk = min(1024, width)
    return pl.pallas_call(
        functools.partial(route_kernel, experts, chunk),
        in_specs=[HBM] * 4,
        out_specs=[VMEM] * 3,
        out_shape=[bf16(experts, CAP, width)] * 2 + [bf16(experts * CAP, tokens)],
        scratch_shapes=[
            pltpu.VMEM((1, tokens), jnp.int32),
            pltpu.VMEM((1, tokens), jnp.float32),
            pltpu.VMEM((tokens, width), jnp.bfloat16),
            pltpu.VMEM((tokens, width), jnp.bfloat16),
            pltpu.SemaphoreType.DMA((2 * (width // chunk) + 2,)),
        ],
        compiler_params=params(16),
        cost_estimate=cost(4 * experts * CAP * tokens * width, 4 * tokens * width),
        name="route_rows",
    )(in_hbm(ids), in_hbm(probs), in_hbm(act), in_hbm(cot))


def forward_kernel(groups, chunk, *refs):
    toks, pair_hbm, down_hbm = refs[:groups], refs[groups], refs[groups + 1]
    gate_out, up_out, pair, down, tok_all, sems = refs[groups + 3 :]
    rows, width = toks[0].shape
    steps = width // chunk
    pairs, downs = [], []
    for step in range(steps):
        at = pl.ds(step * chunk, chunk)
        pairs.append(
            pltpu.make_async_copy(pair_hbm.at[:, at, :], pair.at[:, at, :], sems.at[0, step])
        )
        downs.append(pltpu.make_async_copy(down_hbm.at[:, at], down.at[:, at], sems.at[1, step]))
    for one in pairs + downs:
        one.start()
    for group in range(groups):
        tok_all[group * rows : (group + 1) * rows, :] = toks[group][...]
    gate_out[...] = jnp.zeros_like(gate_out)
    up_out[...] = jnp.zeros_like(up_out)
    for step in range(steps):
        at = slice(step * chunk, (step + 1) * chunk)
        pairs[step].wait()
        gate_out[...] += dot_nn(tok_all[:, at], pair[0, at, :])
        up_out[...] += dot_nn(tok_all[:, at], pair[1, at, :])
    for one in downs:
        one.wait()


def forward(toks, pair, down, after):
    groups = len(toks)
    rows, width = toks[0].shape
    units = down.shape[0]
    chunk = min(512, width)
    total = groups * rows
    return pl.pallas_call(
        functools.partial(forward_kernel, groups, chunk),
        in_specs=[VMEM] * groups + [HBM] * 2 + [pl.BlockSpec(memory_space=pl.ANY)],
        out_specs=[VMEM] * 4,
        out_shape=[
            jax.ShapeDtypeStruct((total, units), jnp.float32),
            jax.ShapeDtypeStruct((total, units), jnp.float32),
            pltpu.VMEM(pair.shape, jnp.bfloat16),
            pltpu.VMEM(down.shape, jnp.bfloat16),
        ],
        scratch_shapes=[
            pltpu.VMEM((total, width), jnp.bfloat16),
            pltpu.SemaphoreType.DMA((2, width // chunk)),
        ],
        compiler_params=params(28),
        cost_estimate=cost(4 * total * width * units, 6 * width * units),
        name="forward_rows",
    )(*toks, in_hbm(pair), in_hbm(down), after)


def backward_kernel(groups, chunk, *refs):
    cots, pre_gate_ref, pre_up_ref = refs[:groups], refs[groups], refs[groups + 1]
    pair, down = refs[groups + 2 : groups + 4]
    gate_out, up_out, hidden_out = refs[groups + 4 : groups + 7]
    parts, acc = refs[groups + 7 : 2 * groups + 7], refs[2 * groups + 7]
    rows, width = cots[0].shape
    steps = width // chunk
    for step in range(steps):
        at = slice(step * chunk, (step + 1) * chunk)
        cot = jnp.concatenate([ref[:, at] for ref in cots], axis=0)
        value = dot_nt(cot, down[:, at])
        acc[...] = value if step == 0 else acc[...] + value
    pre_gate, pre_up, hidden_grad = pre_gate_ref[...], pre_up_ref[...], acc[...]
    sigmoid_gate = jax.nn.sigmoid(pre_gate)
    activated = pre_gate * sigmoid_gate
    hidden_out[...] = (activated * pre_up).astype(jnp.bfloat16)
    gate_grad = (
        hidden_grad * pre_up * sigmoid_gate * (1.0 + pre_gate * (1.0 - sigmoid_gate))
    ).astype(jnp.bfloat16)
    up_grad = (hidden_grad * activated).astype(jnp.bfloat16)
    gate_out[...] = gate_grad
    up_out[...] = up_grad
    for step in range(steps):
        at = slice(step * chunk, (step + 1) * chunk)
        value = dot_nt(gate_grad, pair[0, at, :]) + dot_nt(up_grad, pair[1, at, :])
        for group in range(groups):
            parts[group][:, at] = value[group * rows : (group + 1) * rows].astype(
                parts[group].dtype
            )


def backward(cots, pre_gate, pre_up, pair, down):
    groups = len(cots)
    rows, width = cots[0].shape
    total, units = pre_gate.shape
    chunk = min(512, width)
    out_shape = [bf16(total, units)] * 3
    out_shape += [
        jax.ShapeDtypeStruct((rows, width), jnp.float32 if group == 0 else jnp.bfloat16)
        for group in range(groups)
    ]
    out = pl.pallas_call(
        functools.partial(backward_kernel, groups, chunk),
        in_specs=[VMEM] * (groups + 4),
        out_specs=[VMEM] * len(out_shape),
        out_shape=out_shape,
        scratch_shapes=[pltpu.VMEM((total, units), jnp.float32)],
        compiler_params=params(28),
        cost_estimate=cost(6 * total * width * units, 6 * width * units),
        name="backward_rows",
    )(
        *cots,
        pre_gate,
        pre_up,
        pltpu.with_memory_space_constraint(pair, pltpu.VMEM),
        pltpu.with_memory_space_constraint(down, pltpu.VMEM),
    )
    return out[0], out[1], out[2], out[3:]


def add_parts(own, others, after):
    rows, width = own.shape
    number = rows // CAP
    count = len(others)

    def body(*refs):
        total = refs[0][...]
        for other in refs[1 : 1 + count]:
            total = total + other[...].astype(jnp.float32)
        total = total.astype(jnp.bfloat16)
        for index in range(number):
            refs[2 + count][index] = total[index * CAP : (index + 1) * CAP]

    return pl.pallas_call(
        body,
        in_specs=[VMEM] * (1 + count) + [HBM],
        out_specs=VMEM,
        out_shape=bf16(number, CAP, width),
        compiler_params=params(16),
        cost_estimate=cost(rows * width, 8 * rows * width),
        name="add_parts",
    )(own, *others, in_hbm(after))


def pair_grad_kernel(blocks, chunk, *refs):
    toks, gate_ref, up_ref = refs[:blocks], refs[blocks], refs[blocks + 1]
    out_hbm, buffer, sems = refs[blocks + 3 :]
    width = toks[0].shape[1]
    copies = []
    for step in range(width // chunk):
        at = slice(step * chunk, (step + 1) * chunk)
        tok = jnp.concatenate([ref[:, at] for ref in toks], axis=0)
        for side, ref in enumerate((gate_ref, up_ref)):
            buffer[side, at, :] = dot_tn(tok, ref[...]).astype(jnp.bfloat16)
        where = pl.ds(step * chunk, chunk)
        one = pltpu.make_async_copy(
            buffer.at[:, where, :], out_hbm.at[0, :, where, :], sems.at[step]
        )
        one.start()
        copies.append(one)
    for one in copies:
        one.wait()


def pair_grad(toks, gate_grad, up_grad, after):
    blocks = len(toks)
    width = toks[0].shape[1]
    total, units = gate_grad.shape
    chunk = min(512, width)
    return pl.pallas_call(
        functools.partial(pair_grad_kernel, blocks, chunk),
        in_specs=[VMEM] * (blocks + 2) + [pl.BlockSpec(memory_space=pl.ANY)],
        out_specs=HBM,
        out_shape=bf16(1, 2, width, units),
        scratch_shapes=[
            pltpu.VMEM((2, width, units), jnp.bfloat16),
            pltpu.SemaphoreType.DMA((width // chunk,)),
        ],
        compiler_params=params(32),
        cost_estimate=cost(4 * total * width * units, 4 * width * units),
        name="pair_grad",
    )(*toks, gate_grad, up_grad, after)


def down_grad_kernel(blocks, chunk, *refs):
    cots, hidden_ref, out_hbm = refs[:blocks], refs[blocks], refs[blocks + 1]
    buffer, sems = refs[blocks + 2 :]
    width = cots[0].shape[1]
    copies = []
    for step in range(width // chunk):
        at = slice(step * chunk, (step + 1) * chunk)
        cot = jnp.concatenate([ref[:, at] for ref in cots], axis=0)
        buffer[:, at] = dot_tn(hidden_ref[...], cot).astype(jnp.bfloat16)
        where = pl.ds(step * chunk, chunk)
        one = pltpu.make_async_copy(buffer.at[:, where], out_hbm.at[0, :, where], sems.at[step])
        one.start()
        copies.append(one)
    for one in copies:
        one.wait()


def down_grad(cots, hidden):
    blocks = len(cots)
    width = cots[0].shape[1]
    total, units = hidden.shape
    chunk = min(1024, width)
    return pl.pallas_call(
        functools.partial(down_grad_kernel, blocks, chunk),
        in_specs=[VMEM] * (blocks + 1),
        out_specs=HBM,
        out_shape=bf16(1, units, width),
        scratch_shapes=[
            pltpu.VMEM((units, width), jnp.bfloat16),
            pltpu.SemaphoreType.DMA((width // chunk,)),
        ],
        compiler_params=params(24),
        cost_estimate=cost(2 * total * width * units, 2 * width * units),
        name="down_grad",
    )(*cots, hidden)


def spread_kernel(chunk, rows_ref, place_ref, out_hbm, buffer, sems):
    number, _, width = rows_ref.shape
    place = place_ref[...]
    copies = []
    for step in range(width // chunk):
        at = slice(step * chunk, (step + 1) * chunk)
        rows = jnp.concatenate([rows_ref[index, :, at] for index in range(number)], axis=0)
        buffer[:, at] = dot_tn(place, rows).astype(jnp.bfloat16)
        where = pl.ds(step * chunk, chunk)
        one = pltpu.make_async_copy(buffer.at[:, where], out_hbm.at[:, where], sems.at[step])
        one.start()
        copies.append(one)
    for one in copies:
        one.wait()


def spread(rows, place):
    number, _, width = rows.shape
    tokens = place.shape[1]
    chunk = min(1024, width)
    return pl.pallas_call(
        functools.partial(spread_kernel, chunk),
        in_specs=[VMEM] * 2,
        out_specs=HBM,
        out_shape=bf16(tokens, width),
        scratch_shapes=[
            pltpu.VMEM((tokens, width), jnp.bfloat16),
            pltpu.SemaphoreType.DMA((width // chunk,)),
        ],
        compiler_params=params(16),
        cost_estimate=cost(2 * number * CAP * tokens * width, 2 * tokens * width),
        name="spread_rows",
    )(rows, place)


def per_device(activations, cotangent, expert_ids, gate_probs, gate_up, down_proj):
    experts = lax.axis_size("expert")
    groups = lax.axis_size("dp")
    tokens, width = activations.shape

    def exchange(value):
        return lax.all_to_all(value, "expert", split_axis=0, concat_axis=0, tiled=True)

    def shift(value, by):
        return lax.ppermute(value, "dp", [(i, (i + by) % groups) for i in range(groups)])

    send_tok, send_cot, place = route(
        expert_ids.reshape(1, tokens), gate_probs.reshape(1, tokens), activations, cotangent, experts
    )
    own_tok = exchange(send_tok).reshape(experts * CAP, width)
    toks = [own_tok] + [shift(own_tok, by) for by in range(1, groups)]
    own_cot = exchange(send_cot).reshape(experts * CAP, width)
    cots = [own_cot] + [shift(own_cot, by) for by in range(1, groups)]
    pre_gate, pre_up, pair, down = forward(toks, gate_up[0], down_proj[0], own_cot)
    gate_grad, up_grad, hidden, parts = backward(cots, pre_gate, pre_up, pair, down)
    others = [shift(parts[by], -by) for by in range(1, groups)]
    down_total = down_grad(cots, hidden)
    rounded = add_parts(parts[0], others, down_total)
    returned = exchange(rounded)
    pair_total = pair_grad(toks, gate_grad, up_grad, rounded)
    input_grad = spread(returned, place)
    return input_grad, pair_total, down_total


def solution(mesh):
    rows = P(("dp", "expert"), None)
    pair, down = P("expert", None, None, "dp"), P("expert", "dp", None)
    return jax.shard_map(
        per_device,
        mesh=mesh,
        in_specs=(rows, rows, rows, rows, pair, down),
        out_specs=(rows, pair, down),
        check_vma=False,
    )
```

```python
import functools

import jax
import jax.numpy as jnp
from jax import lax
from jax.experimental import pallas as pl
from jax.experimental.pallas import tpu as pltpu
from jax.sharding import PartitionSpec as P

CAP = 2
MIB = 1024 * 1024
VMEM = pl.BlockSpec(memory_space=pltpu.VMEM)
HBM = pl.BlockSpec(memory_space=pltpu.HBM)


def dot_nn(a, b):
    return lax.dot_general(a, b, (((1,), (0,)), ((), ())), preferred_element_type=jnp.float32)


def dot_nt(a, b):
    return lax.dot_general(a, b, (((1,), (1,)), ((), ())), preferred_element_type=jnp.float32)


def dot_tn(a, b):
    return lax.dot_general(a, b, (((0,), (0,)), ((), ())), preferred_element_type=jnp.float32)


def cost(flops, moved):
    return pl.CostEstimate(flops=int(flops), bytes_accessed=int(moved), transcendentals=0)


def params(mib):
    return pltpu.CompilerParams(vmem_limit_bytes=mib * MIB)


def in_hbm(value):
    return pltpu.with_memory_space_constraint(value, pltpu.HBM)


def bf16(*shape):
    return jax.ShapeDtypeStruct(shape, jnp.bfloat16)


def route_kernel(experts, groups, chunk, ids_hbm, probs_hbm, act_hbm, cot_hbm, *refs):
    send_hbm, place_ref, ids_ref, probs_ref, act, cot, send, sems, out_sems = refs
    tokens, width = act.shape
    steps = width // chunk
    small = (
        pltpu.make_async_copy(ids_hbm, ids_ref, sems.at[2 * steps]),
        pltpu.make_async_copy(probs_hbm, probs_ref, sems.at[2 * steps + 1]),
    )
    large = []
    for step in range(steps):
        at = pl.ds(step * chunk, chunk)
        large.append(
            (
                pltpu.make_async_copy(act_hbm.at[:, at], act.at[:, at], sems.at[2 * step]),
                pltpu.make_async_copy(cot_hbm.at[:, at], cot.at[:, at], sems.at[2 * step + 1]),
            )
        )
    for one in small:
        one.start()
    for pair in large:
        for one in pair:
            one.start()
    for one in small:
        one.wait()

    ids = ids_ref[...]
    inside = ids < experts
    near = jnp.where(inside, ids, -CAP)
    units = lax.broadcasted_iota(jnp.int32, (experts, tokens), 0)
    onehot = jnp.where(units == near, 1.0, 0.0)
    earlier = lax.broadcasted_iota(jnp.int32, (tokens, tokens), 0) < lax.broadcasted_iota(
        jnp.int32, (tokens, tokens), 1
    )
    before = dot_nn(onehot.astype(jnp.bfloat16), jnp.where(earlier, 1.0, 0.0).astype(jnp.bfloat16))
    rank = jnp.sum(before * onehot, axis=0, keepdims=True).astype(jnp.int32)
    slots = lax.broadcasted_iota(jnp.int32, (experts * CAP, tokens), 0)
    place = jnp.where(slots == near * CAP + rank, 1.0, 0.0)
    weight = jnp.sum(place * probs_ref[...], axis=1, keepdims=True)
    place = place.astype(jnp.bfloat16)
    place_ref[...] = place
    sent = []
    for step in range(steps):
        at = slice(step * chunk, (step + 1) * chunk)
        for one in large[step]:
            one.wait()
        rows_tok = dot_nn(place, act[:, at]).astype(jnp.bfloat16)
        rows_cot = (weight * dot_nn(place, cot[:, at])).astype(jnp.bfloat16)
        for unit in range(experts):
            send[unit, :CAP, at] = rows_tok[unit * CAP : (unit + 1) * CAP]
            send[unit, CAP:, at] = rows_cot[unit * CAP : (unit + 1) * CAP]
        where = pl.ds(step * chunk, chunk)
        for group in range(groups):
            block = pl.ds(group * experts, experts)
            one = pltpu.make_async_copy(
                send.at[:, :, where], send_hbm.at[block, :, where], out_sems.at[group, step]
            )
            one.start()
            sent.append(one)
    for one in sent:
        one.wait()


def route(ids, probs, act, cot, experts, groups):
    tokens, width = act.shape
    chunk = min(1024, width)
    return pl.pallas_call(
        functools.partial(route_kernel, experts, groups, chunk),
        in_specs=[HBM] * 4,
        out_specs=[HBM, VMEM],
        out_shape=[
            pltpu.HBM((groups * experts, 2 * CAP, width), jnp.bfloat16),
            bf16(experts * CAP, tokens),
        ],
        scratch_shapes=[
            pltpu.VMEM((1, tokens), jnp.int32),
            pltpu.VMEM((1, tokens), jnp.float32),
            pltpu.VMEM((tokens, width), jnp.bfloat16),
            pltpu.VMEM((tokens, width), jnp.bfloat16),
            pltpu.VMEM((experts, 2 * CAP, width), jnp.bfloat16),
            pltpu.SemaphoreType.DMA((2 * (width // chunk) + 2,)),
            pltpu.SemaphoreType.DMA((groups, width // chunk)),
        ],
        compiler_params=params(16),
        cost_estimate=cost(4 * experts * CAP * tokens * width, 4 * tokens * width),
        name="route_rows",
    )(in_hbm(ids), in_hbm(probs), in_hbm(act), in_hbm(cot))


def load_kernel(chunk, pair_hbm, down_hbm, after, pair, down, sems):
    del after
    width = down.shape[1]
    copies = []
    for step in range(width // chunk):
        at = pl.ds(step * chunk, chunk)
        copies += [
            pltpu.make_async_copy(pair_hbm.at[:, at, :], pair.at[:, at, :], sems.at[0, step]),
            pltpu.make_async_copy(down_hbm.at[:, at], down.at[:, at], sems.at[1, step]),
        ]
    for one in copies:
        one.start()
    for one in copies:
        one.wait()


def load(pair, down, after):
    units, width = down.shape
    chunk = min(1024, width)
    return pl.pallas_call(
        functools.partial(load_kernel, chunk),
        in_specs=[HBM] * 2 + [pl.BlockSpec(memory_space=pl.ANY)],
        out_specs=[VMEM] * 2,
        out_shape=[pltpu.VMEM(pair.shape, jnp.bfloat16), pltpu.VMEM(down.shape, jnp.bfloat16)],
        scratch_shapes=[pltpu.SemaphoreType.DMA((2, width // chunk))],
        compiler_params=params(28),
        cost_estimate=cost(0, 6 * width * units),
        name="load_weights",
    )(in_hbm(pair), in_hbm(down), after)


def expert_kernel(chunk, got, pair, down, *refs):
    gate_out, up_out, hidden_out, tok_all, cot_all, parts_hbm = refs[:6]
    parts, acc_gate, acc_up, acc_hid, sems = refs[6:]
    blocks, _, width = got.shape
    steps = width // chunk
    for step in range(steps):
        at = slice(step * chunk, (step + 1) * chunk)
        tok = jnp.concatenate([got[block, :CAP, at] for block in range(blocks)], axis=0)
        cot = jnp.concatenate([got[block, CAP:, at] for block in range(blocks)], axis=0)
        tok_all[:, at] = tok
        cot_all[:, at] = cot
        gate = dot_nn(tok, pair[0, at, :])
        up = dot_nn(tok, pair[1, at, :])
        hid = dot_nt(cot, down[:, at])
        if step == 0:
            acc_gate[...], acc_up[...], acc_hid[...] = gate, up, hid
        else:
            acc_gate[...] += gate
            acc_up[...] += up
            acc_hid[...] += hid
    pre_gate, pre_up, hidden_grad = acc_gate[...], acc_up[...], acc_hid[...]
    sigmoid_gate = jax.nn.sigmoid(pre_gate)
    activated = pre_gate * sigmoid_gate
    hidden_out[...] = (activated * pre_up).astype(jnp.bfloat16)
    gate_grad = (
        hidden_grad * pre_up * sigmoid_gate * (1.0 + pre_gate * (1.0 - sigmoid_gate))
    ).astype(jnp.bfloat16)
    up_grad = (hidden_grad * activated).astype(jnp.bfloat16)
    gate_out[...] = gate_grad
    up_out[...] = up_grad
    copies = []
    for step in range(steps):
        at = slice(step * chunk, (step + 1) * chunk)
        value = dot_nt(gate_grad, pair[0, at, :]) + dot_nt(up_grad, pair[1, at, :])
        value = value.astype(jnp.bfloat16)
        for block in range(blocks):
            parts[block, :, at] = value[block * CAP : (block + 1) * CAP]
        where = pl.ds(step * chunk, chunk)
        one = pltpu.make_async_copy(
            parts.at[:, :, where], parts_hbm.at[:, :, where], sems.at[step]
        )
        one.start()
        copies.append(one)
    for one in copies:
        one.wait()


def expert_rows(got, pair, down):
    blocks, _, width = got.shape
    units = down.shape[0]
    chunk = min(512, width)
    total = blocks * CAP
    return pl.pallas_call(
        functools.partial(expert_kernel, chunk),
        in_specs=[VMEM] * 3,
        out_specs=[VMEM] * 5 + [HBM],
        out_shape=[bf16(total, units)] * 3
        + [bf16(total, width)] * 2
        + [pltpu.HBM((blocks, CAP, width), jnp.bfloat16)],
        scratch_shapes=[
            pltpu.VMEM((blocks, CAP, width), jnp.bfloat16),
            pltpu.VMEM((total, units), jnp.float32),
            pltpu.VMEM((total, units), jnp.float32),
            pltpu.VMEM((total, units), jnp.float32),
            pltpu.SemaphoreType.DMA((width // chunk,)),
        ],
        compiler_params=params(28),
        cost_estimate=cost(10 * total * width * units, 6 * width * units),
        name="expert_rows",
    )(
        got,
        pltpu.with_memory_space_constraint(pair, pltpu.VMEM),
        pltpu.with_memory_space_constraint(down, pltpu.VMEM),
    )


def pair_grad_kernel(blocks, chunk, *refs):
    toks, gate_ref, up_ref = refs[:blocks], refs[blocks], refs[blocks + 1]
    out_hbm, buffer, sems = refs[blocks + 2 :]
    width = toks[0].shape[1]
    copies = []
    for step in range(width // chunk):
        at = slice(step * chunk, (step + 1) * chunk)
        tok = jnp.concatenate([ref[:, at] for ref in toks], axis=0)
        for side, ref in enumerate((gate_ref, up_ref)):
            buffer[side, at, :] = dot_tn(tok, ref[...]).astype(jnp.bfloat16)
        where = pl.ds(step * chunk, chunk)
        one = pltpu.make_async_copy(
            buffer.at[:, where, :], out_hbm.at[0, :, where, :], sems.at[step]
        )
        one.start()
        copies.append(one)
    for one in copies:
        one.wait()


def pair_grad(toks, gate_grad, up_grad):
    blocks = len(toks)
    width = toks[0].shape[1]
    total, units = gate_grad.shape
    chunk = min(512, width)
    return pl.pallas_call(
        functools.partial(pair_grad_kernel, blocks, chunk),
        in_specs=[VMEM] * (blocks + 2),
        out_specs=HBM,
        out_shape=bf16(1, 2, width, units),
        scratch_shapes=[
            pltpu.VMEM((2, width, units), jnp.bfloat16),
            pltpu.SemaphoreType.DMA((width // chunk,)),
        ],
        compiler_params=params(32),
        cost_estimate=cost(4 * total * width * units, 4 * width * units),
        name="pair_grad",
    )(*toks, gate_grad, up_grad)


def down_grad_kernel(blocks, chunk, *refs):
    cots, hidden_ref, out_hbm = refs[:blocks], refs[blocks], refs[blocks + 1]
    buffer, sems = refs[blocks + 2 :]
    width = cots[0].shape[1]
    copies = []
    for step in range(width // chunk):
        at = slice(step * chunk, (step + 1) * chunk)
        cot = jnp.concatenate([ref[:, at] for ref in cots], axis=0)
        buffer[:, at] = dot_tn(hidden_ref[...], cot).astype(jnp.bfloat16)
        where = pl.ds(step * chunk, chunk)
        one = pltpu.make_async_copy(buffer.at[:, where], out_hbm.at[0, :, where], sems.at[step])
        one.start()
        copies.append(one)
    for one in copies:
        one.wait()


def down_grad(cots, hidden):
    blocks = len(cots)
    width = cots[0].shape[1]
    total, units = hidden.shape
    chunk = min(1024, width)
    return pl.pallas_call(
        functools.partial(down_grad_kernel, blocks, chunk),
        in_specs=[VMEM] * (blocks + 1),
        out_specs=HBM,
        out_shape=bf16(1, units, width),
        scratch_shapes=[
            pltpu.VMEM((units, width), jnp.bfloat16),
            pltpu.SemaphoreType.DMA((width // chunk,)),
        ],
        compiler_params=params(24),
        cost_estimate=cost(2 * total * width * units, 2 * width * units),
        name="down_grad",
    )(*cots, hidden)


def spread_kernel(chunk, rows_ref, place_ref, out_hbm, buffer, sems):
    blocks, _, width = rows_ref.shape
    place = place_ref[...]
    number = place.shape[0] // CAP
    copies = []
    for step in range(width // chunk):
        at = slice(step * chunk, (step + 1) * chunk)
        total = 0.0
        for start in range(0, blocks, number):
            part = [rows_ref[start + index, :, at] for index in range(number)]
            total = total + jnp.concatenate(part, axis=0).astype(jnp.float32)
        buffer[:, at] = dot_tn(place, total.astype(jnp.bfloat16)).astype(jnp.bfloat16)
        where = pl.ds(step * chunk, chunk)
        one = pltpu.make_async_copy(buffer.at[:, where], out_hbm.at[:, where], sems.at[step])
        one.start()
        copies.append(one)
    for one in copies:
        one.wait()


def spread(rows, place):
    width = rows.shape[2]
    slots, tokens = place.shape
    chunk = min(1024, width)
    return pl.pallas_call(
        functools.partial(spread_kernel, chunk),
        in_specs=[VMEM] * 2,
        out_specs=HBM,
        out_shape=bf16(tokens, width),
        scratch_shapes=[
            pltpu.VMEM((tokens, width), jnp.bfloat16),
            pltpu.SemaphoreType.DMA((width // chunk,)),
        ],
        compiler_params=params(16),
        cost_estimate=cost(2 * slots * tokens * width, 2 * tokens * width),
        name="spread_rows",
    )(rows, place)


def per_device(activations, cotangent, expert_ids, gate_probs, gate_up, down_proj):
    experts = lax.axis_size("expert")
    groups = lax.axis_size("dp")
    tokens = activations.shape[0]

    def exchange(value):
        return lax.all_to_all(value, ("dp", "expert"), split_axis=0, concat_axis=0, tiled=True)

    send, place = route(
        expert_ids.reshape(1, tokens),
        gate_probs.reshape(1, tokens),
        activations,
        cotangent,
        experts,
        groups,
    )
    got = exchange(send)
    pair, down = load(gate_up[0], down_proj[0], place)
    gate_grad, up_grad, hidden, tok, cot, parts = expert_rows(got, pair, down)
    returned = exchange(parts)
    down_total = down_grad([cot], hidden)
    pair_total = pair_grad([tok], gate_grad, up_grad)
    input_grad = spread(returned, place)
    return input_grad, pair_total, down_total


def solution(mesh):
    rows = P(("dp", "expert"), None)
    pair, down = P("expert", None, None, "dp"), P("expert", "dp", None)
    return jax.shard_map(
        per_device,
        mesh=mesh,
        in_specs=(rows, rows, rows, rows, pair, down),
        out_specs=(rows, pair, down),
        check_vma=False,
    )
```

```python
import functools

import jax
import jax.numpy as jnp
from jax import lax
from jax.experimental import pallas as pl
from jax.experimental.pallas import tpu as pltpu
from jax.sharding import PartitionSpec as P

CAP = 2
MIB = 1024 * 1024
VMEM = pl.BlockSpec(memory_space=pltpu.VMEM)
HBM = pl.BlockSpec(memory_space=pltpu.HBM)


def dot_nn(a, b):
    return lax.dot_general(a, b, (((1,), (0,)), ((), ())), preferred_element_type=jnp.float32)


def dot_nt(a, b):
    return lax.dot_general(a, b, (((1,), (1,)), ((), ())), preferred_element_type=jnp.float32)


def dot_tn(a, b):
    return lax.dot_general(a, b, (((0,), (0,)), ((), ())), preferred_element_type=jnp.float32)


def cost(flops, moved):
    return pl.CostEstimate(flops=int(flops), bytes_accessed=int(moved), transcendentals=0)


def params(mib):
    return pltpu.CompilerParams(vmem_limit_bytes=mib * MIB)


def in_hbm(value):
    return pltpu.with_memory_space_constraint(value, pltpu.HBM)


def bf16(*shape):
    return jax.ShapeDtypeStruct(shape, jnp.bfloat16)


def factors(experts):
    far = 1
    while 4 * far * far <= experts:
        far *= 2
    return far, experts // far


def route_kernel(experts, chunk, ids_hbm, probs_hbm, act_hbm, cot_hbm, *refs):
    far, near = factors(experts)
    sends, place_ref = refs[:far], refs[far]
    ids_ref, probs_ref, act, cot, sems = refs[far + 1 :]
    tokens, width = act.shape
    steps = width // chunk
    small = (
        pltpu.make_async_copy(ids_hbm, ids_ref, sems.at[2 * steps]),
        pltpu.make_async_copy(probs_hbm, probs_ref, sems.at[2 * steps + 1]),
    )
    large = []
    for step in range(steps):
        at = pl.ds(step * chunk, chunk)
        large.append(
            (
                pltpu.make_async_copy(act_hbm.at[:, at], act.at[:, at], sems.at[2 * step]),
                pltpu.make_async_copy(cot_hbm.at[:, at], cot.at[:, at], sems.at[2 * step + 1]),
            )
        )
    for one in small:
        one.start()
    for pair in large:
        for one in pair:
            one.start()
    for one in small:
        one.wait()

    me = lax.axis_index("expert")
    ids = ids_ref[...]
    inside = ids < experts
    units = lax.broadcasted_iota(jnp.int32, (experts, tokens), 0)
    onehot = jnp.where(units == ids, 1.0, 0.0)
    earlier = lax.broadcasted_iota(jnp.int32, (tokens, tokens), 0) < lax.broadcasted_iota(
        jnp.int32, (tokens, tokens), 1
    )
    before = dot_nn(onehot.astype(jnp.bfloat16), jnp.where(earlier, 1.0, 0.0).astype(jnp.bfloat16))
    rank = jnp.sum(before * onehot, axis=0, keepdims=True).astype(jnp.int32)
    slots = lax.broadcasted_iota(jnp.int32, (experts * CAP, tokens), 0)
    slot = jnp.where(inside, ids * CAP + rank, -1)
    place_ref[...] = jnp.where(slots == slot, 1.0, 0.0).astype(jnp.bfloat16)
    turned = jnp.where(inside, (ids ^ me) * CAP + rank, -1)
    pick = jnp.where(slots == turned, 1.0, 0.0)
    weight = jnp.sum(pick * probs_ref[...], axis=1, keepdims=True)
    pick = pick.astype(jnp.bfloat16)
    for step in range(steps):
        at = slice(step * chunk, (step + 1) * chunk)
        for one in large[step]:
            one.wait()
        rows_tok = dot_nn(pick, act[:, at]).astype(jnp.bfloat16)
        rows_cot = (weight * dot_nn(pick, cot[:, at])).astype(jnp.bfloat16)
        for unit in range(experts):
            rows = slice(unit * CAP, (unit + 1) * CAP)
            sends[unit // near][unit % near, :CAP, at] = rows_tok[rows]
            sends[unit // near][unit % near, CAP:, at] = rows_cot[rows]


def route(ids, probs, act, cot, experts):
    tokens, width = act.shape
    chunk = min(1024, width)
    far, near = factors(experts)
    out = pl.pallas_call(
        functools.partial(route_kernel, experts, chunk),
        in_specs=[HBM] * 4,
        out_specs=[VMEM] * (far + 1),
        out_shape=[bf16(near, 2 * CAP, width)] * far + [bf16(experts * CAP, tokens)],
        scratch_shapes=[
            pltpu.VMEM((1, tokens), jnp.int32),
            pltpu.VMEM((1, tokens), jnp.float32),
            pltpu.VMEM((tokens, width), jnp.bfloat16),
            pltpu.VMEM((tokens, width), jnp.bfloat16),
            pltpu.SemaphoreType.DMA((2 * (width // chunk) + 2,)),
        ],
        compiler_params=params(16),
        cost_estimate=cost(4 * experts * CAP * tokens * width, 4 * tokens * width),
        name="route_rows",
    )(in_hbm(ids), in_hbm(probs), in_hbm(act), in_hbm(cot))
    return out[:far], out[far]


def merge_kernel(far, *refs):
    pieces, outs = refs[:far], refs[far:]
    for index, out in enumerate(outs):
        rows = [piece[index, :CAP, :] for piece in pieces]
        rows += [piece[index, CAP:, :] for piece in pieces]
        out[...] = jnp.concatenate(rows, axis=0)


def merge(pieces):
    far = len(pieces)
    near, _, width = pieces[0].shape
    return pl.pallas_call(
        functools.partial(merge_kernel, far),
        in_specs=[VMEM] * far,
        out_specs=[VMEM] * near,
        out_shape=[bf16(2 * CAP * far, width)] * near,
        compiler_params=params(16),
        cost_estimate=cost(0, 8 * near * CAP * far * width),
        name="merge_rows",
    )(*pieces)


def load_kernel(chunk, pair_hbm, down_hbm, after, pair, down, sems):
    del after
    width = down.shape[1]
    copies = []
    for step in range(width // chunk):
        at = pl.ds(step * chunk, chunk)
        copies += [
            pltpu.make_async_copy(pair_hbm.at[:, at, :], pair.at[:, at, :], sems.at[0, step]),
            pltpu.make_async_copy(down_hbm.at[:, at], down.at[:, at], sems.at[1, step]),
        ]
    for one in copies:
        one.start()
    for one in copies:
        one.wait()


def load(pair, down, after):
    units, width = down.shape
    chunk = min(1024, width)
    return pl.pallas_call(
        functools.partial(load_kernel, chunk),
        in_specs=[HBM] * 2 + [pl.BlockSpec(memory_space=pl.ANY)],
        out_specs=[VMEM] * 2,
        out_shape=[pltpu.VMEM(pair.shape, jnp.bfloat16), pltpu.VMEM(down.shape, jnp.bfloat16)],
        scratch_shapes=[pltpu.SemaphoreType.DMA((2, width // chunk))],
        compiler_params=params(28),
        cost_estimate=cost(0, 6 * width * units),
        name="load_weights",
    )(in_hbm(pair), in_hbm(down), after)


def expert_kernel(experts, groups, chunk, *refs):
    far, near = factors(experts)
    count = groups * near
    got, pair, down = refs[:count], refs[count], refs[count + 1]
    gate_out, up_out, hidden_out, tok_all, cot_all, parts_hbm = refs[count + 2 : count + 8]
    parts, acc_gate, acc_up, acc_hid, sems = refs[count + 8 :]
    half = far * CAP
    width = got[0].shape[1]
    steps = width // chunk
    for step in range(steps):
        at = slice(step * chunk, (step + 1) * chunk)
        tok = jnp.concatenate([piece[:half, at] for piece in got], axis=0)
        cot = jnp.concatenate([piece[half:, at] for piece in got], axis=0)
        tok_all[:, at] = tok
        cot_all[:, at] = cot
        gate = dot_nn(tok, pair[0, at, :])
        up = dot_nn(tok, pair[1, at, :])
        hid = dot_nt(cot, down[:, at])
        if step == 0:
            acc_gate[...], acc_up[...], acc_hid[...] = gate, up, hid
        else:
            acc_gate[...] += gate
            acc_up[...] += up
            acc_hid[...] += hid
    pre_gate, pre_up, hidden_grad = acc_gate[...], acc_up[...], acc_hid[...]
    sigmoid_gate = jax.nn.sigmoid(pre_gate)
    activated = pre_gate * sigmoid_gate
    hidden_out[...] = (activated * pre_up).astype(jnp.bfloat16)
    gate_grad = (
        hidden_grad * pre_up * sigmoid_gate * (1.0 + pre_gate * (1.0 - sigmoid_gate))
    ).astype(jnp.bfloat16)
    up_grad = (hidden_grad * activated).astype(jnp.bfloat16)
    gate_out[...] = gate_grad
    up_out[...] = up_grad
    me, group = lax.axis_index("expert"), lax.axis_index("dp")
    homes = []
    for index in range(count):
        source = lax.rem(group - index // near + groups, groups) * experts
        homes += [source + (me ^ (high * near + index % near)) for high in range(far)]
    copies = []
    for step in range(steps):
        at = slice(step * chunk, (step + 1) * chunk)
        value = dot_nt(gate_grad, pair[0, at, :]) + dot_nt(up_grad, pair[1, at, :])
        value = value.astype(jnp.bfloat16)
        for block, home in enumerate(homes):
            parts[home, :, at] = value[block * CAP : (block + 1) * CAP]
        where = pl.ds(step * chunk, chunk)
        one = pltpu.make_async_copy(
            parts.at[:, :, where], parts_hbm.at[:, :, where], sems.at[step]
        )
        one.start()
        copies.append(one)
    for one in copies:
        one.wait()


def expert_rows(got, pair, down, experts, groups):
    width = got[0].shape[1]
    units = down.shape[0]
    chunk = min(512, width)
    blocks = groups * experts
    total = blocks * CAP
    return pl.pallas_call(
        functools.partial(expert_kernel, experts, groups, chunk),
        in_specs=[VMEM] * (len(got) + 2),
        out_specs=[VMEM] * 5 + [HBM],
        out_shape=[bf16(total, units)] * 3
        + [bf16(total, width)] * 2
        + [pltpu.HBM((blocks, CAP, width), jnp.bfloat16)],
        scratch_shapes=[
            pltpu.VMEM((blocks, CAP, width), jnp.bfloat16),
            pltpu.VMEM((total, units), jnp.float32),
            pltpu.VMEM((total, units), jnp.float32),
            pltpu.VMEM((total, units), jnp.float32),
            pltpu.SemaphoreType.DMA((width // chunk,)),
        ],
        compiler_params=params(28),
        cost_estimate=cost(10 * total * width * units, 6 * width * units),
        name="expert_rows",
    )(
        *got,
        pltpu.with_memory_space_constraint(pair, pltpu.VMEM),
        pltpu.with_memory_space_constraint(down, pltpu.VMEM),
    )


def pair_grad_kernel(blocks, chunk, *refs):
    toks, gate_ref, up_ref = refs[:blocks], refs[blocks], refs[blocks + 1]
    out_hbm, buffer, sems = refs[blocks + 2 :]
    width = toks[0].shape[1]
    copies = []
    for step in range(width // chunk):
        at = slice(step * chunk, (step + 1) * chunk)
        tok = jnp.concatenate([ref[:, at] for ref in toks], axis=0)
        for side, ref in enumerate((gate_ref, up_ref)):
            buffer[side, at, :] = dot_tn(tok, ref[...]).astype(jnp.bfloat16)
        where = pl.ds(step * chunk, chunk)
        one = pltpu.make_async_copy(
            buffer.at[:, where, :], out_hbm.at[0, :, where, :], sems.at[step]
        )
        one.start()
        copies.append(one)
    for one in copies:
        one.wait()


def pair_grad(toks, gate_grad, up_grad):
    blocks = len(toks)
    width = toks[0].shape[1]
    total, units = gate_grad.shape
    chunk = min(512, width)
    return pl.pallas_call(
        functools.partial(pair_grad_kernel, blocks, chunk),
        in_specs=[VMEM] * (blocks + 2),
        out_specs=HBM,
        out_shape=bf16(1, 2, width, units),
        scratch_shapes=[
            pltpu.VMEM((2, width, units), jnp.bfloat16),
            pltpu.SemaphoreType.DMA((width // chunk,)),
        ],
        compiler_params=params(32),
        cost_estimate=cost(4 * total * width * units, 4 * width * units),
        name="pair_grad",
    )(*toks, gate_grad, up_grad)


def down_grad_kernel(blocks, chunk, *refs):
    cots, hidden_ref, out_hbm = refs[:blocks], refs[blocks], refs[blocks + 1]
    buffer, sems = refs[blocks + 2 :]
    width = cots[0].shape[1]
    copies = []
    for step in range(width // chunk):
        at = slice(step * chunk, (step + 1) * chunk)
        cot = jnp.concatenate([ref[:, at] for ref in cots], axis=0)
        buffer[:, at] = dot_tn(hidden_ref[...], cot).astype(jnp.bfloat16)
        where = pl.ds(step * chunk, chunk)
        one = pltpu.make_async_copy(buffer.at[:, where], out_hbm.at[0, :, where], sems.at[step])
        one.start()
        copies.append(one)
    for one in copies:
        one.wait()


def down_grad(cots, hidden):
    blocks = len(cots)
    width = cots[0].shape[1]
    total, units = hidden.shape
    chunk = min(1024, width)
    return pl.pallas_call(
        functools.partial(down_grad_kernel, blocks, chunk),
        in_specs=[VMEM] * (blocks + 1),
        out_specs=HBM,
        out_shape=bf16(1, units, width),
        scratch_shapes=[
            pltpu.VMEM((units, width), jnp.bfloat16),
            pltpu.SemaphoreType.DMA((width // chunk,)),
        ],
        compiler_params=params(24),
        cost_estimate=cost(2 * total * width * units, 2 * width * units),
        name="down_grad",
    )(*cots, hidden)


def spread_kernel(chunk, rows_ref, place_ref, out_hbm, buffer, sems):
    blocks, _, width = rows_ref.shape
    place = place_ref[...]
    number = place.shape[0] // CAP
    copies = []
    for step in range(width // chunk):
        at = slice(step * chunk, (step + 1) * chunk)
        total = 0.0
        for start in range(0, blocks, number):
            part = [rows_ref[start + index, :, at] for index in range(number)]
            total = total + jnp.concatenate(part, axis=0).astype(jnp.float32)
        buffer[:, at] = dot_tn(place, total.astype(jnp.bfloat16)).astype(jnp.bfloat16)
        where = pl.ds(step * chunk, chunk)
        one = pltpu.make_async_copy(buffer.at[:, where], out_hbm.at[:, where], sems.at[step])
        one.start()
        copies.append(one)
    for one in copies:
        one.wait()


def spread(rows, place):
    width = rows.shape[2]
    slots, tokens = place.shape
    chunk = min(1024, width)
    return pl.pallas_call(
        functools.partial(spread_kernel, chunk),
        in_specs=[VMEM] * 2,
        out_specs=HBM,
        out_shape=bf16(tokens, width),
        scratch_shapes=[
            pltpu.VMEM((tokens, width), jnp.bfloat16),
            pltpu.SemaphoreType.DMA((width // chunk,)),
        ],
        compiler_params=params(16),
        cost_estimate=cost(2 * slots * tokens * width, 2 * tokens * width),
        name="spread_rows",
    )(rows, place)


def per_device(activations, cotangent, expert_ids, gate_probs, gate_up, down_proj):
    experts = lax.axis_size("expert")
    groups = lax.axis_size("dp")
    tokens = activations.shape[0]
    far, near = factors(experts)

    def send(value, by_group, by_expert):
        if by_group == 0 and by_expert == 0:
            return value
        pairs = []
        for group in range(groups):
            to = (group + by_group) % groups
            for i in range(experts):
                pairs.append((group * experts + i, to * experts + (i ^ by_expert)))
        return lax.ppermute(value, ("dp", "expert"), pairs)

    pieces, place = route(
        expert_ids.reshape(1, tokens),
        gate_probs.reshape(1, tokens),
        activations,
        cotangent,
        experts,
    )
    pair, down = load(gate_up[0], down_proj[0], place)
    merged = merge([send(pieces[high], 0, high * near) for high in range(far)])
    got = [send(merged[low], group, low) for group in range(groups) for low in range(near)]
    gate_grad, up_grad, hidden, tok, cot, parts = expert_rows(got, pair, down, experts, groups)
    returned = lax.all_to_all(parts, ("dp", "expert"), split_axis=0, concat_axis=0, tiled=True)
    down_total = down_grad([cot], hidden)
    pair_total = pair_grad([tok], gate_grad, up_grad)
    input_grad = spread(returned, place)
    return input_grad, pair_total, down_total


def solution(mesh):
    rows = P(("dp", "expert"), None)
    pair, down = P("expert", None, None, "dp"), P("expert", "dp", None)
    return jax.shard_map(
        per_device,
        mesh=mesh,
        in_specs=(rows, rows, rows, rows, pair, down),
        out_specs=(rows, pair, down),
        check_vma=False,
    )
```

```python
import functools

import jax
import jax.numpy as jnp
from jax import lax
from jax.experimental import pallas as pl
from jax.experimental.pallas import tpu as pltpu
from jax.sharding import PartitionSpec as P

CAP = 2
MIB = 1024 * 1024
VMEM = pl.BlockSpec(memory_space=pltpu.VMEM)
HBM = pl.BlockSpec(memory_space=pltpu.HBM)


def dot_nn(a, b):
    return lax.dot_general(a, b, (((1,), (0,)), ((), ())), preferred_element_type=jnp.float32)


def dot_nt(a, b):
    return lax.dot_general(a, b, (((1,), (1,)), ((), ())), preferred_element_type=jnp.float32)


def dot_tn(a, b):
    return lax.dot_general(a, b, (((0,), (0,)), ((), ())), preferred_element_type=jnp.float32)


def cost(flops, moved):
    return pl.CostEstimate(flops=int(flops), bytes_accessed=int(moved), transcendentals=0)


def params(mib):
    return pltpu.CompilerParams(vmem_limit_bytes=mib * MIB)


def in_hbm(value):
    return pltpu.with_memory_space_constraint(value, pltpu.HBM)


def bf16(*shape):
    return jax.ShapeDtypeStruct(shape, jnp.bfloat16)


def factors(experts):
    far = 1
    while 4 * far * far <= experts:
        far *= 2
    return far, experts // far


def route_kernel(experts, chunk, ids_hbm, probs_hbm, act_hbm, cot_hbm, *refs):
    far, near = factors(experts)
    sends, place_ref = refs[:far], refs[far]
    ids_ref, probs_ref, act, cot, sems = refs[far + 1 :]
    tokens, width = act.shape
    steps = width // chunk
    small = (
        pltpu.make_async_copy(ids_hbm, ids_ref, sems.at[2 * steps]),
        pltpu.make_async_copy(probs_hbm, probs_ref, sems.at[2 * steps + 1]),
    )
    large = []
    for step in range(steps):
        at = pl.ds(step * chunk, chunk)
        large.append(
            (
                pltpu.make_async_copy(act_hbm.at[:, at], act.at[:, at], sems.at[2 * step]),
                pltpu.make_async_copy(cot_hbm.at[:, at], cot.at[:, at], sems.at[2 * step + 1]),
            )
        )
    for one in small:
        one.start()
    for pair in large:
        for one in pair:
            one.start()
    for one in small:
        one.wait()

    me = lax.axis_index("expert")
    ids = ids_ref[...]
    inside = ids < experts
    units = lax.broadcasted_iota(jnp.int32, (experts, tokens), 0)
    onehot = jnp.where(units == ids, 1.0, 0.0)
    earlier = lax.broadcasted_iota(jnp.int32, (tokens, tokens), 0) < lax.broadcasted_iota(
        jnp.int32, (tokens, tokens), 1
    )
    before = dot_nn(onehot.astype(jnp.bfloat16), jnp.where(earlier, 1.0, 0.0).astype(jnp.bfloat16))
    rank = jnp.sum(before * onehot, axis=0, keepdims=True).astype(jnp.int32)
    slots = lax.broadcasted_iota(jnp.int32, (experts * CAP, tokens), 0)
    slot = jnp.where(inside, ids * CAP + rank, -1)
    place_ref[...] = jnp.where(slots == slot, 1.0, 0.0).astype(jnp.bfloat16)
    turned = jnp.where(inside, (ids ^ me) * CAP + rank, -1)
    pick = jnp.where(slots == turned, 1.0, 0.0)
    weight = jnp.sum(pick * probs_ref[...], axis=1, keepdims=True)
    pick = pick.astype(jnp.bfloat16)
    for step in range(steps):
        at = slice(step * chunk, (step + 1) * chunk)
        for one in large[step]:
            one.wait()
        rows_tok = dot_nn(pick, act[:, at]).astype(jnp.bfloat16)
        rows_cot = (weight * dot_nn(pick, cot[:, at])).astype(jnp.bfloat16)
        for unit in range(experts):
            rows = slice(unit * CAP, (unit + 1) * CAP)
            sends[unit // near][unit % near, :CAP, at] = rows_tok[rows]
            sends[unit // near][unit % near, CAP:, at] = rows_cot[rows]


def route(ids, probs, act, cot, experts):
    tokens, width = act.shape
    chunk = min(1024, width)
    far, near = factors(experts)
    out = pl.pallas_call(
        functools.partial(route_kernel, experts, chunk),
        in_specs=[HBM] * 4,
        out_specs=[VMEM] * (far + 1),
        out_shape=[bf16(near, 2 * CAP, width)] * far + [bf16(experts * CAP, tokens)],
        scratch_shapes=[
            pltpu.VMEM((1, tokens), jnp.int32),
            pltpu.VMEM((1, tokens), jnp.float32),
            pltpu.VMEM((tokens, width), jnp.bfloat16),
            pltpu.VMEM((tokens, width), jnp.bfloat16),
            pltpu.SemaphoreType.DMA((2 * (width // chunk) + 2,)),
        ],
        compiler_params=params(16),
        cost_estimate=cost(4 * experts * CAP * tokens * width, 4 * tokens * width),
        name="route_rows",
    )(in_hbm(ids), in_hbm(probs), in_hbm(act), in_hbm(cot))
    return out[:far], out[far]


def merge_kernel(far, *refs):
    pieces, outs = refs[:far], refs[far + 1 :]
    for index, out in enumerate(outs):
        rows = [piece[index, :CAP, :] for piece in pieces]
        rows += [piece[index, CAP:, :] for piece in pieces]
        out[...] = jnp.concatenate(rows, axis=0)


def merge(pieces, after):
    far = len(pieces)
    near, _, width = pieces[0].shape
    return pl.pallas_call(
        functools.partial(merge_kernel, far),
        in_specs=[VMEM] * far + [pl.BlockSpec(memory_space=pl.ANY)],
        out_specs=[VMEM] * near,
        out_shape=[bf16(2 * CAP * far, width)] * near,
        compiler_params=params(16),
        cost_estimate=cost(0, 8 * near * CAP * far * width),
        name="merge_rows",
    )(*pieces, after)


def load_kernel(chunk, pair_hbm, down_hbm, after, pair, down, sems):
    del after
    width = down.shape[1]
    copies = []
    for step in range(width // chunk):
        at = pl.ds(step * chunk, chunk)
        copies += [
            pltpu.make_async_copy(pair_hbm.at[:, at, :], pair.at[:, at, :], sems.at[0, step]),
            pltpu.make_async_copy(down_hbm.at[:, at], down.at[:, at], sems.at[1, step]),
        ]
    for one in copies:
        one.start()
    for one in copies:
        one.wait()


def load(pair, down, after):
    units, width = down.shape
    chunk = min(1024, width)
    return pl.pallas_call(
        functools.partial(load_kernel, chunk),
        in_specs=[HBM] * 2 + [pl.BlockSpec(memory_space=pl.ANY)],
        out_specs=[VMEM] * 2,
        out_shape=[pltpu.VMEM(pair.shape, jnp.bfloat16), pltpu.VMEM(down.shape, jnp.bfloat16)],
        scratch_shapes=[pltpu.SemaphoreType.DMA((2, width // chunk))],
        compiler_params=params(28),
        cost_estimate=cost(0, 6 * width * units),
        name="load_weights",
    )(in_hbm(pair), in_hbm(down), after)


def expert_kernel(experts, groups, chunk, *refs):
    far, near = factors(experts)
    count = groups * near
    got, pair, down = refs[:count], refs[count], refs[count + 1]
    gate_out, up_out, hidden_out, tok_all, cot_all, parts_hbm = refs[count + 2 : count + 8]
    parts, acc_gate, acc_up, acc_hid, sems = refs[count + 8 :]
    half = far * CAP
    width = got[0].shape[1]
    steps = width // chunk
    for step in range(steps):
        at = slice(step * chunk, (step + 1) * chunk)
        tok = jnp.concatenate([piece[:half, at] for piece in got], axis=0)
        cot = jnp.concatenate([piece[half:, at] for piece in got], axis=0)
        tok_all[:, at] = tok
        cot_all[:, at] = cot
        gate = dot_nn(tok, pair[0, at, :])
        up = dot_nn(tok, pair[1, at, :])
        hid = dot_nt(cot, down[:, at])
        if step == 0:
            acc_gate[...], acc_up[...], acc_hid[...] = gate, up, hid
        else:
            acc_gate[...] += gate
            acc_up[...] += up
            acc_hid[...] += hid
    pre_gate, pre_up, hidden_grad = acc_gate[...], acc_up[...], acc_hid[...]
    sigmoid_gate = jax.nn.sigmoid(pre_gate)
    activated = pre_gate * sigmoid_gate
    hidden_out[...] = (activated * pre_up).astype(jnp.bfloat16)
    gate_grad = (
        hidden_grad * pre_up * sigmoid_gate * (1.0 + pre_gate * (1.0 - sigmoid_gate))
    ).astype(jnp.bfloat16)
    up_grad = (hidden_grad * activated).astype(jnp.bfloat16)
    gate_out[...] = gate_grad
    up_out[...] = up_grad
    me, group = lax.axis_index("expert"), lax.axis_index("dp")
    homes = []
    for index in range(count):
        source = lax.rem(group - index // near + groups, groups) * experts
        homes += [source + (me ^ (high * near + index % near)) for high in range(far)]
    copies = []
    for step in range(steps):
        at = slice(step * chunk, (step + 1) * chunk)
        value = dot_nt(gate_grad, pair[0, at, :]) + dot_nt(up_grad, pair[1, at, :])
        value = value.astype(jnp.bfloat16)
        for block, home in enumerate(homes):
            parts[home, :, at] = value[block * CAP : (block + 1) * CAP]
        where = pl.ds(step * chunk, chunk)
        one = pltpu.make_async_copy(
            parts.at[:, :, where], parts_hbm.at[:, :, where], sems.at[step]
        )
        one.start()
        copies.append(one)
    for one in copies:
        one.wait()


def expert_rows(got, pair, down, experts, groups):
    width = got[0].shape[1]
    units = down.shape[0]
    chunk = min(1024, width)
    blocks = groups * experts
    total = blocks * CAP
    return pl.pallas_call(
        functools.partial(expert_kernel, experts, groups, chunk),
        in_specs=[VMEM] * (len(got) + 2),
        out_specs=[VMEM] * 5 + [HBM],
        out_shape=[bf16(total, units)] * 3
        + [bf16(total, width)] * 2
        + [pltpu.HBM((blocks, CAP, width), jnp.bfloat16)],
        scratch_shapes=[
            pltpu.VMEM((blocks, CAP, width), jnp.bfloat16),
            pltpu.VMEM((total, units), jnp.float32),
            pltpu.VMEM((total, units), jnp.float32),
            pltpu.VMEM((total, units), jnp.float32),
            pltpu.SemaphoreType.DMA((width // chunk,)),
        ],
        compiler_params=params(28),
        cost_estimate=cost(10 * total * width * units, 6 * width * units),
        name="expert_rows",
    )(
        *got,
        pltpu.with_memory_space_constraint(pair, pltpu.VMEM),
        pltpu.with_memory_space_constraint(down, pltpu.VMEM),
    )


def pair_grad_kernel(blocks, chunk, *refs):
    toks, gate_ref, up_ref = refs[:blocks], refs[blocks], refs[blocks + 1]
    out_hbm, buffer, sems = refs[blocks + 2 :]
    width = toks[0].shape[1]
    copies = []
    for step in range(width // chunk):
        at = slice(step * chunk, (step + 1) * chunk)
        tok = jnp.concatenate([ref[:, at] for ref in toks], axis=0)
        for side, ref in enumerate((gate_ref, up_ref)):
            buffer[side, at, :] = dot_tn(tok, ref[...]).astype(jnp.bfloat16)
        where = pl.ds(step * chunk, chunk)
        one = pltpu.make_async_copy(
            buffer.at[:, where, :], out_hbm.at[0, :, where, :], sems.at[step]
        )
        one.start()
        copies.append(one)
    for one in copies:
        one.wait()


def pair_grad(toks, gate_grad, up_grad):
    blocks = len(toks)
    width = toks[0].shape[1]
    total, units = gate_grad.shape
    chunk = min(512, width)
    return pl.pallas_call(
        functools.partial(pair_grad_kernel, blocks, chunk),
        in_specs=[VMEM] * (blocks + 2),
        out_specs=HBM,
        out_shape=bf16(1, 2, width, units),
        scratch_shapes=[
            pltpu.VMEM((2, width, units), jnp.bfloat16),
            pltpu.SemaphoreType.DMA((width // chunk,)),
        ],
        compiler_params=params(32),
        cost_estimate=cost(4 * total * width * units, 4 * width * units),
        name="pair_grad",
    )(*toks, gate_grad, up_grad)


def down_grad_kernel(blocks, chunk, *refs):
    cots, hidden_ref, out_hbm = refs[:blocks], refs[blocks], refs[blocks + 1]
    buffer, sems = refs[blocks + 2 :]
    width = cots[0].shape[1]
    copies = []
    for step in range(width // chunk):
        at = slice(step * chunk, (step + 1) * chunk)
        cot = jnp.concatenate([ref[:, at] for ref in cots], axis=0)
        buffer[:, at] = dot_tn(hidden_ref[...], cot).astype(jnp.bfloat16)
        where = pl.ds(step * chunk, chunk)
        one = pltpu.make_async_copy(buffer.at[:, where], out_hbm.at[0, :, where], sems.at[step])
        one.start()
        copies.append(one)
    for one in copies:
        one.wait()


def down_grad(cots, hidden):
    blocks = len(cots)
    width = cots[0].shape[1]
    total, units = hidden.shape
    chunk = min(1024, width)
    return pl.pallas_call(
        functools.partial(down_grad_kernel, blocks, chunk),
        in_specs=[VMEM] * (blocks + 1),
        out_specs=HBM,
        out_shape=bf16(1, units, width),
        scratch_shapes=[
            pltpu.VMEM((units, width), jnp.bfloat16),
            pltpu.SemaphoreType.DMA((width // chunk,)),
        ],
        compiler_params=params(24),
        cost_estimate=cost(2 * total * width * units, 2 * width * units),
        name="down_grad",
    )(*cots, hidden)


def spread_kernel(chunk, rows_ref, place_ref, out_hbm, buffer, sems):
    blocks, _, width = rows_ref.shape
    place = jnp.concatenate([place_ref[...]] * (blocks * CAP // place_ref.shape[0]), axis=0)
    copies = []
    for step in range(width // chunk):
        at = slice(step * chunk, (step + 1) * chunk)
        rows = jnp.concatenate([rows_ref[block, :, at] for block in range(blocks)], axis=0)
        buffer[:, at] = dot_tn(place, rows).astype(jnp.bfloat16)
        where = pl.ds(step * chunk, chunk)
        one = pltpu.make_async_copy(buffer.at[:, where], out_hbm.at[:, where], sems.at[step])
        one.start()
        copies.append(one)
    for one in copies:
        one.wait()


def spread(rows, place):
    width = rows.shape[2]
    slots, tokens = place.shape
    chunk = min(1024, width)
    return pl.pallas_call(
        functools.partial(spread_kernel, chunk),
        in_specs=[VMEM] * 2,
        out_specs=HBM,
        out_shape=bf16(tokens, width),
        scratch_shapes=[
            pltpu.VMEM((tokens, width), jnp.bfloat16),
            pltpu.SemaphoreType.DMA((width // chunk,)),
        ],
        compiler_params=params(16),
        cost_estimate=cost(2 * slots * tokens * width, 2 * tokens * width),
        name="spread_rows",
    )(rows, place)


def per_device(activations, cotangent, expert_ids, gate_probs, gate_up, down_proj):
    experts = lax.axis_size("expert")
    groups = lax.axis_size("dp")
    tokens = activations.shape[0]
    far, near = factors(experts)

    def send(value, by_group, by_expert):
        if by_group == 0 and by_expert == 0:
            return value
        pairs = []
        for group in range(groups):
            to = (group + by_group) % groups
            for i in range(experts):
                pairs.append((group * experts + i, to * experts + (i ^ by_expert)))
        return lax.ppermute(value, ("dp", "expert"), pairs)

    pieces, place = route(
        expert_ids.reshape(1, tokens),
        gate_probs.reshape(1, tokens),
        activations,
        cotangent,
        experts,
    )
    pair, down = load(gate_up[0], down_proj[0], place)
    arrived = [send(pieces[high], 0, high * near) for high in reversed(range(far))]
    merged = merge(arrived[::-1], pltpu.with_memory_space_constraint(down, pltpu.VMEM))
    got = [send(merged[low], group, low) for group in range(groups) for low in range(near)]
    gate_grad, up_grad, hidden, tok, cot, parts = expert_rows(got, pair, down, experts, groups)
    returned = lax.all_to_all(parts, ("dp", "expert"), split_axis=0, concat_axis=0, tiled=True)
    down_total = down_grad([cot], hidden)
    pair_total = pair_grad([tok], gate_grad, up_grad)
    input_grad = spread(returned, place)
    return input_grad, pair_total, down_total


def solution(mesh):
    rows = P(("dp", "expert"), None)
    pair, down = P("expert", None, None, "dp"), P("expert", "dp", None)
    return jax.shard_map(
        per_device,
        mesh=mesh,
        in_specs=(rows, rows, rows, rows, pair, down),
        out_specs=(rows, pair, down),
        check_vma=False,
    )
```

```python
import functools

import jax
import jax.numpy as jnp
from jax import lax
from jax.experimental import pallas as pl
from jax.experimental.pallas import tpu as pltpu
from jax.sharding import PartitionSpec as P

CAP = 2
MIB = 1024 * 1024
VMEM = pl.BlockSpec(memory_space=pltpu.VMEM)
HBM = pl.BlockSpec(memory_space=pltpu.HBM)


def dot_nn(a, b):
    return lax.dot_general(a, b, (((1,), (0,)), ((), ())), preferred_element_type=jnp.float32)


def dot_nt(a, b):
    return lax.dot_general(a, b, (((1,), (1,)), ((), ())), preferred_element_type=jnp.float32)


def dot_tn(a, b):
    return lax.dot_general(a, b, (((0,), (0,)), ((), ())), preferred_element_type=jnp.float32)


def cost(flops, moved):
    return pl.CostEstimate(flops=int(flops), bytes_accessed=int(moved), transcendentals=0)


def params(mib):
    return pltpu.CompilerParams(vmem_limit_bytes=mib * MIB)


def in_hbm(value):
    return pltpu.with_memory_space_constraint(value, pltpu.HBM)


def bf16(*shape):
    return jax.ShapeDtypeStruct(shape, jnp.bfloat16)


def factors(experts):
    far = 1
    while 4 * far * far <= experts:
        far *= 2
    return far, experts // far


def route_kernel(experts, chunk, ids_hbm, probs_hbm, act_hbm, cot_hbm, *refs):
    far, near = factors(experts)
    sends, place_ref = refs[:far], refs[far]
    ids_ref, probs_ref, act, cot, sems = refs[far + 1 :]
    tokens, width = act.shape
    steps = width // chunk
    small = (
        pltpu.make_async_copy(ids_hbm, ids_ref, sems.at[2 * steps]),
        pltpu.make_async_copy(probs_hbm, probs_ref, sems.at[2 * steps + 1]),
    )
    large = []
    for step in range(steps):
        at = pl.ds(step * chunk, chunk)
        large.append(
            (
                pltpu.make_async_copy(act_hbm.at[:, at], act.at[:, at], sems.at[2 * step]),
                pltpu.make_async_copy(cot_hbm.at[:, at], cot.at[:, at], sems.at[2 * step + 1]),
            )
        )
    for one in small:
        one.start()
    for pair in large:
        for one in pair:
            one.start()
    for one in small:
        one.wait()

    me = lax.axis_index("expert")
    ids = ids_ref[...]
    inside = ids < experts
    units = lax.broadcasted_iota(jnp.int32, (experts, tokens), 0)
    onehot = jnp.where(units == ids, 1.0, 0.0)
    earlier = lax.broadcasted_iota(jnp.int32, (tokens, tokens), 0) < lax.broadcasted_iota(
        jnp.int32, (tokens, tokens), 1
    )
    before = dot_nn(onehot.astype(jnp.bfloat16), jnp.where(earlier, 1.0, 0.0).astype(jnp.bfloat16))
    rank = jnp.sum(before * onehot, axis=0, keepdims=True).astype(jnp.int32)
    slots = lax.broadcasted_iota(jnp.int32, (experts * CAP, tokens), 0)
    slot = jnp.where(inside, ids * CAP + rank, -1)
    place_ref[...] = jnp.where(slots == slot, 1.0, 0.0).astype(jnp.bfloat16)
    turned = jnp.where(inside, (ids ^ me) * CAP + rank, -1)
    pick = jnp.where(slots == turned, 1.0, 0.0)
    weight = jnp.sum(pick * probs_ref[...], axis=1, keepdims=True)
    pick = pick.astype(jnp.bfloat16)
    for step in range(steps):
        at = slice(step * chunk, (step + 1) * chunk)
        for one in large[step]:
            one.wait()
        rows_tok = dot_nn(pick, act[:, at]).astype(jnp.bfloat16)
        rows_cot = (weight * dot_nn(pick, cot[:, at])).astype(jnp.bfloat16)
        for unit in range(experts):
            rows = slice(unit * CAP, (unit + 1) * CAP)
            sends[unit // near][unit % near, :CAP, at] = rows_tok[rows]
            sends[unit // near][unit % near, CAP:, at] = rows_cot[rows]


def route(ids, probs, act, cot, experts):
    tokens, width = act.shape
    chunk = min(1024, width)
    far, near = factors(experts)
    out = pl.pallas_call(
        functools.partial(route_kernel, experts, chunk),
        in_specs=[HBM] * 4,
        out_specs=[VMEM] * (far + 1),
        out_shape=[bf16(near, 2 * CAP, width)] * far + [bf16(experts * CAP, tokens)],
        scratch_shapes=[
            pltpu.VMEM((1, tokens), jnp.int32),
            pltpu.VMEM((1, tokens), jnp.float32),
            pltpu.VMEM((tokens, width), jnp.bfloat16),
            pltpu.VMEM((tokens, width), jnp.bfloat16),
            pltpu.SemaphoreType.DMA((2 * (width // chunk) + 2,)),
        ],
        compiler_params=params(16),
        cost_estimate=cost(4 * experts * CAP * tokens * width, 4 * tokens * width),
        name="route_rows",
    )(in_hbm(ids), in_hbm(probs), in_hbm(act), in_hbm(cot))
    return out[:far], out[far]


def merge_kernel(far, *refs):
    pieces, outs = refs[:far], refs[far + 1 :]
    for index, out in enumerate(outs):
        rows = [piece[index, :CAP, :] for piece in pieces]
        rows += [piece[index, CAP:, :] for piece in pieces]
        out[...] = jnp.concatenate(rows, axis=0)


def merge(pieces, after):
    far = len(pieces)
    near, _, width = pieces[0].shape
    return pl.pallas_call(
        functools.partial(merge_kernel, far),
        in_specs=[VMEM] * far + [pl.BlockSpec(memory_space=pl.ANY)],
        out_specs=[VMEM] * near,
        out_shape=[bf16(2 * CAP * far, width)] * near,
        compiler_params=params(16),
        cost_estimate=cost(0, 8 * near * CAP * far * width),
        name="merge_rows",
    )(*pieces, after)


def load_kernel(chunk, pair_hbm, down_hbm, after, pair, down, sems):
    del after
    width = down.shape[1]
    copies = []
    for step in range(width // chunk):
        at = pl.ds(step * chunk, chunk)
        copies += [
            pltpu.make_async_copy(pair_hbm.at[:, at, :], pair.at[:, at, :], sems.at[0, step]),
            pltpu.make_async_copy(down_hbm.at[:, at], down.at[:, at], sems.at[1, step]),
        ]
    for one in copies:
        one.start()
    for one in copies:
        one.wait()


def load(pair, down, after):
    units, width = down.shape
    chunk = min(1024, width)
    return pl.pallas_call(
        functools.partial(load_kernel, chunk),
        in_specs=[HBM] * 2 + [pl.BlockSpec(memory_space=pl.ANY)],
        out_specs=[VMEM] * 2,
        out_shape=[pltpu.VMEM(pair.shape, jnp.bfloat16), pltpu.VMEM(down.shape, jnp.bfloat16)],
        scratch_shapes=[pltpu.SemaphoreType.DMA((2, width // chunk))],
        compiler_params=params(28),
        cost_estimate=cost(0, 6 * width * units),
        name="load_weights",
    )(in_hbm(pair), in_hbm(down), after)


def expert_kernel(experts, groups, chunk, *refs):
    far, near = factors(experts)
    count = groups * near
    got, pair, down = refs[:count], refs[count], refs[count + 1]
    gate_out, up_out, hidden_out, tok_all, cot_all, parts_hbm = refs[count + 2 : count + 8]
    parts, acc_gate, acc_up, acc_hid, sems = refs[count + 8 :]
    half = far * CAP
    width = got[0].shape[1]
    steps = width // chunk
    for step in range(steps):
        at = slice(step * chunk, (step + 1) * chunk)
        tok = jnp.concatenate([piece[:half, at] for piece in got], axis=0)
        cot = jnp.concatenate([piece[half:, at] for piece in got], axis=0)
        tok_all[:, at] = tok
        cot_all[:, at] = cot
        gate = dot_nn(tok, pair[0, at, :])
        up = dot_nn(tok, pair[1, at, :])
        hid = dot_nt(cot, down[:, at])
        if step == 0:
            acc_gate[...], acc_up[...], acc_hid[...] = gate, up, hid
        else:
            acc_gate[...] += gate
            acc_up[...] += up
            acc_hid[...] += hid
    pre_gate, pre_up, hidden_grad = acc_gate[...], acc_up[...], acc_hid[...]
    sigmoid_gate = jax.nn.sigmoid(pre_gate)
    activated = pre_gate * sigmoid_gate
    hidden_out[...] = (activated * pre_up).astype(jnp.bfloat16)
    gate_grad = (
        hidden_grad * pre_up * sigmoid_gate * (1.0 + pre_gate * (1.0 - sigmoid_gate))
    ).astype(jnp.bfloat16)
    up_grad = (hidden_grad * activated).astype(jnp.bfloat16)
    gate_out[...] = gate_grad
    up_out[...] = up_grad
    me, group = lax.axis_index("expert"), lax.axis_index("dp")
    homes = []
    for index in range(count):
        source = lax.rem(group - index // near + groups, groups) * experts
        homes += [source + (me ^ (high * near + index % near)) for high in range(far)]
    copies = []
    for step in range(steps):
        at = slice(step * chunk, (step + 1) * chunk)
        value = dot_nt(gate_grad, pair[0, at, :]) + dot_nt(up_grad, pair[1, at, :])
        value = value.astype(jnp.bfloat16)
        for block, home in enumerate(homes):
            parts[home, :, at] = value[block * CAP : (block + 1) * CAP]
        where = pl.ds(step * chunk, chunk)
        one = pltpu.make_async_copy(
            parts.at[:, :, where], parts_hbm.at[:, :, where], sems.at[step]
        )
        one.start()
        copies.append(one)
    for one in copies:
        one.wait()


def expert_rows(got, pair, down, experts, groups):
    width = got[0].shape[1]
    units = down.shape[0]
    chunk = min(1024, width)
    blocks = groups * experts
    total = blocks * CAP
    return pl.pallas_call(
        functools.partial(expert_kernel, experts, groups, chunk),
        in_specs=[VMEM] * (len(got) + 2),
        out_specs=[VMEM] * 5 + [HBM],
        out_shape=[bf16(total, units)] * 3
        + [bf16(total, width)] * 2
        + [pltpu.HBM((blocks, CAP, width), jnp.bfloat16)],
        scratch_shapes=[
            pltpu.VMEM((blocks, CAP, width), jnp.bfloat16),
            pltpu.VMEM((total, units), jnp.float32),
            pltpu.VMEM((total, units), jnp.float32),
            pltpu.VMEM((total, units), jnp.float32),
            pltpu.SemaphoreType.DMA((width // chunk,)),
        ],
        compiler_params=params(28),
        cost_estimate=cost(10 * total * width * units, 6 * width * units),
        name="expert_rows",
    )(
        *got,
        pltpu.with_memory_space_constraint(pair, pltpu.VMEM),
        pltpu.with_memory_space_constraint(down, pltpu.VMEM),
    )


def pair_grad_kernel(blocks, chunk, *refs):
    toks, gate_ref, up_ref = refs[:blocks], refs[blocks], refs[blocks + 1]
    out_hbm, buffer, sems = refs[blocks + 2 :]
    width = toks[0].shape[1]
    copies = []
    for step in range(width // chunk):
        at = slice(step * chunk, (step + 1) * chunk)
        tok = jnp.concatenate([ref[:, at] for ref in toks], axis=0)
        for side, ref in enumerate((gate_ref, up_ref)):
            buffer[side, at, :] = dot_tn(tok, ref[...]).astype(jnp.bfloat16)
        where = pl.ds(step * chunk, chunk)
        one = pltpu.make_async_copy(
            buffer.at[:, where, :], out_hbm.at[0, :, where, :], sems.at[step]
        )
        one.start()
        copies.append(one)
    for one in copies:
        one.wait()


def pair_grad(toks, gate_grad, up_grad):
    blocks = len(toks)
    width = toks[0].shape[1]
    total, units = gate_grad.shape
    chunk = min(512, width)
    return pl.pallas_call(
        functools.partial(pair_grad_kernel, blocks, chunk),
        in_specs=[VMEM] * (blocks + 2),
        out_specs=HBM,
        out_shape=bf16(1, 2, width, units),
        scratch_shapes=[
            pltpu.VMEM((2, width, units), jnp.bfloat16),
            pltpu.SemaphoreType.DMA((width // chunk,)),
        ],
        compiler_params=params(32),
        cost_estimate=cost(4 * total * width * units, 4 * width * units),
        name="pair_grad",
    )(*toks, gate_grad, up_grad)


def down_grad_kernel(blocks, chunk, *refs):
    cots, hidden_ref, out_hbm = refs[:blocks], refs[blocks], refs[blocks + 1]
    buffer, sems = refs[blocks + 2 :]
    width = cots[0].shape[1]
    copies = []
    for step in range(width // chunk):
        at = slice(step * chunk, (step + 1) * chunk)
        cot = jnp.concatenate([ref[:, at] for ref in cots], axis=0)
        buffer[:, at] = dot_tn(hidden_ref[...], cot).astype(jnp.bfloat16)
        where = pl.ds(step * chunk, chunk)
        one = pltpu.make_async_copy(buffer.at[:, where], out_hbm.at[0, :, where], sems.at[step])
        one.start()
        copies.append(one)
    for one in copies:
        one.wait()


def down_grad(cots, hidden):
    blocks = len(cots)
    width = cots[0].shape[1]
    total, units = hidden.shape
    chunk = min(1024, width)
    return pl.pallas_call(
        functools.partial(down_grad_kernel, blocks, chunk),
        in_specs=[VMEM] * (blocks + 1),
        out_specs=HBM,
        out_shape=bf16(1, units, width),
        scratch_shapes=[
            pltpu.VMEM((units, width), jnp.bfloat16),
            pltpu.SemaphoreType.DMA((width // chunk,)),
        ],
        compiler_params=params(24),
        cost_estimate=cost(2 * total * width * units, 2 * width * units),
        name="down_grad",
    )(*cots, hidden)


def spread_kernel(chunk, rows_ref, place_ref, out_hbm, buffer, sems):
    blocks, _, width = rows_ref.shape
    place = jnp.concatenate([place_ref[...]] * (blocks * CAP // place_ref.shape[0]), axis=0)
    copies = []
    for step in range(width // chunk):
        at = slice(step * chunk, (step + 1) * chunk)
        rows = jnp.concatenate([rows_ref[block, :, at] for block in range(blocks)], axis=0)
        buffer[:, at] = dot_tn(place, rows).astype(jnp.bfloat16)
        where = pl.ds(step * chunk, chunk)
        one = pltpu.make_async_copy(buffer.at[:, where], out_hbm.at[:, where], sems.at[step])
        one.start()
        copies.append(one)
    for one in copies:
        one.wait()


def spread(rows, place):
    width = rows.shape[2]
    slots, tokens = place.shape
    chunk = min(1024, width)
    return pl.pallas_call(
        functools.partial(spread_kernel, chunk),
        in_specs=[VMEM] * 2,
        out_specs=HBM,
        out_shape=bf16(tokens, width),
        scratch_shapes=[
            pltpu.VMEM((tokens, width), jnp.bfloat16),
            pltpu.SemaphoreType.DMA((width // chunk,)),
        ],
        compiler_params=params(16),
        cost_estimate=cost(2 * slots * tokens * width, 2 * tokens * width),
        name="spread_rows",
    )(rows, place)


def per_device(activations, cotangent, expert_ids, gate_probs, gate_up, down_proj):
    experts = lax.axis_size("expert")
    groups = lax.axis_size("dp")
    tokens = activations.shape[0]
    far, near = factors(experts)

    def send(value, by_group, by_expert):
        if by_group == 0 and by_expert == 0:
            return value
        pairs = []
        for group in range(groups):
            to = (group + by_group) % groups
            for i in range(experts):
                pairs.append((group * experts + i, to * experts + (i ^ by_expert)))
        return lax.ppermute(value, ("dp", "expert"), pairs)

    pieces, place = route(
        expert_ids.reshape(1, tokens),
        gate_probs.reshape(1, tokens),
        activations,
        cotangent,
        experts,
    )
    pair, down = load(gate_up[0], down_proj[0], place)
    arrived = [send(pieces[high], 0, high * near) for high in reversed(range(far))]
    merged = merge(arrived[::-1], pltpu.with_memory_space_constraint(down, pltpu.VMEM))
    mine = [send(merged[low], 0, low) for low in range(near)]
    got = [send(mine[low], group, 0) for group in range(groups) for low in range(near)]
    gate_grad, up_grad, hidden, tok, cot, parts = expert_rows(got, pair, down, experts, groups)
    returned = lax.all_to_all(parts, ("dp", "expert"), split_axis=0, concat_axis=0, tiled=True)
    down_total = down_grad([cot], hidden)
    pair_total = pair_grad([tok], gate_grad, up_grad)
    input_grad = spread(returned, place)
    return input_grad, pair_total, down_total


def solution(mesh):
    rows = P(("dp", "expert"), None)
    pair, down = P("expert", None, None, "dp"), P("expert", "dp", None)
    return jax.shard_map(
        per_device,
        mesh=mesh,
        in_specs=(rows, rows, rows, rows, pair, down),
        out_specs=(rows, pair, down),
        check_vma=False,
    )
```

```python
import functools

import jax
import jax.numpy as jnp
from jax import lax
from jax.experimental import pallas as pl
from jax.experimental.pallas import tpu as pltpu
from jax.sharding import PartitionSpec as P

CAP = 2
MIB = 1024 * 1024
VMEM = pl.BlockSpec(memory_space=pltpu.VMEM)
HBM = pl.BlockSpec(memory_space=pltpu.HBM)


def dot_nn(a, b):
    return lax.dot_general(a, b, (((1,), (0,)), ((), ())), preferred_element_type=jnp.float32)


def dot_nt(a, b):
    return lax.dot_general(a, b, (((1,), (1,)), ((), ())), preferred_element_type=jnp.float32)


def dot_tn(a, b):
    return lax.dot_general(a, b, (((0,), (0,)), ((), ())), preferred_element_type=jnp.float32)


def cost(flops, moved):
    return pl.CostEstimate(flops=int(flops), bytes_accessed=int(moved), transcendentals=0)


def params(mib):
    return pltpu.CompilerParams(vmem_limit_bytes=mib * MIB)


def in_hbm(value):
    return pltpu.with_memory_space_constraint(value, pltpu.HBM)


def bf16(*shape):
    return jax.ShapeDtypeStruct(shape, jnp.bfloat16)


def factors(experts):
    far = 1
    while 4 * far * far <= experts:
        far *= 2
    return far, experts // far


def route_kernel(experts, chunk, ids_hbm, probs_hbm, act_hbm, cot_hbm, *refs):
    far, near = factors(experts)
    sends, place_ref = refs[:far], refs[far]
    ids_ref, probs_ref, act, cot, sems = refs[far + 1 :]
    tokens, width = act.shape
    steps = width // chunk
    small = (
        pltpu.make_async_copy(ids_hbm, ids_ref, sems.at[2 * steps]),
        pltpu.make_async_copy(probs_hbm, probs_ref, sems.at[2 * steps + 1]),
    )
    large = []
    for step in range(steps):
        at = pl.ds(step * chunk, chunk)
        large.append(
            (
                pltpu.make_async_copy(act_hbm.at[:, at], act.at[:, at], sems.at[2 * step]),
                pltpu.make_async_copy(cot_hbm.at[:, at], cot.at[:, at], sems.at[2 * step + 1]),
            )
        )
    for one in small:
        one.start()
    for pair in large:
        for one in pair:
            one.start()
    for one in small:
        one.wait()

    me = lax.axis_index("expert")
    ids = ids_ref[...]
    inside = ids < experts
    units = lax.broadcasted_iota(jnp.int32, (experts, tokens), 0)
    onehot = jnp.where(units == ids, 1.0, 0.0)
    earlier = lax.broadcasted_iota(jnp.int32, (tokens, tokens), 0) < lax.broadcasted_iota(
        jnp.int32, (tokens, tokens), 1
    )
    before = dot_nn(onehot.astype(jnp.bfloat16), jnp.where(earlier, 1.0, 0.0).astype(jnp.bfloat16))
    rank = jnp.sum(before * onehot, axis=0, keepdims=True).astype(jnp.int32)
    slots = lax.broadcasted_iota(jnp.int32, (experts * CAP, tokens), 0)
    slot = jnp.where(inside, ids * CAP + rank, -1)
    place_ref[...] = jnp.where(slots == slot, 1.0, 0.0).astype(jnp.bfloat16)
    turned = jnp.where(inside, (ids ^ me) * CAP + rank, -1)
    pick = jnp.where(slots == turned, 1.0, 0.0)
    weight = jnp.sum(pick * probs_ref[...], axis=1, keepdims=True)
    pick = pick.astype(jnp.bfloat16)
    for step in range(steps):
        at = slice(step * chunk, (step + 1) * chunk)
        for one in large[step]:
            one.wait()
        rows_tok = dot_nn(pick, act[:, at]).astype(jnp.bfloat16)
        rows_cot = (weight * dot_nn(pick, cot[:, at])).astype(jnp.bfloat16)
        for unit in range(experts):
            rows = slice(unit * CAP, (unit + 1) * CAP)
            sends[unit // near][unit % near, :CAP, at] = rows_tok[rows]
            sends[unit // near][unit % near, CAP:, at] = rows_cot[rows]


def route(ids, probs, act, cot, experts):
    tokens, width = act.shape
    chunk = min(1024, width)
    far, near = factors(experts)
    out = pl.pallas_call(
        functools.partial(route_kernel, experts, chunk),
        in_specs=[HBM] * 4,
        out_specs=[VMEM] * (far + 1),
        out_shape=[bf16(near, 2 * CAP, width)] * far + [bf16(experts * CAP, tokens)],
        scratch_shapes=[
            pltpu.VMEM((1, tokens), jnp.int32),
            pltpu.VMEM((1, tokens), jnp.float32),
            pltpu.VMEM((tokens, width), jnp.bfloat16),
            pltpu.VMEM((tokens, width), jnp.bfloat16),
            pltpu.SemaphoreType.DMA((2 * (width // chunk) + 2,)),
        ],
        compiler_params=params(16),
        cost_estimate=cost(4 * experts * CAP * tokens * width, 4 * tokens * width),
        name="route_rows",
    )(in_hbm(ids), in_hbm(probs), in_hbm(act), in_hbm(cot))
    return out[:far], out[far]


def merge_kernel(far, *refs):
    pieces, outs = refs[:far], refs[len(refs) - refs[0].shape[0] :]
    for index, out in enumerate(outs):
        rows = [piece[index, :CAP, :] for piece in pieces]
        rows += [piece[index, CAP:, :] for piece in pieces]
        out[...] = jnp.concatenate(rows, axis=0)


def merge(pieces, after=()):
    far = len(pieces)
    near, _, width = pieces[0].shape
    return pl.pallas_call(
        functools.partial(merge_kernel, far),
        in_specs=[VMEM] * far + [pl.BlockSpec(memory_space=pl.ANY)] * len(after),
        out_specs=[VMEM] * near,
        out_shape=[bf16(2 * CAP * far, width)] * near,
        compiler_params=params(16),
        cost_estimate=cost(0, 8 * near * CAP * far * width),
        name="merge_rows",
    )(*pieces, *after)


def load_kernel(chunk, pair_hbm, after, pair, sems):
    del after
    width = pair.shape[1]
    copies = []
    for step in range(width // chunk):
        at = pl.ds(step * chunk, chunk)
        one = pltpu.make_async_copy(pair_hbm.at[:, at, :], pair.at[:, at, :], sems.at[step])
        one.start()
        copies.append(one)
    for one in copies:
        one.wait()


def load(pair, after):
    _, width, units = pair.shape
    chunk = min(1024, width)
    return pl.pallas_call(
        functools.partial(load_kernel, chunk),
        in_specs=[HBM, pl.BlockSpec(memory_space=pl.ANY)],
        out_specs=VMEM,
        out_shape=pltpu.VMEM(pair.shape, jnp.bfloat16),
        scratch_shapes=[pltpu.SemaphoreType.DMA((width // chunk,))],
        compiler_params=params(20),
        cost_estimate=cost(0, 4 * width * units),
        name="load_weights",
    )(in_hbm(pair), after)


def expert_kernel(homes, experts, groups, chunk, count, *refs):
    got, pair, down_hbm = refs[:count], refs[count], refs[count + 1]
    gate_out, up_out, hidden_out, tok_all, cot_all, parts_hbm = refs[count + 2 : count + 8]
    down, parts, acc_gate, acc_up, acc_hid, sems = refs[count + 8 :]
    width = got[0].shape[1]
    steps = width // chunk
    downs = []
    for step in range(steps):
        at = pl.ds(step * chunk, chunk)
        one = pltpu.make_async_copy(down_hbm.at[:, at], down.at[:, at], sems.at[0, step])
        one.start()
        downs.append(one)
    for step in range(steps):
        at = slice(step * chunk, (step + 1) * chunk)
        tok = [piece[: piece.shape[0] // 2, at] for piece in got]
        cot = [piece[piece.shape[0] // 2 :, at] for piece in got]
        tok_all[:, at] = jnp.concatenate(tok, axis=0)
        cot_all[:, at] = jnp.concatenate(cot, axis=0)
        gate = dot_nn(tok_all[:, at], pair[0, at, :])
        up = dot_nn(tok_all[:, at], pair[1, at, :])
        if step == 0:
            acc_gate[...], acc_up[...] = gate, up
        else:
            acc_gate[...] += gate
            acc_up[...] += up
    for step in range(steps):
        at = slice(step * chunk, (step + 1) * chunk)
        downs[step].wait()
        hid = dot_nt(cot_all[:, at], down[:, at])
        if step == 0:
            acc_hid[...] = hid
        else:
            acc_hid[...] += hid
    pre_gate, pre_up, hidden_grad = acc_gate[...], acc_up[...], acc_hid[...]
    sigmoid_gate = jax.nn.sigmoid(pre_gate)
    activated = pre_gate * sigmoid_gate
    hidden_out[...] = (activated * pre_up).astype(jnp.bfloat16)
    gate_grad = (
        hidden_grad * pre_up * sigmoid_gate * (1.0 + pre_gate * (1.0 - sigmoid_gate))
    ).astype(jnp.bfloat16)
    up_grad = (hidden_grad * activated).astype(jnp.bfloat16)
    gate_out[...] = gate_grad
    up_out[...] = up_grad
    me, group = lax.axis_index("expert"), lax.axis_index("dp")
    rows = [
        lax.rem(group - back + groups, groups) * experts + (me ^ turn) for back, turn in homes
    ]
    copies = []
    for step in range(steps):
        at = slice(step * chunk, (step + 1) * chunk)
        value = dot_nt(gate_grad, pair[0, at, :]) + dot_nt(up_grad, pair[1, at, :])
        value = value.astype(jnp.bfloat16)
        for block, row in enumerate(rows):
            parts[row, :, at] = value[block * CAP : (block + 1) * CAP]
        where = pl.ds(step * chunk, chunk)
        one = pltpu.make_async_copy(
            parts.at[:, :, where], parts_hbm.at[:, :, where], sems.at[1, step]
        )
        one.start()
        copies.append(one)
    for one in copies:
        one.wait()


def expert_rows(got, homes, pair, down, experts, groups):
    width = got[0].shape[1]
    units = down.shape[0]
    chunk = min(1024, width)
    blocks = groups * experts
    total = blocks * CAP
    return pl.pallas_call(
        functools.partial(expert_kernel, homes, experts, groups, chunk, len(got)),
        in_specs=[VMEM] * (len(got) + 1) + [HBM],
        out_specs=[VMEM] * 5 + [HBM],
        out_shape=[bf16(total, units)] * 3
        + [bf16(total, width)] * 2
        + [pltpu.HBM((blocks, CAP, width), jnp.bfloat16)],
        scratch_shapes=[
            pltpu.VMEM(down.shape, jnp.bfloat16),
            pltpu.VMEM((blocks, CAP, width), jnp.bfloat16),
            pltpu.VMEM((total, units), jnp.float32),
            pltpu.VMEM((total, units), jnp.float32),
            pltpu.VMEM((total, units), jnp.float32),
            pltpu.SemaphoreType.DMA((2, width // chunk)),
        ],
        compiler_params=params(28),
        cost_estimate=cost(10 * total * width * units, 6 * width * units),
        name="expert_rows",
    )(*got, pltpu.with_memory_space_constraint(pair, pltpu.VMEM), in_hbm(down))


def pair_grad_kernel(blocks, chunk, *refs):
    toks, gate_ref, up_ref = refs[:blocks], refs[blocks], refs[blocks + 1]
    out_hbm, buffer, sems = refs[blocks + 2 :]
    width = toks[0].shape[1]
    copies = []
    for step in range(width // chunk):
        at = slice(step * chunk, (step + 1) * chunk)
        tok = jnp.concatenate([ref[:, at] for ref in toks], axis=0)
        for side, ref in enumerate((gate_ref, up_ref)):
            buffer[side, at, :] = dot_tn(tok, ref[...]).astype(jnp.bfloat16)
        where = pl.ds(step * chunk, chunk)
        one = pltpu.make_async_copy(
            buffer.at[:, where, :], out_hbm.at[0, :, where, :], sems.at[step]
        )
        one.start()
        copies.append(one)
    for one in copies:
        one.wait()


def pair_grad(toks, gate_grad, up_grad):
    blocks = len(toks)
    width = toks[0].shape[1]
    total, units = gate_grad.shape
    chunk = min(512, width)
    return pl.pallas_call(
        functools.partial(pair_grad_kernel, blocks, chunk),
        in_specs=[VMEM] * (blocks + 2),
        out_specs=HBM,
        out_shape=bf16(1, 2, width, units),
        scratch_shapes=[
            pltpu.VMEM((2, width, units), jnp.bfloat16),
            pltpu.SemaphoreType.DMA((width // chunk,)),
        ],
        compiler_params=params(32),
        cost_estimate=cost(4 * total * width * units, 4 * width * units),
        name="pair_grad",
    )(*toks, gate_grad, up_grad)


def down_grad_kernel(blocks, chunk, *refs):
    cots, hidden_ref, out_hbm = refs[:blocks], refs[blocks], refs[blocks + 1]
    buffer, sems = refs[blocks + 2 :]
    width = cots[0].shape[1]
    copies = []
    for step in range(width // chunk):
        at = slice(step * chunk, (step + 1) * chunk)
        cot = jnp.concatenate([ref[:, at] for ref in cots], axis=0)
        buffer[:, at] = dot_tn(hidden_ref[...], cot).astype(jnp.bfloat16)
        where = pl.ds(step * chunk, chunk)
        one = pltpu.make_async_copy(buffer.at[:, where], out_hbm.at[0, :, where], sems.at[step])
        one.start()
        copies.append(one)
    for one in copies:
        one.wait()


def down_grad(cots, hidden):
    blocks = len(cots)
    width = cots[0].shape[1]
    total, units = hidden.shape
    chunk = min(1024, width)
    return pl.pallas_call(
        functools.partial(down_grad_kernel, blocks, chunk),
        in_specs=[VMEM] * (blocks + 1),
        out_specs=HBM,
        out_shape=bf16(1, units, width),
        scratch_shapes=[
            pltpu.VMEM((units, width), jnp.bfloat16),
            pltpu.SemaphoreType.DMA((width // chunk,)),
        ],
        compiler_params=params(24),
        cost_estimate=cost(2 * total * width * units, 2 * width * units),
        name="down_grad",
    )(*cots, hidden)


def spread_kernel(chunk, rows_ref, place_ref, out_hbm, buffer, sems):
    blocks, _, width = rows_ref.shape
    place = jnp.concatenate([place_ref[...]] * (blocks * CAP // place_ref.shape[0]), axis=0)
    copies = []
    for step in range(width // chunk):
        at = slice(step * chunk, (step + 1) * chunk)
        rows = jnp.concatenate([rows_ref[block, :, at] for block in range(blocks)], axis=0)
        buffer[:, at] = dot_tn(place, rows).astype(jnp.bfloat16)
        where = pl.ds(step * chunk, chunk)
        one = pltpu.make_async_copy(buffer.at[:, where], out_hbm.at[:, where], sems.at[step])
        one.start()
        copies.append(one)
    for one in copies:
        one.wait()


def spread(rows, place):
    width = rows.shape[2]
    slots, tokens = place.shape
    chunk = min(1024, width)
    return pl.pallas_call(
        functools.partial(spread_kernel, chunk),
        in_specs=[VMEM] * 2,
        out_specs=HBM,
        out_shape=bf16(tokens, width),
        scratch_shapes=[
            pltpu.VMEM((tokens, width), jnp.bfloat16),
            pltpu.SemaphoreType.DMA((width // chunk,)),
        ],
        compiler_params=params(16),
        cost_estimate=cost(2 * slots * tokens * width, 2 * tokens * width),
        name="spread_rows",
    )(rows, place)


def per_device(activations, cotangent, expert_ids, gate_probs, gate_up, down_proj):
    experts = lax.axis_size("expert")
    groups = lax.axis_size("dp")
    tokens = activations.shape[0]
    far, near = factors(experts)

    def send(value, by_group, by_expert):
        if by_group == 0 and by_expert == 0:
            return value
        pairs = []
        for group in range(groups):
            to = (group + by_group) % groups
            for i in range(experts):
                pairs.append((group * experts + i, to * experts + (i ^ by_expert)))
        return lax.ppermute(value, ("dp", "expert"), pairs)

    pieces, place = route(
        expert_ids.reshape(1, tokens),
        gate_probs.reshape(1, tokens),
        activations,
        cotangent,
        experts,
    )
    early, late = range(far // 2), range(far // 2, far)
    arrived = [send(pieces[high], 0, high * near) for high in late]
    both = [send(pieces[high], group, high * near) for group in range(groups) for high in early]
    pair = load(gate_up[0], place)
    both = merge(both)
    loaded = pltpu.with_memory_space_constraint(pair, pltpu.VMEM)
    own = merge(arrived, (loaded, both[0]))
    got = [send(both[low], 0, low) for low in range(near)]
    mine = [send(own[low], 0, low) for low in range(near)]
    got += [send(mine[low], group, 0) for group in range(groups) for low in range(near)]
    homes = [
        (group, high * near + low)
        for low in range(near)
        for group in range(groups)
        for high in early
    ]
    homes += [
        (group, high * near + low)
        for group in range(groups)
        for low in range(near)
        for high in late
    ]
    gate_grad, up_grad, hidden, tok, cot, parts = expert_rows(
        got, homes, pair, down_proj[0], experts, groups
    )
    returned = lax.all_to_all(parts, ("dp", "expert"), split_axis=0, concat_axis=0, tiled=True)
    down_total = down_grad([cot], hidden)
    pair_total = pair_grad([tok], gate_grad, up_grad)
    input_grad = spread(returned, place)
    return input_grad, pair_total, down_total


def solution(mesh):
    rows = P(("dp", "expert"), None)
    pair, down = P("expert", None, None, "dp"), P("expert", "dp", None)
    return jax.shard_map(
        per_device,
        mesh=mesh,
        in_specs=(rows, rows, rows, rows, pair, down),
        out_specs=(rows, pair, down),
        check_vma=False,
    )
```

```python
import functools

import jax
import jax.numpy as jnp
from jax import lax
from jax.experimental import pallas as pl
from jax.experimental.pallas import tpu as pltpu
from jax.sharding import PartitionSpec as P

CAP = 2
HALVES = 2
MIB = 1024 * 1024
VMEM = pl.BlockSpec(memory_space=pltpu.VMEM)
HBM = pl.BlockSpec(memory_space=pltpu.HBM)


def dot_nn(a, b):
    return lax.dot_general(a, b, (((1,), (0,)), ((), ())), preferred_element_type=jnp.float32)


def dot_nt(a, b):
    return lax.dot_general(a, b, (((1,), (1,)), ((), ())), preferred_element_type=jnp.float32)


def dot_tn(a, b):
    return lax.dot_general(a, b, (((0,), (0,)), ((), ())), preferred_element_type=jnp.float32)


def cost(flops, moved):
    return pl.CostEstimate(flops=int(flops), bytes_accessed=int(moved), transcendentals=0)


def params(mib):
    return pltpu.CompilerParams(vmem_limit_bytes=mib * MIB)


def in_hbm(value):
    return pltpu.with_memory_space_constraint(value, pltpu.HBM)


def bf16(*shape):
    return jax.ShapeDtypeStruct(shape, jnp.bfloat16)


def factors(experts):
    far = 1
    while 4 * far * far <= experts:
        far *= 2
    return far, experts // far


def route_kernel(experts, chunk, ids_hbm, probs_hbm, act_hbm, cot_hbm, *refs):
    far, near = factors(experts)
    sends, place_ref = refs[: HALVES * far], refs[HALVES * far]
    ids_ref, probs_ref, act, cot, sems = refs[HALVES * far + 1 :]
    tokens, width = act.shape
    half = width // HALVES
    steps = width // chunk
    small = (
        pltpu.make_async_copy(ids_hbm, ids_ref, sems.at[2 * steps]),
        pltpu.make_async_copy(probs_hbm, probs_ref, sems.at[2 * steps + 1]),
    )
    large = []
    for step in range(steps):
        at = pl.ds(step * chunk, chunk)
        large.append(
            (
                pltpu.make_async_copy(act_hbm.at[:, at], act.at[:, at], sems.at[2 * step]),
                pltpu.make_async_copy(cot_hbm.at[:, at], cot.at[:, at], sems.at[2 * step + 1]),
            )
        )
    for one in small:
        one.start()
    for pair in large:
        for one in pair:
            one.start()
    for one in small:
        one.wait()

    me = lax.axis_index("expert")
    ids = ids_ref[...]
    inside = ids < experts
    units = lax.broadcasted_iota(jnp.int32, (experts, tokens), 0)
    onehot = jnp.where(units == ids, 1.0, 0.0)
    earlier = lax.broadcasted_iota(jnp.int32, (tokens, tokens), 0) < lax.broadcasted_iota(
        jnp.int32, (tokens, tokens), 1
    )
    before = dot_nn(onehot.astype(jnp.bfloat16), jnp.where(earlier, 1.0, 0.0).astype(jnp.bfloat16))
    rank = jnp.sum(before * onehot, axis=0, keepdims=True).astype(jnp.int32)
    slots = lax.broadcasted_iota(jnp.int32, (experts * CAP, tokens), 0)
    slot = jnp.where(inside, ids * CAP + rank, -1)
    place_ref[...] = jnp.where(slots == slot, 1.0, 0.0).astype(jnp.bfloat16)
    turned = jnp.where(inside, (ids ^ me) * CAP + rank, -1)
    pick = jnp.where(slots == turned, 1.0, 0.0)
    weight = jnp.sum(pick * probs_ref[...], axis=1, keepdims=True)
    pick = pick.astype(jnp.bfloat16)
    for step in range(steps):
        at = slice(step * chunk, (step + 1) * chunk)
        for one in large[step]:
            one.wait()
        rows_tok = dot_nn(pick, act[:, at]).astype(jnp.bfloat16)
        rows_cot = (weight * dot_nn(pick, cot[:, at])).astype(jnp.bfloat16)
        for unit in range(experts):
            rows = slice(unit * CAP, (unit + 1) * CAP)
            target = sends[step * chunk // half * far + unit // near]
            there = slice(step * chunk % half, step * chunk % half + chunk)
            target[unit % near, :CAP, there] = rows_tok[rows]
            target[unit % near, CAP:, there] = rows_cot[rows]


def route(ids, probs, act, cot, experts):
    tokens, width = act.shape
    chunk = min(1024, width // HALVES)
    far, near = factors(experts)
    out = pl.pallas_call(
        functools.partial(route_kernel, experts, chunk),
        in_specs=[HBM] * 4,
        out_specs=[VMEM] * (HALVES * far + 1),
        out_shape=[bf16(near, 2 * CAP, width // HALVES)] * (HALVES * far)
        + [bf16(experts * CAP, tokens)],
        scratch_shapes=[
            pltpu.VMEM((1, tokens), jnp.int32),
            pltpu.VMEM((1, tokens), jnp.float32),
            pltpu.VMEM((tokens, width), jnp.bfloat16),
            pltpu.VMEM((tokens, width), jnp.bfloat16),
            pltpu.SemaphoreType.DMA((2 * (width // chunk) + 2,)),
        ],
        compiler_params=params(16),
        cost_estimate=cost(4 * experts * CAP * tokens * width, 4 * tokens * width),
        name="route_rows",
    )(in_hbm(ids), in_hbm(probs), in_hbm(act), in_hbm(cot))
    return [out[half * far : (half + 1) * far] for half in range(HALVES)], out[HALVES * far]


def merge_kernel(far, *refs):
    pieces, outs = refs[:far], refs[far:]
    for index, out in enumerate(outs):
        rows = [piece[index, :CAP, :] for piece in pieces]
        rows += [piece[index, CAP:, :] for piece in pieces]
        out[...] = jnp.concatenate(rows, axis=0)


def merge(pieces):
    far = len(pieces)
    near, _, width = pieces[0].shape
    return pl.pallas_call(
        functools.partial(merge_kernel, far),
        in_specs=[VMEM] * far,
        out_specs=[VMEM] * near,
        out_shape=[bf16(2 * CAP * far, width)] * near,
        compiler_params=params(16),
        cost_estimate=cost(0, 8 * near * CAP * far * width),
        name="merge_rows",
    )(*pieces)


def stack_kernel(number, *refs):
    pieces, out = refs[:number], refs[number]
    rows = pieces[0].shape[0] // 2
    for index, piece in enumerate(pieces):
        out[index * rows : (index + 1) * rows, :] = piece[:rows, :]
        out[(number + index) * rows : (number + index + 1) * rows, :] = piece[rows:, :]


def stack(pieces):
    number = len(pieces)
    rows, width = pieces[0].shape
    return pl.pallas_call(
        functools.partial(stack_kernel, number),
        in_specs=[VMEM] * number,
        out_specs=VMEM,
        out_shape=bf16(number * rows, width),
        compiler_params=params(16),
        cost_estimate=cost(0, 4 * number * rows * width),
        name="stack_rows",
    )(*pieces)


def upper(refs, at):
    return jnp.concatenate([ref[: ref.shape[0] // 2, at] for ref in refs], axis=0)


def lower(refs, at):
    return jnp.concatenate([ref[ref.shape[0] // 2 :, at] for ref in refs], axis=0)


def first_kernel(groups, chunk, *refs):
    rows, pair_hbm, down_hbm = refs[:groups], refs[groups], refs[groups + 1]
    gate, up, hid, pair, down, sems = refs[groups + 2 :]
    half, width = rows[0].shape[1], down.shape[1]
    pairs, downs = [], []
    for step in range(width // chunk):
        at = pl.ds(step * chunk, chunk)
        pairs.append(
            pltpu.make_async_copy(pair_hbm.at[:, at, :], pair.at[:, at, :], sems.at[0, step])
        )
        downs.append(pltpu.make_async_copy(down_hbm.at[:, at], down.at[:, at], sems.at[1, step]))
        pairs[step].start()
        downs[step].start()
    for step in range(half // chunk):
        at = slice(step * chunk, (step + 1) * chunk)
        tok, cot = upper(rows, at), lower(rows, at)
        pairs[step].wait()
        part_gate = dot_nn(tok, pair[0, at, :])
        part_up = dot_nn(tok, pair[1, at, :])
        downs[step].wait()
        part_hid = dot_nt(cot, down[:, at])
        if step == 0:
            gate[...], up[...], hid[...] = part_gate, part_up, part_hid
        else:
            gate[...] += part_gate
            up[...] += part_up
            hid[...] += part_hid
    for step in range(half // chunk, width // chunk):
        pairs[step].wait()
        downs[step].wait()


def first_half(rows, pair, down):
    groups = len(rows)
    total = groups * rows[0].shape[0] // 2
    half = rows[0].shape[1]
    units, width = down.shape
    chunk = min(1024, half)
    return pl.pallas_call(
        functools.partial(first_kernel, groups, chunk),
        in_specs=[VMEM] * groups + [HBM] * 2,
        out_specs=[VMEM] * 5,
        out_shape=[jax.ShapeDtypeStruct((total, units), jnp.float32)] * 3
        + [pltpu.VMEM(pair.shape, jnp.bfloat16), pltpu.VMEM(down.shape, jnp.bfloat16)],
        scratch_shapes=[pltpu.SemaphoreType.DMA((2, width // chunk))],
        compiler_params=params(28),
        cost_estimate=cost(6 * total * half * units, 6 * width * units),
        name="first_half",
    )(*rows, in_hbm(pair), in_hbm(down))


def second_kernel(homes, experts, groups, chunk, *refs):
    rows, sums = refs[:groups], refs[groups : groups + 3]
    pair, down = refs[groups + 3 : groups + 5]
    gate_out, up_out, hidden_out, parts_hbm, parts, sems = refs[groups + 5 :]
    half, width = rows[0].shape[1], down.shape[1]
    pre_gate, pre_up, hidden_grad = (ref[...] for ref in sums)
    for step in range(half // chunk):
        at = slice(step * chunk, (step + 1) * chunk)
        there = slice(half + step * chunk, half + (step + 1) * chunk)
        tok, cot = upper(rows, at), lower(rows, at)
        pre_gate = pre_gate + dot_nn(tok, pair[0, there, :])
        pre_up = pre_up + dot_nn(tok, pair[1, there, :])
        hidden_grad = hidden_grad + dot_nt(cot, down[:, there])
    sigmoid_gate = jax.nn.sigmoid(pre_gate)
    activated = pre_gate * sigmoid_gate
    hidden_out[...] = (activated * pre_up).astype(jnp.bfloat16)
    gate_grad = (
        hidden_grad * pre_up * sigmoid_gate * (1.0 + pre_gate * (1.0 - sigmoid_gate))
    ).astype(jnp.bfloat16)
    up_grad = (hidden_grad * activated).astype(jnp.bfloat16)
    gate_out[...] = gate_grad
    up_out[...] = up_grad
    me, group = lax.axis_index("expert"), lax.axis_index("dp")
    targets = [
        lax.rem(group - back + groups, groups) * experts + (me ^ turn) for back, turn in homes
    ]
    copies = []
    for step in range(width // chunk):
        at = slice(step * chunk, (step + 1) * chunk)
        value = dot_nt(gate_grad, pair[0, at, :]) + dot_nt(up_grad, pair[1, at, :])
        value = value.astype(jnp.bfloat16)
        for block, target in enumerate(targets):
            parts[target, :, at] = value[block * CAP : (block + 1) * CAP]
        where = pl.ds(step * chunk, chunk)
        one = pltpu.make_async_copy(
            parts.at[:, :, where], parts_hbm.at[:, :, where], sems.at[step]
        )
        one.start()
        copies.append(one)
    for one in copies:
        one.wait()


def second_half(rows, sums, pair, down, homes, experts):
    groups = len(rows)
    total, units = sums[0].shape
    half, width = rows[0].shape[1], down.shape[1]
    chunk = min(1024, half)
    blocks = total // CAP
    return pl.pallas_call(
        functools.partial(second_kernel, homes, experts, groups, chunk),
        in_specs=[VMEM] * (groups + 5),
        out_specs=[VMEM] * 3 + [HBM],
        out_shape=[bf16(total, units)] * 3 + [pltpu.HBM((blocks, CAP, width), jnp.bfloat16)],
        scratch_shapes=[
            pltpu.VMEM((blocks, CAP, width), jnp.bfloat16),
            pltpu.SemaphoreType.DMA((width // chunk,)),
        ],
        compiler_params=params(28),
        cost_estimate=cost(7 * total * width * units, 6 * width * units),
        name="second_half",
    )(
        *rows,
        *sums,
        pltpu.with_memory_space_constraint(pair, pltpu.VMEM),
        pltpu.with_memory_space_constraint(down, pltpu.VMEM),
    )


def pair_grad_kernel(groups, chunk, *refs):
    rows, gate_ref, up_ref = refs[: HALVES * groups], refs[HALVES * groups], refs[HALVES * groups + 1]
    out_hbm, buffer, sems = refs[HALVES * groups + 2 :]
    half = rows[0].shape[1]
    copies = []
    for step in range(HALVES * half // chunk):
        at = slice(step * chunk, (step + 1) * chunk)
        there = slice(step * chunk % half, step * chunk % half + chunk)
        which = step * chunk // half
        tok = upper(rows[which * groups : (which + 1) * groups], there)
        for side, ref in enumerate((gate_ref, up_ref)):
            buffer[side, at, :] = dot_tn(tok, ref[...]).astype(jnp.bfloat16)
        where = pl.ds(step * chunk, chunk)
        one = pltpu.make_async_copy(
            buffer.at[:, where, :], out_hbm.at[0, :, where, :], sems.at[step]
        )
        one.start()
        copies.append(one)
    for one in copies:
        one.wait()


def pair_grad(rows, gate_grad, up_grad):
    groups = len(rows) // HALVES
    width = HALVES * rows[0].shape[1]
    total, units = gate_grad.shape
    chunk = min(512, width // HALVES)
    return pl.pallas_call(
        functools.partial(pair_grad_kernel, groups, chunk),
        in_specs=[VMEM] * (len(rows) + 2),
        out_specs=HBM,
        out_shape=bf16(1, 2, width, units),
        scratch_shapes=[
            pltpu.VMEM((2, width, units), jnp.bfloat16),
            pltpu.SemaphoreType.DMA((width // chunk,)),
        ],
        compiler_params=params(32),
        cost_estimate=cost(4 * total * width * units, 4 * width * units),
        name="pair_grad",
    )(*rows, gate_grad, up_grad)


def down_grad_kernel(groups, chunk, *refs):
    rows, hidden_ref = refs[: HALVES * groups], refs[HALVES * groups]
    out_hbm, buffer, sems = refs[HALVES * groups + 1 :]
    half = rows[0].shape[1]
    copies = []
    for step in range(HALVES * half // chunk):
        at = slice(step * chunk, (step + 1) * chunk)
        there = slice(step * chunk % half, step * chunk % half + chunk)
        which = step * chunk // half
        cot = lower(rows[which * groups : (which + 1) * groups], there)
        buffer[:, at] = dot_tn(hidden_ref[...], cot).astype(jnp.bfloat16)
        where = pl.ds(step * chunk, chunk)
        one = pltpu.make_async_copy(buffer.at[:, where], out_hbm.at[0, :, where], sems.at[step])
        one.start()
        copies.append(one)
    for one in copies:
        one.wait()


def down_grad(rows, hidden):
    groups = len(rows) // HALVES
    width = HALVES * rows[0].shape[1]
    total, units = hidden.shape
    chunk = min(1024, width // HALVES)
    return pl.pallas_call(
        functools.partial(down_grad_kernel, groups, chunk),
        in_specs=[VMEM] * (len(rows) + 1),
        out_specs=HBM,
        out_shape=bf16(1, units, width),
        scratch_shapes=[
            pltpu.VMEM((units, width), jnp.bfloat16),
            pltpu.SemaphoreType.DMA((width // chunk,)),
        ],
        compiler_params=params(24),
        cost_estimate=cost(2 * total * width * units, 2 * width * units),
        name="down_grad",
    )(*rows, hidden)


def spread_kernel(chunk, rows_ref, place_ref, out_hbm, buffer, sems):
    blocks, _, width = rows_ref.shape
    place = jnp.concatenate([place_ref[...]] * (blocks * CAP // place_ref.shape[0]), axis=0)
    copies = []
    for step in range(width // chunk):
        at = slice(step * chunk, (step + 1) * chunk)
        rows = jnp.concatenate([rows_ref[block, :, at] for block in range(blocks)], axis=0)
        buffer[:, at] = dot_tn(place, rows).astype(jnp.bfloat16)
        where = pl.ds(step * chunk, chunk)
        one = pltpu.make_async_copy(buffer.at[:, where], out_hbm.at[:, where], sems.at[step])
        one.start()
        copies.append(one)
    for one in copies:
        one.wait()


def spread(rows, place):
    width = rows.shape[2]
    slots, tokens = place.shape
    chunk = min(1024, width)
    return pl.pallas_call(
        functools.partial(spread_kernel, chunk),
        in_specs=[VMEM] * 2,
        out_specs=HBM,
        out_shape=bf16(tokens, width),
        scratch_shapes=[
            pltpu.VMEM((tokens, width), jnp.bfloat16),
            pltpu.SemaphoreType.DMA((width // chunk,)),
        ],
        compiler_params=params(16),
        cost_estimate=cost(2 * slots * tokens * width, 2 * tokens * width),
        name="spread_rows",
    )(rows, place)


def per_device(activations, cotangent, expert_ids, gate_probs, gate_up, down_proj):
    experts = lax.axis_size("expert")
    groups = lax.axis_size("dp")
    tokens = activations.shape[0]
    far, near = factors(experts)

    def send(value, by_group, by_expert):
        if by_group == 0 and by_expert == 0:
            return value
        pairs = []
        for group in range(groups):
            to = (group + by_group) % groups
            for i in range(experts):
                pairs.append((group * experts + i, to * experts + (i ^ by_expert)))
        return lax.ppermute(value, ("dp", "expert"), pairs)

    pieces, place = route(
        expert_ids.reshape(1, tokens),
        gate_probs.reshape(1, tokens),
        activations,
        cotangent,
        experts,
    )
    halves = []
    for half in range(HALVES):
        merged = merge([send(pieces[half][high], 0, high * near) for high in range(far)])
        own = stack([send(merged[low], 0, low) for low in range(near)])
        halves.append([send(own, group, 0) for group in range(groups)])
    homes = [
        (group, high * near + low)
        for group in range(groups)
        for low in range(near)
        for high in range(far)
    ]
    *sums, pair, down = first_half(halves[0], gate_up[0], down_proj[0])
    gate_grad, up_grad, hidden, parts = second_half(halves[1], sums, pair, down, homes, experts)
    rows = halves[0] + halves[1]
    returned = lax.all_to_all(parts, ("dp", "expert"), split_axis=0, concat_axis=0, tiled=True)
    down_total = down_grad(rows, hidden)
    pair_total = pair_grad(rows, gate_grad, up_grad)
    input_grad = spread(returned, place)
    return input_grad, pair_total, down_total


def solution(mesh):
    rows = P(("dp", "expert"), None)
    pair, down = P("expert", None, None, "dp"), P("expert", "dp", None)
    return jax.shard_map(
        per_device,
        mesh=mesh,
        in_specs=(rows, rows, rows, rows, pair, down),
        out_specs=(rows, pair, down),
        check_vma=False,
    )
```

```python
import functools

import jax
import jax.numpy as jnp
from jax import lax
from jax.experimental import pallas as pl
from jax.experimental.pallas import tpu as pltpu
from jax.sharding import PartitionSpec as P

CAP = 2
MIB = 1024 * 1024
VMEM = pl.BlockSpec(memory_space=pltpu.VMEM)
HBM = pl.BlockSpec(memory_space=pltpu.HBM)


def dot_nn(a, b):
    return lax.dot_general(a, b, (((1,), (0,)), ((), ())), preferred_element_type=jnp.float32)


def dot_nt(a, b):
    return lax.dot_general(a, b, (((1,), (1,)), ((), ())), preferred_element_type=jnp.float32)


def dot_tn(a, b):
    return lax.dot_general(a, b, (((0,), (0,)), ((), ())), preferred_element_type=jnp.float32)


def cost(flops, moved):
    return pl.CostEstimate(flops=int(flops), bytes_accessed=int(moved), transcendentals=0)


def params(mib):
    return pltpu.CompilerParams(vmem_limit_bytes=mib * MIB)


def in_hbm(value):
    return pltpu.with_memory_space_constraint(value, pltpu.HBM)


def bf16(*shape):
    return jax.ShapeDtypeStruct(shape, jnp.bfloat16)


def factors(experts):
    far = 1
    while 4 * far * far <= experts:
        far *= 2
    return far, experts // far


def route_kernel(experts, chunk, ids_hbm, probs_hbm, act_hbm, cot_hbm, *refs):
    far, near = factors(experts)
    sends, place_ref = refs[:far], refs[far]
    ids_ref, probs_ref, act, cot, sems = refs[far + 1 :]
    tokens, width = act.shape
    steps = width // chunk
    small = (
        pltpu.make_async_copy(ids_hbm, ids_ref, sems.at[2 * steps]),
        pltpu.make_async_copy(probs_hbm, probs_ref, sems.at[2 * steps + 1]),
    )
    large = []
    for step in range(steps):
        at = pl.ds(step * chunk, chunk)
        large.append(
            (
                pltpu.make_async_copy(act_hbm.at[:, at], act.at[:, at], sems.at[2 * step]),
                pltpu.make_async_copy(cot_hbm.at[:, at], cot.at[:, at], sems.at[2 * step + 1]),
            )
        )
    for one in small:
        one.start()
    for pair in large:
        for one in pair:
            one.start()
    for one in small:
        one.wait()

    me = lax.axis_index("expert")
    ids = ids_ref[...]
    inside = ids < experts
    units = lax.broadcasted_iota(jnp.int32, (experts, tokens), 0)
    onehot = jnp.where(units == ids, 1.0, 0.0)
    earlier = lax.broadcasted_iota(jnp.int32, (tokens, tokens), 0) < lax.broadcasted_iota(
        jnp.int32, (tokens, tokens), 1
    )
    before = dot_nn(onehot.astype(jnp.bfloat16), jnp.where(earlier, 1.0, 0.0).astype(jnp.bfloat16))
    rank = jnp.sum(before * onehot, axis=0, keepdims=True).astype(jnp.int32)
    slots = lax.broadcasted_iota(jnp.int32, (experts * CAP, tokens), 0)
    slot = jnp.where(inside, ids * CAP + rank, -1)
    place_ref[...] = jnp.where(slots == slot, 1.0, 0.0).astype(jnp.bfloat16)
    turned = jnp.where(inside, (ids ^ me) * CAP + rank, -1)
    pick = jnp.where(slots == turned, 1.0, 0.0)
    weight = jnp.sum(pick * probs_ref[...], axis=1, keepdims=True)
    pick = pick.astype(jnp.bfloat16)
    for step in range(steps):
        at = slice(step * chunk, (step + 1) * chunk)
        for one in large[step]:
            one.wait()
        rows_tok = dot_nn(pick, act[:, at]).astype(jnp.bfloat16)
        rows_cot = (weight * dot_nn(pick, cot[:, at])).astype(jnp.bfloat16)
        for unit in range(experts):
            rows = slice(unit * CAP, (unit + 1) * CAP)
            sends[unit // near][unit % near, :CAP, at] = rows_tok[rows]
            sends[unit // near][unit % near, CAP:, at] = rows_cot[rows]


def route(ids, probs, act, cot, experts):
    tokens, width = act.shape
    chunk = min(1024, width)
    far, near = factors(experts)
    out = pl.pallas_call(
        functools.partial(route_kernel, experts, chunk),
        in_specs=[HBM] * 4,
        out_specs=[VMEM] * (far + 1),
        out_shape=[bf16(near, 2 * CAP, width)] * far + [bf16(experts * CAP, tokens)],
        scratch_shapes=[
            pltpu.VMEM((1, tokens), jnp.int32),
            pltpu.VMEM((1, tokens), jnp.float32),
            pltpu.VMEM((tokens, width), jnp.bfloat16),
            pltpu.VMEM((tokens, width), jnp.bfloat16),
            pltpu.SemaphoreType.DMA((2 * (width // chunk) + 2,)),
        ],
        compiler_params=params(16),
        cost_estimate=cost(4 * experts * CAP * tokens * width, 4 * tokens * width),
        name="route_rows",
    )(in_hbm(ids), in_hbm(probs), in_hbm(act), in_hbm(cot))
    return out[:far], out[far]


def merge_kernel(far, *refs):
    pieces, outs = refs[:far], refs[len(refs) - refs[0].shape[0] :]
    for index, out in enumerate(outs):
        rows = [piece[index, :CAP, :] for piece in pieces]
        rows += [piece[index, CAP:, :] for piece in pieces]
        out[...] = jnp.concatenate(rows, axis=0)


def merge(pieces, after=()):
    far = len(pieces)
    near, _, width = pieces[0].shape
    return pl.pallas_call(
        functools.partial(merge_kernel, far),
        in_specs=[VMEM] * far + [pl.BlockSpec(memory_space=pl.ANY)] * len(after),
        out_specs=[VMEM] * near,
        out_shape=[bf16(2 * CAP * far, width)] * near,
        compiler_params=params(16),
        cost_estimate=cost(0, 8 * near * CAP * far * width),
        name="merge_rows",
    )(*pieces, *after)


def load_kernel(chunk, pair_hbm, down_hbm, after, pair, down, sems):
    del after
    width = down.shape[1]
    copies = []
    for step in range(width // chunk):
        at = pl.ds(step * chunk, chunk)
        copies += [
            pltpu.make_async_copy(pair_hbm.at[:, at, :], pair.at[:, at, :], sems.at[0, step]),
            pltpu.make_async_copy(down_hbm.at[:, at], down.at[:, at], sems.at[1, step]),
        ]
    for one in copies:
        one.start()
    for one in copies:
        one.wait()


def load(pair, down, after):
    units, width = down.shape
    chunk = min(1024, width)
    return pl.pallas_call(
        functools.partial(load_kernel, chunk),
        in_specs=[HBM] * 2 + [pl.BlockSpec(memory_space=pl.ANY)],
        out_specs=[VMEM] * 2,
        out_shape=[pltpu.VMEM(pair.shape, jnp.bfloat16), pltpu.VMEM(down.shape, jnp.bfloat16)],
        scratch_shapes=[pltpu.SemaphoreType.DMA((2, width // chunk))],
        compiler_params=params(28),
        cost_estimate=cost(0, 6 * width * units),
        name="load_weights",
    )(in_hbm(pair), in_hbm(down), after)


def expert_kernel(homes, experts, groups, chunk, count, *refs):
    got, pair, down = refs[:count], refs[count], refs[count + 1]
    gate_out, up_out, hidden_out, tok_all, cot_all, parts_hbm = refs[count + 2 : count + 8]
    parts, acc_gate, acc_up, acc_hid, sems = refs[count + 8 :]
    half = got[0].shape[0] // 2
    width = got[0].shape[1]
    steps = width // chunk
    for step in range(steps):
        at = slice(step * chunk, (step + 1) * chunk)
        tok = jnp.concatenate([piece[:half, at] for piece in got], axis=0)
        cot = jnp.concatenate([piece[half:, at] for piece in got], axis=0)
        tok_all[:, at] = tok
        cot_all[:, at] = cot
        gate = dot_nn(tok, pair[0, at, :])
        up = dot_nn(tok, pair[1, at, :])
        hid = dot_nt(cot, down[:, at])
        if step == 0:
            acc_gate[...], acc_up[...], acc_hid[...] = gate, up, hid
        else:
            acc_gate[...] += gate
            acc_up[...] += up
            acc_hid[...] += hid
    pre_gate, pre_up, hidden_grad = acc_gate[...], acc_up[...], acc_hid[...]
    sigmoid_gate = jax.nn.sigmoid(pre_gate)
    activated = pre_gate * sigmoid_gate
    hidden_out[...] = (activated * pre_up).astype(jnp.bfloat16)
    gate_grad = (
        hidden_grad * pre_up * sigmoid_gate * (1.0 + pre_gate * (1.0 - sigmoid_gate))
    ).astype(jnp.bfloat16)
    up_grad = (hidden_grad * activated).astype(jnp.bfloat16)
    gate_out[...] = gate_grad
    up_out[...] = up_grad
    me, group = lax.axis_index("expert"), lax.axis_index("dp")
    rows = [
        lax.rem(group - back + groups, groups) * experts + (me ^ turn) for back, turn in homes
    ]
    copies = []
    for step in range(steps):
        at = slice(step * chunk, (step + 1) * chunk)
        value = dot_nt(gate_grad, pair[0, at, :]) + dot_nt(up_grad, pair[1, at, :])
        value = value.astype(jnp.bfloat16)
        for block, row in enumerate(rows):
            parts[row, :, at] = value[block * CAP : (block + 1) * CAP]
        where = pl.ds(step * chunk, chunk)
        one = pltpu.make_async_copy(
            parts.at[:, :, where], parts_hbm.at[:, :, where], sems.at[step]
        )
        one.start()
        copies.append(one)
    for one in copies:
        one.wait()


def expert_rows(got, homes, pair, down, experts, groups):
    width = got[0].shape[1]
    units = down.shape[0]
    chunk = min(1024, width)
    blocks = groups * experts
    total = blocks * CAP
    return pl.pallas_call(
        functools.partial(expert_kernel, homes, experts, groups, chunk, len(got)),
        in_specs=[VMEM] * (len(got) + 2),
        out_specs=[VMEM] * 5 + [HBM],
        out_shape=[bf16(total, units)] * 3
        + [bf16(total, width)] * 2
        + [pltpu.HBM((blocks, CAP, width), jnp.bfloat16)],
        scratch_shapes=[
            pltpu.VMEM((blocks, CAP, width), jnp.bfloat16),
            pltpu.VMEM((total, units), jnp.float32),
            pltpu.VMEM((total, units), jnp.float32),
            pltpu.VMEM((total, units), jnp.float32),
            pltpu.SemaphoreType.DMA((width // chunk,)),
        ],
        compiler_params=params(28),
        cost_estimate=cost(10 * total * width * units, 6 * width * units),
        name="expert_rows",
    )(
        *got,
        pltpu.with_memory_space_constraint(pair, pltpu.VMEM),
        pltpu.with_memory_space_constraint(down, pltpu.VMEM),
    )


def pair_grad_kernel(blocks, chunk, *refs):
    toks, gate_ref, up_ref = refs[:blocks], refs[blocks], refs[blocks + 1]
    out_hbm, buffer, sems = refs[blocks + 2 :]
    width = toks[0].shape[1]
    copies = []
    for step in range(width // chunk):
        at = slice(step * chunk, (step + 1) * chunk)
        tok = jnp.concatenate([ref[:, at] for ref in toks], axis=0)
        for side, ref in enumerate((gate_ref, up_ref)):
            buffer[side, at, :] = dot_tn(tok, ref[...]).astype(jnp.bfloat16)
        where = pl.ds(step * chunk, chunk)
        one = pltpu.make_async_copy(
            buffer.at[:, where, :], out_hbm.at[0, :, where, :], sems.at[step]
        )
        one.start()
        copies.append(one)
    for one in copies:
        one.wait()


def pair_grad(toks, gate_grad, up_grad):
    blocks = len(toks)
    width = toks[0].shape[1]
    total, units = gate_grad.shape
    chunk = min(512, width)
    return pl.pallas_call(
        functools.partial(pair_grad_kernel, blocks, chunk),
        in_specs=[VMEM] * (blocks + 2),
        out_specs=HBM,
        out_shape=bf16(1, 2, width, units),
        scratch_shapes=[
            pltpu.VMEM((2, width, units), jnp.bfloat16),
            pltpu.SemaphoreType.DMA((width // chunk,)),
        ],
        compiler_params=params(32),
        cost_estimate=cost(4 * total * width * units, 4 * width * units),
        name="pair_grad",
    )(*toks, gate_grad, up_grad)


def down_grad_kernel(blocks, chunk, *refs):
    cots, hidden_ref, out_hbm = refs[:blocks], refs[blocks], refs[blocks + 1]
    buffer, sems = refs[blocks + 2 :]
    width = cots[0].shape[1]
    copies = []
    for step in range(width // chunk):
        at = slice(step * chunk, (step + 1) * chunk)
        cot = jnp.concatenate([ref[:, at] for ref in cots], axis=0)
        buffer[:, at] = dot_tn(hidden_ref[...], cot).astype(jnp.bfloat16)
        where = pl.ds(step * chunk, chunk)
        one = pltpu.make_async_copy(buffer.at[:, where], out_hbm.at[0, :, where], sems.at[step])
        one.start()
        copies.append(one)
    for one in copies:
        one.wait()


def down_grad(cots, hidden):
    blocks = len(cots)
    width = cots[0].shape[1]
    total, units = hidden.shape
    chunk = min(1024, width)
    return pl.pallas_call(
        functools.partial(down_grad_kernel, blocks, chunk),
        in_specs=[VMEM] * (blocks + 1),
        out_specs=HBM,
        out_shape=bf16(1, units, width),
        scratch_shapes=[
            pltpu.VMEM((units, width), jnp.bfloat16),
            pltpu.SemaphoreType.DMA((width // chunk,)),
        ],
        compiler_params=params(24),
        cost_estimate=cost(2 * total * width * units, 2 * width * units),
        name="down_grad",
    )(*cots, hidden)


def spread_kernel(chunk, rows_ref, place_ref, out_hbm, buffer, sems):
    blocks, _, width = rows_ref.shape
    place = jnp.concatenate([place_ref[...]] * (blocks * CAP // place_ref.shape[0]), axis=0)
    copies = []
    for step in range(width // chunk):
        at = slice(step * chunk, (step + 1) * chunk)
        rows = jnp.concatenate([rows_ref[block, :, at] for block in range(blocks)], axis=0)
        buffer[:, at] = dot_tn(place, rows).astype(jnp.bfloat16)
        where = pl.ds(step * chunk, chunk)
        one = pltpu.make_async_copy(buffer.at[:, where], out_hbm.at[:, where], sems.at[step])
        one.start()
        copies.append(one)
    for one in copies:
        one.wait()


def spread(rows, place):
    width = rows.shape[2]
    slots, tokens = place.shape
    chunk = min(1024, width)
    return pl.pallas_call(
        functools.partial(spread_kernel, chunk),
        in_specs=[VMEM] * 2,
        out_specs=HBM,
        out_shape=bf16(tokens, width),
        scratch_shapes=[
            pltpu.VMEM((tokens, width), jnp.bfloat16),
            pltpu.SemaphoreType.DMA((width // chunk,)),
        ],
        compiler_params=params(16),
        cost_estimate=cost(2 * slots * tokens * width, 2 * tokens * width),
        name="spread_rows",
    )(rows, place)


def per_device(activations, cotangent, expert_ids, gate_probs, gate_up, down_proj):
    experts = lax.axis_size("expert")
    groups = lax.axis_size("dp")
    tokens = activations.shape[0]
    far, near = factors(experts)

    def send(value, by_group, by_expert):
        if by_group == 0 and by_expert == 0:
            return value
        pairs = []
        for group in range(groups):
            to = (group + by_group) % groups
            for i in range(experts):
                pairs.append((group * experts + i, to * experts + (i ^ by_expert)))
        return lax.ppermute(value, ("dp", "expert"), pairs)

    pieces, place = route(
        expert_ids.reshape(1, tokens),
        gate_probs.reshape(1, tokens),
        activations,
        cotangent,
        experts,
    )
    pair, down = load(gate_up[0], down_proj[0], place)
    arrived = [send(pieces[high], 0, high * near) for high in range(far)]
    early, late = range(far // 2), range(far // 2, far)
    first = [send(pieces[high], group, high * near) for group in range(1, groups) for high in early]
    second = [send(arrived[high], group, 0) for group in range(1, groups) for high in late]
    loaded = pltpu.with_memory_space_constraint(down, pltpu.VMEM)
    first = merge([arrived[high] for high in early] + first, (loaded,))
    second = merge([arrived[high] for high in late] + second, (first[0],))
    got = [send(rows[low], 0, low) for rows in (first, second) for low in range(near)]
    homes = [
        (group, high * near + low)
        for part in (early, late)
        for low in range(near)
        for group in range(groups)
        for high in part
    ]
    gate_grad, up_grad, hidden, tok, cot, parts = expert_rows(
        got, homes, pair, down, experts, groups
    )
    returned = lax.all_to_all(parts, ("dp", "expert"), split_axis=0, concat_axis=0, tiled=True)
    down_total = down_grad([cot], hidden)
    pair_total = pair_grad([tok], gate_grad, up_grad)
    input_grad = spread(returned, place)
    return input_grad, pair_total, down_total


def solution(mesh):
    rows = P(("dp", "expert"), None)
    pair, down = P("expert", None, None, "dp"), P("expert", "dp", None)
    return jax.shard_map(
        per_device,
        mesh=mesh,
        in_specs=(rows, rows, rows, rows, pair, down),
        out_specs=(rows, pair, down),
        check_vma=False,
    )
```

```python
import functools

import jax
import jax.numpy as jnp
from jax import lax
from jax.experimental import pallas as pl
from jax.experimental.pallas import tpu as pltpu
from jax.sharding import PartitionSpec as P

CAP = 2
MIB = 1024 * 1024
VMEM = pl.BlockSpec(memory_space=pltpu.VMEM)
HBM = pl.BlockSpec(memory_space=pltpu.HBM)


def dot_nn(a, b):
    return lax.dot_general(a, b, (((1,), (0,)), ((), ())), preferred_element_type=jnp.float32)


def dot_nt(a, b):
    return lax.dot_general(a, b, (((1,), (1,)), ((), ())), preferred_element_type=jnp.float32)


def dot_tn(a, b):
    return lax.dot_general(a, b, (((0,), (0,)), ((), ())), preferred_element_type=jnp.float32)


def cost(flops, moved):
    return pl.CostEstimate(flops=int(flops), bytes_accessed=int(moved), transcendentals=0)


def params(mib):
    return pltpu.CompilerParams(vmem_limit_bytes=mib * MIB)


def in_hbm(value):
    return pltpu.with_memory_space_constraint(value, pltpu.HBM)


def bf16(*shape):
    return jax.ShapeDtypeStruct(shape, jnp.bfloat16)


def factors(experts):
    far = 1
    while 4 * far * far <= experts:
        far *= 2
    return far, experts // far


def route_kernel(experts, chunk, ids_hbm, probs_hbm, act_hbm, cot_hbm, *refs):
    far, near = factors(experts)
    sends, place_ref = refs[:far], refs[far]
    ids_ref, probs_ref, act, cot, sems = refs[far + 1 :]
    tokens, width = act.shape
    steps = width // chunk
    small = (
        pltpu.make_async_copy(ids_hbm, ids_ref, sems.at[2 * steps]),
        pltpu.make_async_copy(probs_hbm, probs_ref, sems.at[2 * steps + 1]),
    )
    large = []
    for step in range(steps):
        at = pl.ds(step * chunk, chunk)
        large.append(
            (
                pltpu.make_async_copy(act_hbm.at[:, at], act.at[:, at], sems.at[2 * step]),
                pltpu.make_async_copy(cot_hbm.at[:, at], cot.at[:, at], sems.at[2 * step + 1]),
            )
        )
    for one in small:
        one.start()
    for pair in large:
        for one in pair:
            one.start()
    for one in small:
        one.wait()

    me = lax.axis_index("expert")
    ids = ids_ref[...]
    inside = ids < experts
    units = lax.broadcasted_iota(jnp.int32, (experts, tokens), 0)
    onehot = jnp.where(units == ids, 1.0, 0.0)
    earlier = lax.broadcasted_iota(jnp.int32, (tokens, tokens), 0) < lax.broadcasted_iota(
        jnp.int32, (tokens, tokens), 1
    )
    before = dot_nn(onehot.astype(jnp.bfloat16), jnp.where(earlier, 1.0, 0.0).astype(jnp.bfloat16))
    rank = jnp.sum(before * onehot, axis=0, keepdims=True).astype(jnp.int32)
    slots = lax.broadcasted_iota(jnp.int32, (experts * CAP, tokens), 0)
    slot = jnp.where(inside, ids * CAP + rank, -1)
    place_ref[...] = jnp.where(slots == slot, 1.0, 0.0).astype(jnp.bfloat16)
    turned = jnp.where(inside, (ids ^ me) * CAP + rank, -1)
    pick = jnp.where(slots == turned, 1.0, 0.0)
    weight = jnp.sum(pick * probs_ref[...], axis=1, keepdims=True)
    pick = pick.astype(jnp.bfloat16)
    for step in range(steps):
        at = slice(step * chunk, (step + 1) * chunk)
        for one in large[step]:
            one.wait()
        rows_tok = dot_nn(pick, act[:, at]).astype(jnp.bfloat16)
        rows_cot = (weight * dot_nn(pick, cot[:, at])).astype(jnp.bfloat16)
        for unit in range(experts):
            rows = slice(unit * CAP, (unit + 1) * CAP)
            sends[unit // near][unit % near, :CAP, at] = rows_tok[rows]
            sends[unit // near][unit % near, CAP:, at] = rows_cot[rows]


def route(ids, probs, act, cot, experts):
    tokens, width = act.shape
    chunk = min(1024, width)
    far, near = factors(experts)
    out = pl.pallas_call(
        functools.partial(route_kernel, experts, chunk),
        in_specs=[HBM] * 4,
        out_specs=[VMEM] * (far + 1),
        out_shape=[bf16(near, 2 * CAP, width)] * far + [bf16(experts * CAP, tokens)],
        scratch_shapes=[
            pltpu.VMEM((1, tokens), jnp.int32),
            pltpu.VMEM((1, tokens), jnp.float32),
            pltpu.VMEM((tokens, width), jnp.bfloat16),
            pltpu.VMEM((tokens, width), jnp.bfloat16),
            pltpu.SemaphoreType.DMA((2 * (width // chunk) + 2,)),
        ],
        compiler_params=params(16),
        cost_estimate=cost(4 * experts * CAP * tokens * width, 4 * tokens * width),
        name="route_rows",
    )(in_hbm(ids), in_hbm(probs), in_hbm(act), in_hbm(cot))
    return out[:far], out[far]


def merge_kernel(far, *refs):
    pieces, outs = refs[:far], refs[len(refs) - refs[0].shape[0] :]
    for index, out in enumerate(outs):
        rows = [piece[index, :CAP, :] for piece in pieces]
        rows += [piece[index, CAP:, :] for piece in pieces]
        out[...] = jnp.concatenate(rows, axis=0)


def merge(pieces, after=()):
    far = len(pieces)
    near, _, width = pieces[0].shape
    return pl.pallas_call(
        functools.partial(merge_kernel, far),
        in_specs=[VMEM] * far + [pl.BlockSpec(memory_space=pl.ANY)] * len(after),
        out_specs=[VMEM] * near,
        out_shape=[bf16(2 * CAP * far, width)] * near,
        compiler_params=params(16),
        cost_estimate=cost(0, 8 * near * CAP * far * width),
        name="merge_rows",
    )(*pieces, *after)


def stack_kernel(number, *refs):
    pieces, out = refs[:number], refs[-1]
    rows = pieces[0].shape[0] // 2
    for side in range(2):
        picked = [piece[side * rows : (side + 1) * rows, :] for piece in pieces]
        out[side * number * rows : (side + 1) * number * rows, :] = jnp.concatenate(picked, axis=0)


def stack(pieces, after=()):
    number = len(pieces)
    rows, width = pieces[0].shape
    return pl.pallas_call(
        functools.partial(stack_kernel, number),
        in_specs=[VMEM] * number + [pl.BlockSpec(memory_space=pl.ANY)] * len(after),
        out_specs=VMEM,
        out_shape=bf16(number * rows, width),
        compiler_params=params(16),
        cost_estimate=cost(0, 4 * number * rows * width),
        name="stack_rows",
    )(*pieces, *after)


def load_kernel(chunk, pair_hbm, down_hbm, after, pair, down, sems):
    del after
    width = down.shape[1]
    copies = []
    for step in range(width // chunk):
        at = pl.ds(step * chunk, chunk)
        copies += [
            pltpu.make_async_copy(pair_hbm.at[:, at, :], pair.at[:, at, :], sems.at[0, step]),
            pltpu.make_async_copy(down_hbm.at[:, at], down.at[:, at], sems.at[1, step]),
        ]
    for one in copies:
        one.start()
    for one in copies:
        one.wait()


def load(pair, down, after):
    units, width = down.shape
    chunk = min(1024, width)
    return pl.pallas_call(
        functools.partial(load_kernel, chunk),
        in_specs=[HBM] * 2 + [pl.BlockSpec(memory_space=pl.ANY)],
        out_specs=[VMEM] * 2,
        out_shape=[pltpu.VMEM(pair.shape, jnp.bfloat16), pltpu.VMEM(down.shape, jnp.bfloat16)],
        scratch_shapes=[pltpu.SemaphoreType.DMA((2, width // chunk))],
        compiler_params=params(28),
        cost_estimate=cost(0, 6 * width * units),
        name="load_weights",
    )(in_hbm(pair), in_hbm(down), after)


def expert_kernel(homes, experts, groups, chunk, count, *refs):
    got, pair, down = refs[:count], refs[count], refs[count + 1]
    gate_out, up_out, hidden_out, tok_all, cot_all, parts_hbm = refs[count + 2 : count + 8]
    parts, acc_gate, acc_up, acc_hid, sems = refs[count + 8 :]
    width = got[0].shape[1]
    steps = width // chunk
    for step in range(steps):
        at = slice(step * chunk, (step + 1) * chunk)
        tok = jnp.concatenate([piece[: piece.shape[0] // 2, at] for piece in got], axis=0)
        cot = jnp.concatenate([piece[piece.shape[0] // 2 :, at] for piece in got], axis=0)
        tok_all[:, at] = tok
        cot_all[:, at] = cot
        gate = dot_nn(tok, pair[0, at, :])
        up = dot_nn(tok, pair[1, at, :])
        hid = dot_nt(cot, down[:, at])
        if step == 0:
            acc_gate[...], acc_up[...], acc_hid[...] = gate, up, hid
        else:
            acc_gate[...] += gate
            acc_up[...] += up
            acc_hid[...] += hid
    pre_gate, pre_up, hidden_grad = acc_gate[...], acc_up[...], acc_hid[...]
    sigmoid_gate = jax.nn.sigmoid(pre_gate)
    activated = pre_gate * sigmoid_gate
    hidden_out[...] = (activated * pre_up).astype(jnp.bfloat16)
    gate_grad = (
        hidden_grad * pre_up * sigmoid_gate * (1.0 + pre_gate * (1.0 - sigmoid_gate))
    ).astype(jnp.bfloat16)
    up_grad = (hidden_grad * activated).astype(jnp.bfloat16)
    gate_out[...] = gate_grad
    up_out[...] = up_grad
    me, group = lax.axis_index("expert"), lax.axis_index("dp")
    rows = [
        lax.rem(group - back + groups, groups) * experts + (me ^ turn) for back, turn in homes
    ]
    copies = []
    for step in range(steps):
        at = slice(step * chunk, (step + 1) * chunk)
        value = dot_nt(gate_grad, pair[0, at, :]) + dot_nt(up_grad, pair[1, at, :])
        value = value.astype(jnp.bfloat16)
        for block, row in enumerate(rows):
            parts[row, :, at] = value[block * CAP : (block + 1) * CAP]
        where = pl.ds(step * chunk, chunk)
        one = pltpu.make_async_copy(
            parts.at[:, :, where], parts_hbm.at[:, :, where], sems.at[step]
        )
        one.start()
        copies.append(one)
    for one in copies:
        one.wait()


def expert_rows(got, homes, pair, down, experts, groups):
    width = got[0].shape[1]
    units = down.shape[0]
    chunk = min(1024, width)
    blocks = groups * experts
    total = blocks * CAP
    return pl.pallas_call(
        functools.partial(expert_kernel, homes, experts, groups, chunk, len(got)),
        in_specs=[VMEM] * (len(got) + 2),
        out_specs=[VMEM] * 5 + [HBM],
        out_shape=[bf16(total, units)] * 3
        + [bf16(total, width)] * 2
        + [pltpu.HBM((blocks, CAP, width), jnp.bfloat16)],
        scratch_shapes=[
            pltpu.VMEM((blocks, CAP, width), jnp.bfloat16),
            pltpu.VMEM((total, units), jnp.float32),
            pltpu.VMEM((total, units), jnp.float32),
            pltpu.VMEM((total, units), jnp.float32),
            pltpu.SemaphoreType.DMA((width // chunk,)),
        ],
        compiler_params=params(28),
        cost_estimate=cost(10 * total * width * units, 6 * width * units),
        name="expert_rows",
    )(
        *got,
        pltpu.with_memory_space_constraint(pair, pltpu.VMEM),
        pltpu.with_memory_space_constraint(down, pltpu.VMEM),
    )


def pair_grad_kernel(blocks, chunk, *refs):
    toks, gate_ref, up_ref = refs[:blocks], refs[blocks], refs[blocks + 1]
    out_hbm, buffer, sems = refs[blocks + 2 :]
    width = toks[0].shape[1]
    copies = []
    for step in range(width // chunk):
        at = slice(step * chunk, (step + 1) * chunk)
        tok = jnp.concatenate([ref[:, at] for ref in toks], axis=0)
        for side, ref in enumerate((gate_ref, up_ref)):
            buffer[side, at, :] = dot_tn(tok, ref[...]).astype(jnp.bfloat16)
        where = pl.ds(step * chunk, chunk)
        one = pltpu.make_async_copy(
            buffer.at[:, where, :], out_hbm.at[0, :, where, :], sems.at[step]
        )
        one.start()
        copies.append(one)
    for one in copies:
        one.wait()


def pair_grad(toks, gate_grad, up_grad):
    blocks = len(toks)
    width = toks[0].shape[1]
    total, units = gate_grad.shape
    chunk = min(512, width)
    return pl.pallas_call(
        functools.partial(pair_grad_kernel, blocks, chunk),
        in_specs=[VMEM] * (blocks + 2),
        out_specs=HBM,
        out_shape=bf16(1, 2, width, units),
        scratch_shapes=[
            pltpu.VMEM((2, width, units), jnp.bfloat16),
            pltpu.SemaphoreType.DMA((width // chunk,)),
        ],
        compiler_params=params(32),
        cost_estimate=cost(4 * total * width * units, 4 * width * units),
        name="pair_grad",
    )(*toks, gate_grad, up_grad)


def down_grad_kernel(blocks, chunk, *refs):
    cots, hidden_ref, out_hbm = refs[:blocks], refs[blocks], refs[blocks + 1]
    buffer, sems = refs[blocks + 2 :]
    width = cots[0].shape[1]
    copies = []
    for step in range(width // chunk):
        at = slice(step * chunk, (step + 1) * chunk)
        cot = jnp.concatenate([ref[:, at] for ref in cots], axis=0)
        buffer[:, at] = dot_tn(hidden_ref[...], cot).astype(jnp.bfloat16)
        where = pl.ds(step * chunk, chunk)
        one = pltpu.make_async_copy(buffer.at[:, where], out_hbm.at[0, :, where], sems.at[step])
        one.start()
        copies.append(one)
    for one in copies:
        one.wait()


def down_grad(cots, hidden):
    blocks = len(cots)
    width = cots[0].shape[1]
    total, units = hidden.shape
    chunk = min(1024, width)
    return pl.pallas_call(
        functools.partial(down_grad_kernel, blocks, chunk),
        in_specs=[VMEM] * (blocks + 1),
        out_specs=HBM,
        out_shape=bf16(1, units, width),
        scratch_shapes=[
            pltpu.VMEM((units, width), jnp.bfloat16),
            pltpu.SemaphoreType.DMA((width // chunk,)),
        ],
        compiler_params=params(24),
        cost_estimate=cost(2 * total * width * units, 2 * width * units),
        name="down_grad",
    )(*cots, hidden)


def spread_kernel(chunk, rows_ref, place_ref, out_hbm, buffer, sems):
    blocks, _, width = rows_ref.shape
    place = jnp.concatenate([place_ref[...]] * (blocks * CAP // place_ref.shape[0]), axis=0)
    copies = []
    for step in range(width // chunk):
        at = slice(step * chunk, (step + 1) * chunk)
        rows = jnp.concatenate([rows_ref[block, :, at] for block in range(blocks)], axis=0)
        buffer[:, at] = dot_tn(place, rows).astype(jnp.bfloat16)
        where = pl.ds(step * chunk, chunk)
        one = pltpu.make_async_copy(buffer.at[:, where], out_hbm.at[:, where], sems.at[step])
        one.start()
        copies.append(one)
    for one in copies:
        one.wait()


def spread(rows, place):
    width = rows.shape[2]
    slots, tokens = place.shape
    chunk = min(1024, width)
    return pl.pallas_call(
        functools.partial(spread_kernel, chunk),
        in_specs=[VMEM] * 2,
        out_specs=HBM,
        out_shape=bf16(tokens, width),
        scratch_shapes=[
            pltpu.VMEM((tokens, width), jnp.bfloat16),
            pltpu.SemaphoreType.DMA((width // chunk,)),
        ],
        compiler_params=params(16),
        cost_estimate=cost(2 * slots * tokens * width, 2 * tokens * width),
        name="spread_rows",
    )(rows, place)


def per_device(activations, cotangent, expert_ids, gate_probs, gate_up, down_proj):
    experts = lax.axis_size("expert")
    groups = lax.axis_size("dp")
    tokens = activations.shape[0]
    far, near = factors(experts)

    def send(value, by_group, by_expert):
        if by_group == 0 and by_expert == 0:
            return value
        pairs = []
        for group in range(groups):
            to = (group + by_group) % groups
            for i in range(experts):
                pairs.append((group * experts + i, to * experts + (i ^ by_expert)))
        return lax.ppermute(value, ("dp", "expert"), pairs)

    pieces, place = route(
        expert_ids.reshape(1, tokens),
        gate_probs.reshape(1, tokens),
        activations,
        cotangent,
        experts,
    )
    pair, down = load(gate_up[0], down_proj[0], place)
    arrived = [send(pieces[high], 0, high * near) for high in range(far)]
    early, late = range(far // 2), range(far // 2, far)
    first = [send(pieces[high], group, high * near) for group in range(1, groups) for high in early]
    first = merge([arrived[high] for high in early] + first)
    loaded = pltpu.with_memory_space_constraint(down, pltpu.VMEM)
    second = merge([arrived[high] for high in late], (loaded,))
    second = stack([send(second[low], 0, low) for low in range(near)], (first[0],))
    got = [send(first[low], 0, low) for low in range(near)]
    got += [send(second, group, 0) for group in range(groups)]
    homes = [
        (group, high * near + low)
        for low in range(near)
        for group in range(groups)
        for high in early
    ]
    homes += [
        (group, high * near + low)
        for group in range(groups)
        for low in range(near)
        for high in late
    ]
    gate_grad, up_grad, hidden, tok, cot, parts = expert_rows(
        got, homes, pair, down, experts, groups
    )
    returned = lax.all_to_all(parts, ("dp", "expert"), split_axis=0, concat_axis=0, tiled=True)
    down_total = down_grad([cot], hidden)
    pair_total = pair_grad([tok], gate_grad, up_grad)
    input_grad = spread(returned, place)
    return input_grad, pair_total, down_total


def solution(mesh):
    rows = P(("dp", "expert"), None)
    pair, down = P("expert", None, None, "dp"), P("expert", "dp", None)
    return jax.shard_map(
        per_device,
        mesh=mesh,
        in_specs=(rows, rows, rows, rows, pair, down),
        out_specs=(rows, pair, down),
        check_vma=False,
    )
```

```python
import functools

import jax
import jax.numpy as jnp
from jax import lax
from jax.experimental import pallas as pl
from jax.experimental.pallas import tpu as pltpu
from jax.sharding import PartitionSpec as P

CAP = 2
MIB = 1024 * 1024
VMEM = pl.BlockSpec(memory_space=pltpu.VMEM)
HBM = pl.BlockSpec(memory_space=pltpu.HBM)


def dot_nn(a, b):
    return lax.dot_general(a, b, (((1,), (0,)), ((), ())), preferred_element_type=jnp.float32)


def dot_nt(a, b):
    return lax.dot_general(a, b, (((1,), (1,)), ((), ())), preferred_element_type=jnp.float32)


def dot_tn(a, b):
    return lax.dot_general(a, b, (((0,), (0,)), ((), ())), preferred_element_type=jnp.float32)


def cost(flops, moved):
    return pl.CostEstimate(flops=int(flops), bytes_accessed=int(moved), transcendentals=0)


def params(mib):
    return pltpu.CompilerParams(vmem_limit_bytes=mib * MIB)


def in_hbm(value):
    return pltpu.with_memory_space_constraint(value, pltpu.HBM)


def bf16(*shape):
    return jax.ShapeDtypeStruct(shape, jnp.bfloat16)


def factors(experts):
    far = 1
    while 4 * far * far <= experts:
        far *= 2
    return far, experts // far


def route_kernel(experts, chunk, ids_hbm, probs_hbm, act_hbm, cot_hbm, *refs):
    far, near = factors(experts)
    sends, place_ref = refs[:far], refs[far]
    ids_ref, probs_ref, act, cot, sems = refs[far + 1 :]
    tokens, width = act.shape
    steps = width // chunk
    small = (
        pltpu.make_async_copy(ids_hbm, ids_ref, sems.at[2 * steps]),
        pltpu.make_async_copy(probs_hbm, probs_ref, sems.at[2 * steps + 1]),
    )
    large = []
    for step in range(steps):
        at = pl.ds(step * chunk, chunk)
        large.append(
            (
                pltpu.make_async_copy(act_hbm.at[:, at], act.at[:, at], sems.at[2 * step]),
                pltpu.make_async_copy(cot_hbm.at[:, at], cot.at[:, at], sems.at[2 * step + 1]),
            )
        )
    for one in small:
        one.start()
    for pair in large:
        for one in pair:
            one.start()
    for one in small:
        one.wait()

    me = lax.axis_index("expert")
    ids = ids_ref[...]
    inside = ids < experts
    units = lax.broadcasted_iota(jnp.int32, (experts, tokens), 0)
    onehot = jnp.where(units == ids, 1.0, 0.0)
    earlier = lax.broadcasted_iota(jnp.int32, (tokens, tokens), 0) < lax.broadcasted_iota(
        jnp.int32, (tokens, tokens), 1
    )
    before = dot_nn(onehot.astype(jnp.bfloat16), jnp.where(earlier, 1.0, 0.0).astype(jnp.bfloat16))
    rank = jnp.sum(before * onehot, axis=0, keepdims=True).astype(jnp.int32)
    slots = lax.broadcasted_iota(jnp.int32, (experts * CAP, tokens), 0)
    slot = jnp.where(inside, ids * CAP + rank, -1)
    place_ref[...] = jnp.where(slots == slot, 1.0, 0.0).astype(jnp.bfloat16)
    turned = jnp.where(inside, (ids ^ me) * CAP + rank, -1)
    pick = jnp.where(slots == turned, 1.0, 0.0)
    weight = jnp.sum(pick * probs_ref[...], axis=1, keepdims=True)
    pick = pick.astype(jnp.bfloat16)
    for step in range(steps):
        at = slice(step * chunk, (step + 1) * chunk)
        for one in large[step]:
            one.wait()
        rows_tok = dot_nn(pick, act[:, at]).astype(jnp.bfloat16)
        rows_cot = (weight * dot_nn(pick, cot[:, at])).astype(jnp.bfloat16)
        for unit in range(experts):
            rows = slice(unit * CAP, (unit + 1) * CAP)
            sends[unit // near][unit % near, :CAP, at] = rows_tok[rows]
            sends[unit // near][unit % near, CAP:, at] = rows_cot[rows]


def route(ids, probs, act, cot, experts):
    tokens, width = act.shape
    chunk = min(1024, width)
    far, near = factors(experts)
    out = pl.pallas_call(
        functools.partial(route_kernel, experts, chunk),
        in_specs=[HBM] * 4,
        out_specs=[VMEM] * (far + 1),
        out_shape=[bf16(near, 2 * CAP, width)] * far + [bf16(experts * CAP, tokens)],
        scratch_shapes=[
            pltpu.VMEM((1, tokens), jnp.int32),
            pltpu.VMEM((1, tokens), jnp.float32),
            pltpu.VMEM((tokens, width), jnp.bfloat16),
            pltpu.VMEM((tokens, width), jnp.bfloat16),
            pltpu.SemaphoreType.DMA((2 * (width // chunk) + 2,)),
        ],
        compiler_params=params(16),
        cost_estimate=cost(4 * experts * CAP * tokens * width, 4 * tokens * width),
        name="route_rows",
    )(in_hbm(ids), in_hbm(probs), in_hbm(act), in_hbm(cot))
    return out[:far], out[far]


def merge_kernel(far, *refs):
    pieces, outs = refs[:far], refs[len(refs) - refs[0].shape[0] :]
    for index, out in enumerate(outs):
        rows = [piece[index, :CAP, :] for piece in pieces]
        rows += [piece[index, CAP:, :] for piece in pieces]
        out[...] = jnp.concatenate(rows, axis=0)


def merge(pieces, after=()):
    far = len(pieces)
    near, _, width = pieces[0].shape
    return pl.pallas_call(
        functools.partial(merge_kernel, far),
        in_specs=[VMEM] * far + [pl.BlockSpec(memory_space=pl.ANY)] * len(after),
        out_specs=[VMEM] * near,
        out_shape=[bf16(2 * CAP * far, width)] * near,
        compiler_params=params(16),
        cost_estimate=cost(0, 8 * near * CAP * far * width),
        name="merge_rows",
    )(*pieces, *after)


def stack_kernel(number, *refs):
    pieces, out = refs[:number], refs[-1]
    rows = pieces[0].shape[0] // 2
    for side in range(2):
        picked = [piece[side * rows : (side + 1) * rows, :] for piece in pieces]
        out[side * number * rows : (side + 1) * number * rows, :] = jnp.concatenate(picked, axis=0)


def stack(pieces, after=()):
    number = len(pieces)
    rows, width = pieces[0].shape
    return pl.pallas_call(
        functools.partial(stack_kernel, number),
        in_specs=[VMEM] * number + [pl.BlockSpec(memory_space=pl.ANY)] * len(after),
        out_specs=VMEM,
        out_shape=bf16(number * rows, width),
        compiler_params=params(16),
        cost_estimate=cost(0, 4 * number * rows * width),
        name="stack_rows",
    )(*pieces, *after)


def load_kernel(chunk, pair_hbm, down_hbm, after, pair, down, sems):
    del after
    width = down.shape[1]
    copies = []
    for step in range(width // chunk):
        at = pl.ds(step * chunk, chunk)
        copies += [
            pltpu.make_async_copy(pair_hbm.at[:, at, :], pair.at[:, at, :], sems.at[0, step]),
            pltpu.make_async_copy(down_hbm.at[:, at], down.at[:, at], sems.at[1, step]),
        ]
    for one in copies:
        one.start()
    for one in copies:
        one.wait()


def load(pair, down, after):
    units, width = down.shape
    chunk = min(1024, width)
    return pl.pallas_call(
        functools.partial(load_kernel, chunk),
        in_specs=[HBM] * 2 + [pl.BlockSpec(memory_space=pl.ANY)],
        out_specs=[VMEM] * 2,
        out_shape=[pltpu.VMEM(pair.shape, jnp.bfloat16), pltpu.VMEM(down.shape, jnp.bfloat16)],
        scratch_shapes=[pltpu.SemaphoreType.DMA((2, width // chunk))],
        compiler_params=params(28),
        cost_estimate=cost(0, 6 * width * units),
        name="load_weights",
    )(in_hbm(pair), in_hbm(down), after)


def expert_kernel(homes, experts, groups, chunk, count, *refs):
    got, pair, down = refs[:count], refs[count], refs[count + 1]
    gate_out, up_out, hidden_out, tok_all, cot_all, parts_hbm = refs[count + 2 : count + 8]
    parts, acc_gate, acc_up, acc_hid, sems = refs[count + 8 :]
    width = got[0].shape[1]
    steps = width // chunk
    for step in range(steps):
        at = slice(step * chunk, (step + 1) * chunk)
        tok = jnp.concatenate([piece[: piece.shape[0] // 2, at] for piece in got], axis=0)
        cot = jnp.concatenate([piece[piece.shape[0] // 2 :, at] for piece in got], axis=0)
        tok_all[:, at] = tok
        cot_all[:, at] = cot
        gate = dot_nn(tok, pair[0, at, :])
        up = dot_nn(tok, pair[1, at, :])
        hid = dot_nt(cot, down[:, at])
        if step == 0:
            acc_gate[...], acc_up[...], acc_hid[...] = gate, up, hid
        else:
            acc_gate[...] += gate
            acc_up[...] += up
            acc_hid[...] += hid
    pre_gate, pre_up, hidden_grad = acc_gate[...], acc_up[...], acc_hid[...]
    sigmoid_gate = jax.nn.sigmoid(pre_gate)
    activated = pre_gate * sigmoid_gate
    hidden_out[...] = (activated * pre_up).astype(jnp.bfloat16)
    gate_grad = (
        hidden_grad * pre_up * sigmoid_gate * (1.0 + pre_gate * (1.0 - sigmoid_gate))
    ).astype(jnp.bfloat16)
    up_grad = (hidden_grad * activated).astype(jnp.bfloat16)
    gate_out[...] = gate_grad
    up_out[...] = up_grad
    me, group = lax.axis_index("expert"), lax.axis_index("dp")
    rows = [
        lax.rem(group - back + groups, groups) * experts + (me ^ turn) for back, turn in homes
    ]
    copies = []
    for step in range(steps):
        at = slice(step * chunk, (step + 1) * chunk)
        value = dot_nt(gate_grad, pair[0, at, :]) + dot_nt(up_grad, pair[1, at, :])
        value = value.astype(jnp.bfloat16)
        for block, row in enumerate(rows):
            parts[row, :, at] = value[block * CAP : (block + 1) * CAP]
        where = pl.ds(step * chunk, chunk)
        one = pltpu.make_async_copy(
            parts.at[:, :, where], parts_hbm.at[:, :, where], sems.at[step]
        )
        one.start()
        copies.append(one)
    for one in copies:
        one.wait()


def expert_rows(got, homes, pair, down, experts, groups):
    width = got[0].shape[1]
    units = down.shape[0]
    chunk = min(1024, width)
    blocks = groups * experts
    total = blocks * CAP
    return pl.pallas_call(
        functools.partial(expert_kernel, homes, experts, groups, chunk, len(got)),
        in_specs=[VMEM] * (len(got) + 2),
        out_specs=[VMEM] * 5 + [HBM],
        out_shape=[bf16(total, units)] * 3
        + [bf16(total, width)] * 2
        + [pltpu.HBM((blocks, CAP, width), jnp.bfloat16)],
        scratch_shapes=[
            pltpu.VMEM((blocks, CAP, width), jnp.bfloat16),
            pltpu.VMEM((total, units), jnp.float32),
            pltpu.VMEM((total, units), jnp.float32),
            pltpu.VMEM((total, units), jnp.float32),
            pltpu.SemaphoreType.DMA((width // chunk,)),
        ],
        compiler_params=params(28),
        cost_estimate=cost(10 * total * width * units, 6 * width * units),
        name="expert_rows",
    )(
        *got,
        pltpu.with_memory_space_constraint(pair, pltpu.VMEM),
        pltpu.with_memory_space_constraint(down, pltpu.VMEM),
    )


def pair_grad_kernel(blocks, chunk, *refs):
    toks, gate_ref, up_ref = refs[:blocks], refs[blocks], refs[blocks + 1]
    out_hbm, buffer, sems = refs[blocks + 2 :]
    width = toks[0].shape[1]
    copies = []
    for step in range(width // chunk):
        at = slice(step * chunk, (step + 1) * chunk)
        tok = jnp.concatenate([ref[:, at] for ref in toks], axis=0)
        for side, ref in enumerate((gate_ref, up_ref)):
            buffer[side, at, :] = dot_tn(tok, ref[...]).astype(jnp.bfloat16)
        where = pl.ds(step * chunk, chunk)
        one = pltpu.make_async_copy(
            buffer.at[:, where, :], out_hbm.at[0, :, where, :], sems.at[step]
        )
        one.start()
        copies.append(one)
    for one in copies:
        one.wait()


def pair_grad(toks, gate_grad, up_grad):
    blocks = len(toks)
    width = toks[0].shape[1]
    total, units = gate_grad.shape
    chunk = min(512, width)
    return pl.pallas_call(
        functools.partial(pair_grad_kernel, blocks, chunk),
        in_specs=[VMEM] * (blocks + 2),
        out_specs=HBM,
        out_shape=bf16(1, 2, width, units),
        scratch_shapes=[
            pltpu.VMEM((2, width, units), jnp.bfloat16),
            pltpu.SemaphoreType.DMA((width // chunk,)),
        ],
        compiler_params=params(32),
        cost_estimate=cost(4 * total * width * units, 4 * width * units),
        name="pair_grad",
    )(*toks, gate_grad, up_grad)


def down_grad_kernel(blocks, chunk, *refs):
    cots, hidden_ref, out_hbm = refs[:blocks], refs[blocks], refs[blocks + 1]
    buffer, sems = refs[blocks + 2 :]
    width = cots[0].shape[1]
    copies = []
    for step in range(width // chunk):
        at = slice(step * chunk, (step + 1) * chunk)
        cot = jnp.concatenate([ref[:, at] for ref in cots], axis=0)
        buffer[:, at] = dot_tn(hidden_ref[...], cot).astype(jnp.bfloat16)
        where = pl.ds(step * chunk, chunk)
        one = pltpu.make_async_copy(buffer.at[:, where], out_hbm.at[0, :, where], sems.at[step])
        one.start()
        copies.append(one)
    for one in copies:
        one.wait()


def down_grad(cots, hidden):
    blocks = len(cots)
    width = cots[0].shape[1]
    total, units = hidden.shape
    chunk = min(1024, width)
    return pl.pallas_call(
        functools.partial(down_grad_kernel, blocks, chunk),
        in_specs=[VMEM] * (blocks + 1),
        out_specs=HBM,
        out_shape=bf16(1, units, width),
        scratch_shapes=[
            pltpu.VMEM((units, width), jnp.bfloat16),
            pltpu.SemaphoreType.DMA((width // chunk,)),
        ],
        compiler_params=params(24),
        cost_estimate=cost(2 * total * width * units, 2 * width * units),
        name="down_grad",
    )(*cots, hidden)


def spread_kernel(chunk, rows_ref, place_ref, out_hbm, buffer, sems):
    blocks, _, width = rows_ref.shape
    place = jnp.concatenate([place_ref[...]] * (blocks * CAP // place_ref.shape[0]), axis=0)
    copies = []
    for step in range(width // chunk):
        at = slice(step * chunk, (step + 1) * chunk)
        rows = jnp.concatenate([rows_ref[block, :, at] for block in range(blocks)], axis=0)
        buffer[:, at] = dot_tn(place, rows).astype(jnp.bfloat16)
        where = pl.ds(step * chunk, chunk)
        one = pltpu.make_async_copy(buffer.at[:, where], out_hbm.at[:, where], sems.at[step])
        one.start()
        copies.append(one)
    for one in copies:
        one.wait()


def spread(rows, place):
    width = rows.shape[2]
    slots, tokens = place.shape
    chunk = min(1024, width)
    return pl.pallas_call(
        functools.partial(spread_kernel, chunk),
        in_specs=[VMEM] * 2,
        out_specs=HBM,
        out_shape=bf16(tokens, width),
        scratch_shapes=[
            pltpu.VMEM((tokens, width), jnp.bfloat16),
            pltpu.SemaphoreType.DMA((width // chunk,)),
        ],
        compiler_params=params(16),
        cost_estimate=cost(2 * slots * tokens * width, 2 * tokens * width),
        name="spread_rows",
    )(rows, place)


def per_device(activations, cotangent, expert_ids, gate_probs, gate_up, down_proj):
    experts = lax.axis_size("expert")
    groups = lax.axis_size("dp")
    tokens = activations.shape[0]
    far, near = factors(experts)

    def send(value, by_group, by_expert):
        if by_group == 0 and by_expert == 0:
            return value
        pairs = []
        for group in range(groups):
            to = (group + by_group) % groups
            for i in range(experts):
                pairs.append((group * experts + i, to * experts + (i ^ by_expert)))
        return lax.ppermute(value, ("dp", "expert"), pairs)

    pieces, place = route(
        expert_ids.reshape(1, tokens),
        gate_probs.reshape(1, tokens),
        activations,
        cotangent,
        experts,
    )
    pair, down = load(gate_up[0], down_proj[0], place)
    arrived = [send(pieces[high], 0, high * near) for high in range(far)]
    early, late = range(far // 2), range(far // 2, far)
    first = [send(pieces[high], group, high * near) for group in range(1, groups) for high in early]
    first = merge([arrived[high] for high in early] + first)
    loaded = pltpu.with_memory_space_constraint(down, pltpu.VMEM)
    second = merge([arrived[high] for high in late], (loaded,))
    mine = [send(second[low], 0, low) for low in range(near)]
    second = [stack(mine[: near // 2])]
    second.append(stack(mine[near // 2 :], (second[0],)))
    got = [send(first[low], 0, low) for low in range(near)]
    got += [send(part, group, 0) for group in range(groups) for part in second]
    homes = [
        (group, high * near + low)
        for low in range(near)
        for group in range(groups)
        for high in early
    ]
    homes += [
        (group, high * near + low)
        for group in range(groups)
        for low in range(near)
        for high in late
    ]
    gate_grad, up_grad, hidden, tok, cot, parts = expert_rows(
        got, homes, pair, down, experts, groups
    )
    returned = lax.all_to_all(parts, ("dp", "expert"), split_axis=0, concat_axis=0, tiled=True)
    down_total = down_grad([cot], hidden)
    pair_total = pair_grad([tok], gate_grad, up_grad)
    input_grad = spread(returned, place)
    return input_grad, pair_total, down_total


def solution(mesh):
    rows = P(("dp", "expert"), None)
    pair, down = P("expert", None, None, "dp"), P("expert", "dp", None)
    return jax.shard_map(
        per_device,
        mesh=mesh,
        in_specs=(rows, rows, rows, rows, pair, down),
        out_specs=(rows, pair, down),
        check_vma=False,
    )
```

```python
import functools

import jax
import jax.numpy as jnp
from jax import lax
from jax.experimental import pallas as pl
from jax.experimental.pallas import tpu as pltpu
from jax.sharding import PartitionSpec as P

CAP = 2
HALVES = 2
MIB = 1024 * 1024
VMEM = pl.BlockSpec(memory_space=pltpu.VMEM)
HBM = pl.BlockSpec(memory_space=pltpu.HBM)


def dot_nn(a, b):
    return lax.dot_general(a, b, (((1,), (0,)), ((), ())), preferred_element_type=jnp.float32)


def dot_nt(a, b):
    return lax.dot_general(a, b, (((1,), (1,)), ((), ())), preferred_element_type=jnp.float32)


def dot_tn(a, b):
    return lax.dot_general(a, b, (((0,), (0,)), ((), ())), preferred_element_type=jnp.float32)


def cost(flops, moved):
    return pl.CostEstimate(flops=int(flops), bytes_accessed=int(moved), transcendentals=0)


def params(mib):
    return pltpu.CompilerParams(vmem_limit_bytes=mib * MIB)


def in_hbm(value):
    return pltpu.with_memory_space_constraint(value, pltpu.HBM)


def bf16(*shape):
    return jax.ShapeDtypeStruct(shape, jnp.bfloat16)


def factors(experts):
    far = 1
    while 4 * far * far <= experts:
        far *= 2
    return far, experts // far


def route_kernel(experts, chunk, ids_hbm, probs_hbm, act_hbm, cot_hbm, *refs):
    far, near = factors(experts)
    sends, place_ref = refs[:far], refs[far]
    ids_ref, probs_ref, act, cot, sems = refs[far + 1 :]
    tokens, width = act.shape
    steps = width // chunk
    small = (
        pltpu.make_async_copy(ids_hbm, ids_ref, sems.at[2 * steps]),
        pltpu.make_async_copy(probs_hbm, probs_ref, sems.at[2 * steps + 1]),
    )
    large = []
    for step in range(steps):
        at = pl.ds(step * chunk, chunk)
        large.append(
            (
                pltpu.make_async_copy(act_hbm.at[:, at], act.at[:, at], sems.at[2 * step]),
                pltpu.make_async_copy(cot_hbm.at[:, at], cot.at[:, at], sems.at[2 * step + 1]),
            )
        )
    for one in small:
        one.start()
    for pair in large:
        for one in pair:
            one.start()
    for one in small:
        one.wait()

    me = lax.axis_index("expert")
    ids = ids_ref[...]
    inside = ids < experts
    units = lax.broadcasted_iota(jnp.int32, (experts, tokens), 0)
    onehot = jnp.where(units == ids, 1.0, 0.0)
    earlier = lax.broadcasted_iota(jnp.int32, (tokens, tokens), 0) < lax.broadcasted_iota(
        jnp.int32, (tokens, tokens), 1
    )
    before = dot_nn(onehot.astype(jnp.bfloat16), jnp.where(earlier, 1.0, 0.0).astype(jnp.bfloat16))
    rank = jnp.sum(before * onehot, axis=0, keepdims=True).astype(jnp.int32)
    slots = lax.broadcasted_iota(jnp.int32, (experts * CAP, tokens), 0)
    slot = jnp.where(inside, ids * CAP + rank, -1)
    place_ref[...] = jnp.where(slots == slot, 1.0, 0.0).astype(jnp.bfloat16)
    turned = jnp.where(inside, (ids ^ me) * CAP + rank, -1)
    pick = jnp.where(slots == turned, 1.0, 0.0)
    weight = jnp.sum(pick * probs_ref[...], axis=1, keepdims=True)
    pick = pick.astype(jnp.bfloat16)
    for step in range(steps):
        at = slice(step * chunk, (step + 1) * chunk)
        for one in large[step]:
            one.wait()
        rows_tok = dot_nn(pick, act[:, at]).astype(jnp.bfloat16)
        rows_cot = (weight * dot_nn(pick, cot[:, at])).astype(jnp.bfloat16)
        for unit in range(experts):
            rows = slice(unit * CAP, (unit + 1) * CAP)
            sends[unit // near][unit % near, :CAP, at] = rows_tok[rows]
            sends[unit // near][unit % near, CAP:, at] = rows_cot[rows]


def route(ids, probs, act, cot, experts):
    tokens, width = act.shape
    chunk = min(1024, width)
    far, near = factors(experts)
    out = pl.pallas_call(
        functools.partial(route_kernel, experts, chunk),
        in_specs=[HBM] * 4,
        out_specs=[VMEM] * (far + 1),
        out_shape=[bf16(near, 2 * CAP, width)] * far + [bf16(experts * CAP, tokens)],
        scratch_shapes=[
            pltpu.VMEM((1, tokens), jnp.int32),
            pltpu.VMEM((1, tokens), jnp.float32),
            pltpu.VMEM((tokens, width), jnp.bfloat16),
            pltpu.VMEM((tokens, width), jnp.bfloat16),
            pltpu.SemaphoreType.DMA((2 * (width // chunk) + 2,)),
        ],
        compiler_params=params(16),
        cost_estimate=cost(4 * experts * CAP * tokens * width, 4 * tokens * width),
        name="route_rows",
    )(in_hbm(ids), in_hbm(probs), in_hbm(act), in_hbm(cot))
    return out[:far], out[far]


def merge_kernel(far, *refs):
    pieces, outs = refs[:far], refs[len(refs) - refs[0].shape[0] :]
    for index, out in enumerate(outs):
        rows = [piece[index, :CAP, :] for piece in pieces]
        rows += [piece[index, CAP:, :] for piece in pieces]
        out[...] = jnp.concatenate(rows, axis=0)


def merge(pieces, after=()):
    far = len(pieces)
    near, _, width = pieces[0].shape
    return pl.pallas_call(
        functools.partial(merge_kernel, far),
        in_specs=[VMEM] * far + [pl.BlockSpec(memory_space=pl.ANY)] * len(after),
        out_specs=[VMEM] * near,
        out_shape=[bf16(2 * CAP * far, width)] * near,
        compiler_params=params(16),
        cost_estimate=cost(0, 8 * near * CAP * far * width),
        name="merge_rows",
    )(*pieces, *after)


def stack_kernel(number, *refs):
    pieces, outs = refs[:number], refs[number:]
    rows, width = pieces[0].shape[0] // 2, outs[0].shape[1]
    for half, out in enumerate(outs):
        at = slice(half * width, (half + 1) * width)
        picked = [piece[:rows, at] for piece in pieces] + [piece[rows:, at] for piece in pieces]
        out[...] = jnp.concatenate(picked, axis=0)


def stack(pieces):
    number = len(pieces)
    rows, width = pieces[0].shape
    return pl.pallas_call(
        functools.partial(stack_kernel, number),
        in_specs=[VMEM] * number,
        out_specs=[VMEM] * HALVES,
        out_shape=[bf16(number * rows, width // HALVES)] * HALVES,
        compiler_params=params(16),
        cost_estimate=cost(0, 4 * number * rows * width),
        name="stack_rows",
    )(*pieces)


def load_kernel(chunk, pair_hbm, down_hbm, after, pair, down, sems):
    del after
    width = down.shape[1]
    copies = []
    for step in range(width // chunk):
        at = pl.ds(step * chunk, chunk)
        copies += [
            pltpu.make_async_copy(pair_hbm.at[:, at, :], pair.at[:, at, :], sems.at[0, step]),
            pltpu.make_async_copy(down_hbm.at[:, at], down.at[:, at], sems.at[1, step]),
        ]
    for one in copies:
        one.start()
    for one in copies:
        one.wait()


def load(pair, down, after):
    units, width = down.shape
    chunk = min(1024, width)
    return pl.pallas_call(
        functools.partial(load_kernel, chunk),
        in_specs=[HBM] * 2 + [pl.BlockSpec(memory_space=pl.ANY)],
        out_specs=[VMEM] * 2,
        out_shape=[pltpu.VMEM(pair.shape, jnp.bfloat16), pltpu.VMEM(down.shape, jnp.bfloat16)],
        scratch_shapes=[pltpu.SemaphoreType.DMA((2, width // chunk))],
        compiler_params=params(28),
        cost_estimate=cost(0, 6 * width * units),
        name="load_weights",
    )(in_hbm(pair), in_hbm(down), after)


def gather_columns(near_rows, far_rows, near_at, far_at):
    pieces = [(ref, near_at) for ref in near_rows] + [(ref, far_at) for ref in far_rows]
    tok = [ref[: ref.shape[0] // 2, at] for ref, at in pieces]
    cot = [ref[ref.shape[0] // 2 :, at] for ref, at in pieces]
    return jnp.concatenate(tok, axis=0), jnp.concatenate(cot, axis=0)


def first_kernel(near, groups, chunk, *refs):
    near_rows, far_rows = refs[:near], refs[near : near + groups]
    pair, down, gate, up, hid, tok_all, cot_all = refs[near + groups :]
    for step in range(tok_all.shape[1] // chunk):
        at = slice(step * chunk, (step + 1) * chunk)
        tok, cot = gather_columns(near_rows, far_rows, at, at)
        tok_all[:, at] = tok
        cot_all[:, at] = cot
        part_gate = dot_nn(tok, pair[0, at, :])
        part_up = dot_nn(tok, pair[1, at, :])
        part_hid = dot_nt(cot, down[:, at])
        if step == 0:
            gate[...], up[...], hid[...] = part_gate, part_up, part_hid
        else:
            gate[...] += part_gate
            up[...] += part_up
            hid[...] += part_hid


def first_half(near_rows, far_rows, pair, down):
    near, groups = len(near_rows), len(far_rows)
    total = (near * near_rows[0].shape[0] + groups * far_rows[0].shape[0]) // 2
    half = far_rows[0].shape[1]
    units = down.shape[0]
    chunk = min(1024, half)
    return pl.pallas_call(
        functools.partial(first_kernel, near, groups, chunk),
        in_specs=[VMEM] * (near + groups + 2),
        out_specs=[VMEM] * 5,
        out_shape=[jax.ShapeDtypeStruct((total, units), jnp.float32)] * 3
        + [bf16(total, half)] * 2,
        compiler_params=params(24),
        cost_estimate=cost(6 * total * half * units, 6 * half * units),
        name="first_half",
    )(*near_rows, *far_rows, pair, down)


def second_kernel(homes, experts, near, groups, chunk, *refs):
    near_rows, far_rows = refs[:near], refs[near : near + groups]
    gate_sum, up_sum, hid_sum, pair, down = refs[near + groups : near + groups + 5]
    gate_out, up_out, hidden_out, tok_all, cot_all, parts_hbm = refs[
        near + groups + 5 : near + groups + 11
    ]
    parts, acc_gate, acc_up, acc_hid, sems = refs[near + groups + 11 :]
    half, width = tok_all.shape[1], down.shape[1]
    for step in range(half // chunk):
        at = slice(step * chunk, (step + 1) * chunk)
        there = slice(half + step * chunk, half + (step + 1) * chunk)
        tok, cot = gather_columns(near_rows, far_rows, there, at)
        tok_all[:, at] = tok
        cot_all[:, at] = cot
        before = (gate_sum, up_sum, hid_sum) if step == 0 else (acc_gate, acc_up, acc_hid)
        acc_gate[...] = before[0][...] + dot_nn(tok, pair[0, there, :])
        acc_up[...] = before[1][...] + dot_nn(tok, pair[1, there, :])
        acc_hid[...] = before[2][...] + dot_nt(cot, down[:, there])
    pre_gate, pre_up, hidden_grad = acc_gate[...], acc_up[...], acc_hid[...]
    sigmoid_gate = jax.nn.sigmoid(pre_gate)
    activated = pre_gate * sigmoid_gate
    hidden_out[...] = (activated * pre_up).astype(jnp.bfloat16)
    gate_grad = (
        hidden_grad * pre_up * sigmoid_gate * (1.0 + pre_gate * (1.0 - sigmoid_gate))
    ).astype(jnp.bfloat16)
    up_grad = (hidden_grad * activated).astype(jnp.bfloat16)
    gate_out[...] = gate_grad
    up_out[...] = up_grad
    me, group = lax.axis_index("expert"), lax.axis_index("dp")
    rows = [
        lax.rem(group - back + groups, groups) * experts + (me ^ turn) for back, turn in homes
    ]
    copies = []
    for step in range(width // chunk):
        at = slice(step * chunk, (step + 1) * chunk)
        value = dot_nt(gate_grad, pair[0, at, :]) + dot_nt(up_grad, pair[1, at, :])
        value = value.astype(jnp.bfloat16)
        for block, row in enumerate(rows):
            parts[row, :, at] = value[block * CAP : (block + 1) * CAP]
        where = pl.ds(step * chunk, chunk)
        one = pltpu.make_async_copy(
            parts.at[:, :, where], parts_hbm.at[:, :, where], sems.at[step]
        )
        one.start()
        copies.append(one)
    for one in copies:
        one.wait()


def second_half(near_rows, far_rows, sums, pair, down, homes, experts):
    near, groups = len(near_rows), len(far_rows)
    total, units = sums[0].shape
    half, width = far_rows[0].shape[1], down.shape[1]
    chunk = min(1024, half)
    blocks = total // CAP
    return pl.pallas_call(
        functools.partial(second_kernel, homes, experts, near, groups, chunk),
        in_specs=[VMEM] * (near + groups + 5),
        out_specs=[VMEM] * 5 + [HBM],
        out_shape=[bf16(total, units)] * 3
        + [bf16(total, half)] * 2
        + [pltpu.HBM((blocks, CAP, width), jnp.bfloat16)],
        scratch_shapes=[
            pltpu.VMEM((blocks, CAP, width), jnp.bfloat16),
            pltpu.VMEM((total, units), jnp.float32),
            pltpu.VMEM((total, units), jnp.float32),
            pltpu.VMEM((total, units), jnp.float32),
            pltpu.SemaphoreType.DMA((width // chunk,)),
        ],
        compiler_params=params(24),
        cost_estimate=cost(7 * total * width * units, 6 * width * units),
        name="second_half",
    )(*near_rows, *far_rows, *sums, pair, down)


def pair_grad_kernel(blocks, chunk, *refs):
    toks, gate_ref, up_ref = refs[:blocks], refs[blocks], refs[blocks + 1]
    half = toks[0].shape[1]
    out_hbm, buffer, sems = refs[blocks + 2 :]
    copies = []
    for step in range(blocks * half // chunk):
        at = slice(step * chunk, (step + 1) * chunk)
        tok = toks[step * chunk // half][:, step * chunk % half : step * chunk % half + chunk]
        for side, ref in enumerate((gate_ref, up_ref)):
            buffer[side, at, :] = dot_tn(tok, ref[...]).astype(jnp.bfloat16)
        where = pl.ds(step * chunk, chunk)
        one = pltpu.make_async_copy(
            buffer.at[:, where, :], out_hbm.at[0, :, where, :], sems.at[step]
        )
        one.start()
        copies.append(one)
    for one in copies:
        one.wait()


def pair_grad(toks, gate_grad, up_grad):
    blocks = len(toks)
    width = blocks * toks[0].shape[1]
    total, units = gate_grad.shape
    chunk = min(512, width // blocks)
    return pl.pallas_call(
        functools.partial(pair_grad_kernel, blocks, chunk),
        in_specs=[VMEM] * (blocks + 2),
        out_specs=HBM,
        out_shape=bf16(1, 2, width, units),
        scratch_shapes=[
            pltpu.VMEM((2, width, units), jnp.bfloat16),
            pltpu.SemaphoreType.DMA((width // chunk,)),
        ],
        compiler_params=params(32),
        cost_estimate=cost(4 * total * width * units, 4 * width * units),
        name="pair_grad",
    )(*toks, gate_grad, up_grad)


def down_grad_kernel(blocks, chunk, *refs):
    cots, hidden_ref, out_hbm = refs[:blocks], refs[blocks], refs[blocks + 1]
    buffer, sems = refs[blocks + 2 :]
    half = cots[0].shape[1]
    copies = []
    for step in range(blocks * half // chunk):
        at = slice(step * chunk, (step + 1) * chunk)
        cot = cots[step * chunk // half][:, step * chunk % half : step * chunk % half + chunk]
        buffer[:, at] = dot_tn(hidden_ref[...], cot).astype(jnp.bfloat16)
        where = pl.ds(step * chunk, chunk)
        one = pltpu.make_async_copy(buffer.at[:, where], out_hbm.at[0, :, where], sems.at[step])
        one.start()
        copies.append(one)
    for one in copies:
        one.wait()


def down_grad(cots, hidden):
    blocks = len(cots)
    width = blocks * cots[0].shape[1]
    total, units = hidden.shape
    chunk = min(1024, width // blocks)
    return pl.pallas_call(
        functools.partial(down_grad_kernel, blocks, chunk),
        in_specs=[VMEM] * (blocks + 1),
        out_specs=HBM,
        out_shape=bf16(1, units, width),
        scratch_shapes=[
            pltpu.VMEM((units, width), jnp.bfloat16),
            pltpu.SemaphoreType.DMA((width // chunk,)),
        ],
        compiler_params=params(24),
        cost_estimate=cost(2 * total * width * units, 2 * width * units),
        name="down_grad",
    )(*cots, hidden)


def spread_kernel(chunk, rows_ref, place_ref, out_hbm, buffer, sems):
    blocks, _, width = rows_ref.shape
    place = jnp.concatenate([place_ref[...]] * (blocks * CAP // place_ref.shape[0]), axis=0)
    copies = []
    for step in range(width // chunk):
        at = slice(step * chunk, (step + 1) * chunk)
        rows = jnp.concatenate([rows_ref[block, :, at] for block in range(blocks)], axis=0)
        buffer[:, at] = dot_tn(place, rows).astype(jnp.bfloat16)
        where = pl.ds(step * chunk, chunk)
        one = pltpu.make_async_copy(buffer.at[:, where], out_hbm.at[:, where], sems.at[step])
        one.start()
        copies.append(one)
    for one in copies:
        one.wait()


def spread(rows, place):
    width = rows.shape[2]
    slots, tokens = place.shape
    chunk = min(1024, width)
    return pl.pallas_call(
        functools.partial(spread_kernel, chunk),
        in_specs=[VMEM] * 2,
        out_specs=HBM,
        out_shape=bf16(tokens, width),
        scratch_shapes=[
            pltpu.VMEM((tokens, width), jnp.bfloat16),
            pltpu.SemaphoreType.DMA((width // chunk,)),
        ],
        compiler_params=params(16),
        cost_estimate=cost(2 * slots * tokens * width, 2 * tokens * width),
        name="spread_rows",
    )(rows, place)


def per_device(activations, cotangent, expert_ids, gate_probs, gate_up, down_proj):
    experts = lax.axis_size("expert")
    groups = lax.axis_size("dp")
    tokens = activations.shape[0]
    far, near = factors(experts)

    def send(value, by_group, by_expert):
        if by_group == 0 and by_expert == 0:
            return value
        pairs = []
        for group in range(groups):
            to = (group + by_group) % groups
            for i in range(experts):
                pairs.append((group * experts + i, to * experts + (i ^ by_expert)))
        return lax.ppermute(value, ("dp", "expert"), pairs)

    pieces, place = route(
        expert_ids.reshape(1, tokens),
        gate_probs.reshape(1, tokens),
        activations,
        cotangent,
        experts,
    )
    pair, down = load(gate_up[0], down_proj[0], place)
    arrived = [send(pieces[high], 0, high * near) for high in range(far)]
    early, late = range(far // 2), range(far // 2, far)
    first = [send(pieces[high], group, high * near) for group in range(1, groups) for high in early]
    first = merge([arrived[high] for high in early] + first)
    loaded = pltpu.with_memory_space_constraint(down, pltpu.VMEM)
    second = merge([arrived[high] for high in late], (loaded,))
    mine = [send(second[low], 0, low) for low in range(near)]
    halves = stack(mine)
    near_rows = [send(first[low], 0, low) for low in range(near)]
    far_rows = [[send(half, group, 0) for group in range(groups)] for half in halves]
    homes = [
        (group, high * near + low)
        for low in range(near)
        for group in range(groups)
        for high in early
    ]
    homes += [
        (group, high * near + low)
        for group in range(groups)
        for low in range(near)
        for high in late
    ]
    pair = pltpu.with_memory_space_constraint(pair, pltpu.VMEM)
    *sums, tok_first, cot_first = first_half(near_rows, far_rows[0], pair, loaded)
    gate_grad, up_grad, hidden, tok_second, cot_second, parts = second_half(
        near_rows, far_rows[1], sums, pair, loaded, homes, experts
    )
    returned = lax.all_to_all(parts, ("dp", "expert"), split_axis=0, concat_axis=0, tiled=True)
    down_total = down_grad([cot_first, cot_second], hidden)
    pair_total = pair_grad([tok_first, tok_second], gate_grad, up_grad)
    input_grad = spread(returned, place)
    return input_grad, pair_total, down_total


def solution(mesh):
    rows = P(("dp", "expert"), None)
    pair, down = P("expert", None, None, "dp"), P("expert", "dp", None)
    return jax.shard_map(
        per_device,
        mesh=mesh,
        in_specs=(rows, rows, rows, rows, pair, down),
        out_specs=(rows, pair, down),
        check_vma=False,
    )
```

```python
import functools

import jax
import jax.numpy as jnp
from jax import lax
from jax.experimental import pallas as pl
from jax.experimental.pallas import tpu as pltpu
from jax.sharding import PartitionSpec as P

CAP = 2
HALVES = 2
MIB = 1024 * 1024
VMEM = pl.BlockSpec(memory_space=pltpu.VMEM)
HBM = pl.BlockSpec(memory_space=pltpu.HBM)


def dot_nn(a, b):
    return lax.dot_general(a, b, (((1,), (0,)), ((), ())), preferred_element_type=jnp.float32)


def dot_nt(a, b):
    return lax.dot_general(a, b, (((1,), (1,)), ((), ())), preferred_element_type=jnp.float32)


def dot_tn(a, b):
    return lax.dot_general(a, b, (((0,), (0,)), ((), ())), preferred_element_type=jnp.float32)


def cost(flops, moved):
    return pl.CostEstimate(flops=int(flops), bytes_accessed=int(moved), transcendentals=0)


def params(mib):
    return pltpu.CompilerParams(vmem_limit_bytes=mib * MIB)


def in_hbm(value):
    return pltpu.with_memory_space_constraint(value, pltpu.HBM)


def bf16(*shape):
    return jax.ShapeDtypeStruct(shape, jnp.bfloat16)


def factors(experts):
    far = 1
    while 4 * far * far <= experts:
        far *= 2
    return far, experts // far


def route_kernel(experts, chunk, ids_hbm, probs_hbm, act_hbm, cot_hbm, *refs):
    far, near = factors(experts)
    sends, place_ref = refs[:far], refs[far]
    ids_ref, probs_ref, act, cot, sems = refs[far + 1 :]
    tokens, width = act.shape
    steps = width // chunk
    small = (
        pltpu.make_async_copy(ids_hbm, ids_ref, sems.at[2 * steps]),
        pltpu.make_async_copy(probs_hbm, probs_ref, sems.at[2 * steps + 1]),
    )
    large = []
    for step in range(steps):
        at = pl.ds(step * chunk, chunk)
        large.append(
            (
                pltpu.make_async_copy(act_hbm.at[:, at], act.at[:, at], sems.at[2 * step]),
                pltpu.make_async_copy(cot_hbm.at[:, at], cot.at[:, at], sems.at[2 * step + 1]),
            )
        )
    for one in small:
        one.start()
    for pair in large:
        for one in pair:
            one.start()
    for one in small:
        one.wait()

    me = lax.axis_index("expert")
    ids = ids_ref[...]
    inside = ids < experts
    units = lax.broadcasted_iota(jnp.int32, (experts, tokens), 0)
    onehot = jnp.where(units == ids, 1.0, 0.0)
    earlier = lax.broadcasted_iota(jnp.int32, (tokens, tokens), 0) < lax.broadcasted_iota(
        jnp.int32, (tokens, tokens), 1
    )
    before = dot_nn(onehot.astype(jnp.bfloat16), jnp.where(earlier, 1.0, 0.0).astype(jnp.bfloat16))
    rank = jnp.sum(before * onehot, axis=0, keepdims=True).astype(jnp.int32)
    slots = lax.broadcasted_iota(jnp.int32, (experts * CAP, tokens), 0)
    slot = jnp.where(inside, ids * CAP + rank, -1)
    place_ref[...] = jnp.where(slots == slot, 1.0, 0.0).astype(jnp.bfloat16)
    turned = jnp.where(inside, (ids ^ me) * CAP + rank, -1)
    pick = jnp.where(slots == turned, 1.0, 0.0)
    weight = jnp.sum(pick * probs_ref[...], axis=1, keepdims=True)
    pick = pick.astype(jnp.bfloat16)
    for step in range(steps):
        at = slice(step * chunk, (step + 1) * chunk)
        for one in large[step]:
            one.wait()
        rows_tok = dot_nn(pick, act[:, at]).astype(jnp.bfloat16)
        rows_cot = (weight * dot_nn(pick, cot[:, at])).astype(jnp.bfloat16)
        for unit in range(experts):
            rows = slice(unit * CAP, (unit + 1) * CAP)
            sends[unit // near][unit % near, :CAP, at] = rows_tok[rows]
            sends[unit // near][unit % near, CAP:, at] = rows_cot[rows]


def route(ids, probs, act, cot, experts):
    tokens, width = act.shape
    chunk = min(1024, width)
    far, near = factors(experts)
    out = pl.pallas_call(
        functools.partial(route_kernel, experts, chunk),
        in_specs=[HBM] * 4,
        out_specs=[VMEM] * (far + 1),
        out_shape=[bf16(near, 2 * CAP, width)] * far + [bf16(experts * CAP, tokens)],
        scratch_shapes=[
            pltpu.VMEM((1, tokens), jnp.int32),
            pltpu.VMEM((1, tokens), jnp.float32),
            pltpu.VMEM((tokens, width), jnp.bfloat16),
            pltpu.VMEM((tokens, width), jnp.bfloat16),
            pltpu.SemaphoreType.DMA((2 * (width // chunk) + 2,)),
        ],
        compiler_params=params(16),
        cost_estimate=cost(4 * experts * CAP * tokens * width, 4 * tokens * width),
        name="route_rows",
    )(in_hbm(ids), in_hbm(probs), in_hbm(act), in_hbm(cot))
    return out[:far], out[far]


def merge_kernel(far, *refs):
    pieces, outs = refs[:far], refs[len(refs) - refs[0].shape[0] :]
    for index, out in enumerate(outs):
        rows = [piece[index, :CAP, :] for piece in pieces]
        rows += [piece[index, CAP:, :] for piece in pieces]
        out[...] = jnp.concatenate(rows, axis=0)


def merge(pieces, after=()):
    far = len(pieces)
    near, _, width = pieces[0].shape
    return pl.pallas_call(
        functools.partial(merge_kernel, far),
        in_specs=[VMEM] * far + [pl.BlockSpec(memory_space=pl.ANY)] * len(after),
        out_specs=[VMEM] * near,
        out_shape=[bf16(2 * CAP * far, width)] * near,
        compiler_params=params(16),
        cost_estimate=cost(0, 8 * near * CAP * far * width),
        name="merge_rows",
    )(*pieces, *after)


def stack_kernel(number, *refs):
    pieces, outs = refs[:number], refs[number:]
    rows, width = pieces[0].shape[0] // 2, outs[0].shape[1]
    for half, out in enumerate(outs):
        at = slice(half * width, (half + 1) * width)
        picked = [piece[:rows, at] for piece in pieces] + [piece[rows:, at] for piece in pieces]
        out[...] = jnp.concatenate(picked, axis=0)


def stack(pieces):
    number = len(pieces)
    rows, width = pieces[0].shape
    return pl.pallas_call(
        functools.partial(stack_kernel, number),
        in_specs=[VMEM] * number,
        out_specs=[VMEM] * HALVES,
        out_shape=[bf16(number * rows, width // HALVES)] * HALVES,
        compiler_params=params(16),
        cost_estimate=cost(0, 4 * number * rows * width),
        name="stack_rows",
    )(*pieces)


def load_kernel(chunk, pair_hbm, down_hbm, after, pair, down, sems):
    del after
    width = down.shape[1]
    copies = []
    for step in range(width // chunk):
        at = pl.ds(step * chunk, chunk)
        copies += [
            pltpu.make_async_copy(pair_hbm.at[:, at, :], pair.at[:, at, :], sems.at[0, step]),
            pltpu.make_async_copy(down_hbm.at[:, at], down.at[:, at], sems.at[1, step]),
        ]
    for one in copies:
        one.start()
    for one in copies:
        one.wait()


def load(pair, down, after):
    units, width = down.shape
    chunk = min(1024, width)
    return pl.pallas_call(
        functools.partial(load_kernel, chunk),
        in_specs=[HBM] * 2 + [pl.BlockSpec(memory_space=pl.ANY)],
        out_specs=[VMEM] * 2,
        out_shape=[pltpu.VMEM(pair.shape, jnp.bfloat16), pltpu.VMEM(down.shape, jnp.bfloat16)],
        scratch_shapes=[pltpu.SemaphoreType.DMA((2, width // chunk))],
        compiler_params=params(28),
        cost_estimate=cost(0, 6 * width * units),
        name="load_weights",
    )(in_hbm(pair), in_hbm(down), after)


def gather_columns(near_rows, far_rows, near_at, far_at):
    pieces = [(ref, near_at) for ref in near_rows] + [(ref, far_at) for ref in far_rows]
    tok = [ref[: ref.shape[0] // 2, at] for ref, at in pieces]
    cot = [ref[ref.shape[0] // 2 :, at] for ref, at in pieces]
    return jnp.concatenate(tok, axis=0), jnp.concatenate(cot, axis=0)


def first_kernel(near, groups, chunk, *refs):
    near_rows, far_rows = refs[:near], refs[near : near + groups]
    pair, down, gate, up, hid, tok_all, cot_all = refs[near + groups :]
    for step in range(tok_all.shape[1] // chunk):
        at = slice(step * chunk, (step + 1) * chunk)
        tok, cot = gather_columns(near_rows, far_rows, at, at)
        tok_all[:, at] = tok
        cot_all[:, at] = cot
        part_gate = dot_nn(tok, pair[0, at, :])
        part_up = dot_nn(tok, pair[1, at, :])
        part_hid = dot_nt(cot, down[:, at])
        if step == 0:
            gate[...], up[...], hid[...] = part_gate, part_up, part_hid
        else:
            gate[...] += part_gate
            up[...] += part_up
            hid[...] += part_hid


def first_half(near_rows, far_rows, pair, down):
    near, groups = len(near_rows), len(far_rows)
    total = (near * near_rows[0].shape[0] + groups * far_rows[0].shape[0]) // 2
    half = far_rows[0].shape[1]
    units = down.shape[0]
    chunk = half
    return pl.pallas_call(
        functools.partial(first_kernel, near, groups, chunk),
        in_specs=[VMEM] * (near + groups + 2),
        out_specs=[VMEM] * 5,
        out_shape=[jax.ShapeDtypeStruct((total, units), jnp.float32)] * 3
        + [bf16(total, half)] * 2,
        compiler_params=params(24),
        cost_estimate=cost(6 * total * half * units, 6 * half * units),
        name="first_half",
    )(*near_rows, *far_rows, pair, down)


def second_kernel(homes, experts, near, groups, chunk, *refs):
    near_rows, far_rows = refs[:near], refs[near : near + groups]
    gate_sum, up_sum, hid_sum, pair, down = refs[near + groups : near + groups + 5]
    gate_out, up_out, hidden_out, tok_all, cot_all, parts_hbm = refs[
        near + groups + 5 : near + groups + 11
    ]
    parts, sems = refs[near + groups + 11 :]
    half, width = tok_all.shape[1], down.shape[1]
    there = slice(half, width)
    tok, cot = gather_columns(near_rows, far_rows, there, slice(0, half))
    tok_all[...] = tok
    cot_all[...] = cot
    pre_gate = gate_sum[...] + dot_nn(tok, pair[0, there, :])
    pre_up = up_sum[...] + dot_nn(tok, pair[1, there, :])
    hidden_grad = hid_sum[...] + dot_nt(cot, down[:, there])
    sigmoid_gate = jax.nn.sigmoid(pre_gate)
    activated = pre_gate * sigmoid_gate
    hidden_out[...] = (activated * pre_up).astype(jnp.bfloat16)
    gate_grad = (
        hidden_grad * pre_up * sigmoid_gate * (1.0 + pre_gate * (1.0 - sigmoid_gate))
    ).astype(jnp.bfloat16)
    up_grad = (hidden_grad * activated).astype(jnp.bfloat16)
    gate_out[...] = gate_grad
    up_out[...] = up_grad
    me, group = lax.axis_index("expert"), lax.axis_index("dp")
    rows = [
        lax.rem(group - back + groups, groups) * experts + (me ^ turn) for back, turn in homes
    ]
    copies = []
    for step in range(width // chunk):
        at = slice(step * chunk, (step + 1) * chunk)
        value = dot_nt(gate_grad, pair[0, at, :]) + dot_nt(up_grad, pair[1, at, :])
        value = value.astype(jnp.bfloat16)
        for block, row in enumerate(rows):
            parts[row, :, at] = value[block * CAP : (block + 1) * CAP]
        where = pl.ds(step * chunk, chunk)
        one = pltpu.make_async_copy(
            parts.at[:, :, where], parts_hbm.at[:, :, where], sems.at[step]
        )
        one.start()
        copies.append(one)
    for one in copies:
        one.wait()


def second_half(near_rows, far_rows, sums, pair, down, homes, experts):
    near, groups = len(near_rows), len(far_rows)
    total, units = sums[0].shape
    half, width = far_rows[0].shape[1], down.shape[1]
    chunk = min(512, half)
    blocks = total // CAP
    return pl.pallas_call(
        functools.partial(second_kernel, homes, experts, near, groups, chunk),
        in_specs=[VMEM] * (near + groups + 5),
        out_specs=[VMEM] * 5 + [HBM],
        out_shape=[bf16(total, units)] * 3
        + [bf16(total, half)] * 2
        + [pltpu.HBM((blocks, CAP, width), jnp.bfloat16)],
        scratch_shapes=[
            pltpu.VMEM((blocks, CAP, width), jnp.bfloat16),
            pltpu.SemaphoreType.DMA((width // chunk,)),
        ],
        compiler_params=params(24),
        cost_estimate=cost(7 * total * width * units, 6 * width * units),
        name="second_half",
    )(*near_rows, *far_rows, *sums, pair, down)


def pair_grad_kernel(blocks, chunk, *refs):
    toks, gate_ref, up_ref = refs[:blocks], refs[blocks], refs[blocks + 1]
    half = toks[0].shape[1]
    out_hbm, buffer, sems = refs[blocks + 2 :]
    copies = []
    for step in range(blocks * half // chunk):
        at = slice(step * chunk, (step + 1) * chunk)
        tok = toks[step * chunk // half][:, step * chunk % half : step * chunk % half + chunk]
        for side, ref in enumerate((gate_ref, up_ref)):
            buffer[side, at, :] = dot_tn(tok, ref[...]).astype(jnp.bfloat16)
        where = pl.ds(step * chunk, chunk)
        one = pltpu.make_async_copy(
            buffer.at[:, where, :], out_hbm.at[0, :, where, :], sems.at[step]
        )
        one.start()
        copies.append(one)
    for one in copies:
        one.wait()


def pair_grad(toks, gate_grad, up_grad):
    blocks = len(toks)
    width = blocks * toks[0].shape[1]
    total, units = gate_grad.shape
    chunk = min(512, width // blocks)
    return pl.pallas_call(
        functools.partial(pair_grad_kernel, blocks, chunk),
        in_specs=[VMEM] * (blocks + 2),
        out_specs=HBM,
        out_shape=bf16(1, 2, width, units),
        scratch_shapes=[
            pltpu.VMEM((2, width, units), jnp.bfloat16),
            pltpu.SemaphoreType.DMA((width // chunk,)),
        ],
        compiler_params=params(32),
        cost_estimate=cost(4 * total * width * units, 4 * width * units),
        name="pair_grad",
    )(*toks, gate_grad, up_grad)


def down_grad_kernel(blocks, chunk, *refs):
    cots, hidden_ref, out_hbm = refs[:blocks], refs[blocks], refs[blocks + 1]
    buffer, sems = refs[blocks + 2 :]
    half = cots[0].shape[1]
    copies = []
    for step in range(blocks * half // chunk):
        at = slice(step * chunk, (step + 1) * chunk)
        cot = cots[step * chunk // half][:, step * chunk % half : step * chunk % half + chunk]
        buffer[:, at] = dot_tn(hidden_ref[...], cot).astype(jnp.bfloat16)
        where = pl.ds(step * chunk, chunk)
        one = pltpu.make_async_copy(buffer.at[:, where], out_hbm.at[0, :, where], sems.at[step])
        one.start()
        copies.append(one)
    for one in copies:
        one.wait()


def down_grad(cots, hidden):
    blocks = len(cots)
    width = blocks * cots[0].shape[1]
    total, units = hidden.shape
    chunk = min(1024, width // blocks)
    return pl.pallas_call(
        functools.partial(down_grad_kernel, blocks, chunk),
        in_specs=[VMEM] * (blocks + 1),
        out_specs=HBM,
        out_shape=bf16(1, units, width),
        scratch_shapes=[
            pltpu.VMEM((units, width), jnp.bfloat16),
            pltpu.SemaphoreType.DMA((width // chunk,)),
        ],
        compiler_params=params(24),
        cost_estimate=cost(2 * total * width * units, 2 * width * units),
        name="down_grad",
    )(*cots, hidden)


def spread_kernel(chunk, rows_ref, place_ref, out_hbm, buffer, sems):
    blocks, _, width = rows_ref.shape
    place = jnp.concatenate([place_ref[...]] * (blocks * CAP // place_ref.shape[0]), axis=0)
    copies = []
    for step in range(width // chunk):
        at = slice(step * chunk, (step + 1) * chunk)
        rows = jnp.concatenate([rows_ref[block, :, at] for block in range(blocks)], axis=0)
        buffer[:, at] = dot_tn(place, rows).astype(jnp.bfloat16)
        where = pl.ds(step * chunk, chunk)
        one = pltpu.make_async_copy(buffer.at[:, where], out_hbm.at[:, where], sems.at[step])
        one.start()
        copies.append(one)
    for one in copies:
        one.wait()


def spread(rows, place):
    width = rows.shape[2]
    slots, tokens = place.shape
    chunk = min(1024, width)
    return pl.pallas_call(
        functools.partial(spread_kernel, chunk),
        in_specs=[VMEM] * 2,
        out_specs=HBM,
        out_shape=bf16(tokens, width),
        scratch_shapes=[
            pltpu.VMEM((tokens, width), jnp.bfloat16),
            pltpu.SemaphoreType.DMA((width // chunk,)),
        ],
        compiler_params=params(16),
        cost_estimate=cost(2 * slots * tokens * width, 2 * tokens * width),
        name="spread_rows",
    )(rows, place)


def per_device(activations, cotangent, expert_ids, gate_probs, gate_up, down_proj):
    experts = lax.axis_size("expert")
    groups = lax.axis_size("dp")
    tokens = activations.shape[0]
    far, near = factors(experts)

    def send(value, by_group, by_expert):
        if by_group == 0 and by_expert == 0:
            return value
        pairs = []
        for group in range(groups):
            to = (group + by_group) % groups
            for i in range(experts):
                pairs.append((group * experts + i, to * experts + (i ^ by_expert)))
        return lax.ppermute(value, ("dp", "expert"), pairs)

    pieces, place = route(
        expert_ids.reshape(1, tokens),
        gate_probs.reshape(1, tokens),
        activations,
        cotangent,
        experts,
    )
    pair, down = load(gate_up[0], down_proj[0], place)
    arrived = [send(pieces[high], 0, high * near) for high in range(far)]
    early, late = range(far // 2), range(far // 2, far)
    first = [send(pieces[high], group, high * near) for group in range(1, groups) for high in early]
    first = merge([arrived[high] for high in early] + first)
    loaded = pltpu.with_memory_space_constraint(down, pltpu.VMEM)
    second = merge([arrived[high] for high in late], (loaded,))
    mine = [send(second[low], 0, low) for low in range(near)]
    halves = stack(mine)
    near_rows = [send(first[low], 0, low) for low in range(near)]
    far_rows = [[send(half, group, 0) for group in range(groups)] for half in halves]
    homes = [
        (group, high * near + low)
        for low in range(near)
        for group in range(groups)
        for high in early
    ]
    homes += [
        (group, high * near + low)
        for group in range(groups)
        for low in range(near)
        for high in late
    ]
    pair = pltpu.with_memory_space_constraint(pair, pltpu.VMEM)
    *sums, tok_first, cot_first = first_half(near_rows, far_rows[0], pair, loaded)
    gate_grad, up_grad, hidden, tok_second, cot_second, parts = second_half(
        near_rows, far_rows[1], sums, pair, loaded, homes, experts
    )
    returned = lax.all_to_all(parts, ("dp", "expert"), split_axis=0, concat_axis=0, tiled=True)
    down_total = down_grad([cot_first, cot_second], hidden)
    pair_total = pair_grad([tok_first, tok_second], gate_grad, up_grad)
    input_grad = spread(returned, place)
    return input_grad, pair_total, down_total


def solution(mesh):
    rows = P(("dp", "expert"), None)
    pair, down = P("expert", None, None, "dp"), P("expert", "dp", None)
    return jax.shard_map(
        per_device,
        mesh=mesh,
        in_specs=(rows, rows, rows, rows, pair, down),
        out_specs=(rows, pair, down),
        check_vma=False,
    )
```

```python
import functools

import jax
import jax.numpy as jnp
from jax import lax
from jax.experimental import pallas as pl
from jax.experimental.pallas import tpu as pltpu
from jax.sharding import PartitionSpec as P

CAP = 2
HALVES = 2
MIB = 1024 * 1024
VMEM = pl.BlockSpec(memory_space=pltpu.VMEM)
HBM = pl.BlockSpec(memory_space=pltpu.HBM)


def dot_nn(a, b):
    return lax.dot_general(a, b, (((1,), (0,)), ((), ())), preferred_element_type=jnp.float32)


def dot_nt(a, b):
    return lax.dot_general(a, b, (((1,), (1,)), ((), ())), preferred_element_type=jnp.float32)


def dot_tn(a, b):
    return lax.dot_general(a, b, (((0,), (0,)), ((), ())), preferred_element_type=jnp.float32)


def cost(flops, moved):
    return pl.CostEstimate(flops=int(flops), bytes_accessed=int(moved), transcendentals=0)


def params(mib):
    return pltpu.CompilerParams(vmem_limit_bytes=mib * MIB)


def in_hbm(value):
    return pltpu.with_memory_space_constraint(value, pltpu.HBM)


def bf16(*shape):
    return jax.ShapeDtypeStruct(shape, jnp.bfloat16)


def factors(experts):
    far = 1
    while 4 * far * far <= experts:
        far *= 2
    return far, experts // far


def route_kernel(experts, chunk, ids_hbm, probs_hbm, act_hbm, cot_hbm, *refs):
    far, near = factors(experts)
    sends, place_ref = refs[:far], refs[far]
    ids_ref, probs_ref, act, cot, sems = refs[far + 1 :]
    tokens, width = act.shape
    steps = width // chunk
    small = (
        pltpu.make_async_copy(ids_hbm, ids_ref, sems.at[2 * steps]),
        pltpu.make_async_copy(probs_hbm, probs_ref, sems.at[2 * steps + 1]),
    )
    large = []
    for step in range(steps):
        at = pl.ds(step * chunk, chunk)
        large.append(
            (
                pltpu.make_async_copy(act_hbm.at[:, at], act.at[:, at], sems.at[2 * step]),
                pltpu.make_async_copy(cot_hbm.at[:, at], cot.at[:, at], sems.at[2 * step + 1]),
            )
        )
    for one in small:
        one.start()
    for pair in large:
        for one in pair:
            one.start()
    for one in small:
        one.wait()

    me = lax.axis_index("expert")
    ids = ids_ref[...]
    inside = ids < experts
    units = lax.broadcasted_iota(jnp.int32, (experts, tokens), 0)
    onehot = jnp.where(units == ids, 1.0, 0.0)
    earlier = lax.broadcasted_iota(jnp.int32, (tokens, tokens), 0) < lax.broadcasted_iota(
        jnp.int32, (tokens, tokens), 1
    )
    before = dot_nn(onehot.astype(jnp.bfloat16), jnp.where(earlier, 1.0, 0.0).astype(jnp.bfloat16))
    rank = jnp.sum(before * onehot, axis=0, keepdims=True).astype(jnp.int32)
    slots = lax.broadcasted_iota(jnp.int32, (experts * CAP, tokens), 0)
    slot = jnp.where(inside, ids * CAP + rank, -1)
    place_ref[...] = jnp.where(slots == slot, 1.0, 0.0).astype(jnp.bfloat16)
    turned = jnp.where(inside, (ids ^ me) * CAP + rank, -1)
    pick = jnp.where(slots == turned, 1.0, 0.0)
    weight = jnp.sum(pick * probs_ref[...], axis=1, keepdims=True)
    pick = pick.astype(jnp.bfloat16)
    for step in range(steps):
        at = slice(step * chunk, (step + 1) * chunk)
        for one in large[step]:
            one.wait()
        rows_tok = dot_nn(pick, act[:, at]).astype(jnp.bfloat16)
        rows_cot = (weight * dot_nn(pick, cot[:, at])).astype(jnp.bfloat16)
        for unit in range(experts):
            rows = slice(unit * CAP, (unit + 1) * CAP)
            sends[unit // near][unit % near, :CAP, at] = rows_tok[rows]
            sends[unit // near][unit % near, CAP:, at] = rows_cot[rows]


def route(ids, probs, act, cot, experts):
    tokens, width = act.shape
    chunk = min(1024, width)
    far, near = factors(experts)
    out = pl.pallas_call(
        functools.partial(route_kernel, experts, chunk),
        in_specs=[HBM] * 4,
        out_specs=[VMEM] * (far + 1),
        out_shape=[bf16(near, 2 * CAP, width)] * far + [bf16(experts * CAP, tokens)],
        scratch_shapes=[
            pltpu.VMEM((1, tokens), jnp.int32),
            pltpu.VMEM((1, tokens), jnp.float32),
            pltpu.VMEM((tokens, width), jnp.bfloat16),
            pltpu.VMEM((tokens, width), jnp.bfloat16),
            pltpu.SemaphoreType.DMA((2 * (width // chunk) + 2,)),
        ],
        compiler_params=params(16),
        cost_estimate=cost(4 * experts * CAP * tokens * width, 4 * tokens * width),
        name="route_rows",
    )(in_hbm(ids), in_hbm(probs), in_hbm(act), in_hbm(cot))
    return out[:far], out[far]


def merge_kernel(far, *refs):
    pieces, outs = refs[:far], refs[len(refs) - refs[0].shape[0] :]
    for index, out in enumerate(outs):
        rows = [piece[index, :CAP, :] for piece in pieces]
        rows += [piece[index, CAP:, :] for piece in pieces]
        out[...] = jnp.concatenate(rows, axis=0)


def merge(pieces, after=()):
    far = len(pieces)
    near, _, width = pieces[0].shape
    return pl.pallas_call(
        functools.partial(merge_kernel, far),
        in_specs=[VMEM] * far + [pl.BlockSpec(memory_space=pl.ANY)] * len(after),
        out_specs=[VMEM] * near,
        out_shape=[bf16(2 * CAP * far, width)] * near,
        compiler_params=params(16),
        cost_estimate=cost(0, 8 * near * CAP * far * width),
        name="merge_rows",
    )(*pieces, *after)


def stack_kernel(number, *refs):
    pieces, outs = refs[:number], refs[number:]
    rows, width = pieces[0].shape[0] // 2, outs[0].shape[1]
    for half, out in enumerate(outs):
        at = slice(half * width, (half + 1) * width)
        picked = [piece[:rows, at] for piece in pieces] + [piece[rows:, at] for piece in pieces]
        out[...] = jnp.concatenate(picked, axis=0)


def stack(pieces):
    number = len(pieces)
    rows, width = pieces[0].shape
    return pl.pallas_call(
        functools.partial(stack_kernel, number),
        in_specs=[VMEM] * number,
        out_specs=[VMEM] * HALVES,
        out_shape=[bf16(number * rows, width // HALVES)] * HALVES,
        compiler_params=params(16),
        cost_estimate=cost(0, 4 * number * rows * width),
        name="stack_rows",
    )(*pieces)


def load_kernel(chunk, pair_hbm, down_hbm, after, pair, down, sems):
    del after
    width = down.shape[1]
    copies = []
    for step in range(width // chunk):
        at = pl.ds(step * chunk, chunk)
        copies += [
            pltpu.make_async_copy(pair_hbm.at[:, at, :], pair.at[:, at, :], sems.at[0, step]),
            pltpu.make_async_copy(down_hbm.at[:, at], down.at[:, at], sems.at[1, step]),
        ]
    for one in copies:
        one.start()
    for one in copies:
        one.wait()


def load(pair, down, after):
    units, width = down.shape
    chunk = min(1024, width)
    return pl.pallas_call(
        functools.partial(load_kernel, chunk),
        in_specs=[HBM] * 2 + [pl.BlockSpec(memory_space=pl.ANY)],
        out_specs=[VMEM] * 2,
        out_shape=[pltpu.VMEM(pair.shape, jnp.bfloat16), pltpu.VMEM(down.shape, jnp.bfloat16)],
        scratch_shapes=[pltpu.SemaphoreType.DMA((2, width // chunk))],
        compiler_params=params(28),
        cost_estimate=cost(0, 6 * width * units),
        name="load_weights",
    )(in_hbm(pair), in_hbm(down), after)


def gather_columns(near_rows, far_rows, near_at, far_at):
    pieces = [(ref, near_at) for ref in near_rows] + [(ref, far_at) for ref in far_rows]
    tok = [ref[: ref.shape[0] // 2, at] for ref, at in pieces]
    cot = [ref[ref.shape[0] // 2 :, at] for ref, at in pieces]
    return jnp.concatenate(tok, axis=0), jnp.concatenate(cot, axis=0)


def first_kernel(near, groups, chunk, *refs):
    near_rows, far_rows = refs[:near], refs[near : near + groups]
    pair, down, gate, up, hid, tok_all, cot_all = refs[near + groups :]
    for step in range(tok_all.shape[1] // chunk):
        at = slice(step * chunk, (step + 1) * chunk)
        tok, cot = gather_columns(near_rows, far_rows, at, at)
        tok_all[:, at] = tok
        cot_all[:, at] = cot
        part_gate = dot_nn(tok, pair[0, at, :])
        part_up = dot_nn(tok, pair[1, at, :])
        part_hid = dot_nt(cot, down[:, at])
        if step == 0:
            gate[...], up[...], hid[...] = part_gate, part_up, part_hid
        else:
            gate[...] += part_gate
            up[...] += part_up
            hid[...] += part_hid


def first_half(near_rows, far_rows, pair, down):
    near, groups = len(near_rows), len(far_rows)
    total = (near * near_rows[0].shape[0] + groups * far_rows[0].shape[0]) // 2
    half = far_rows[0].shape[1]
    units = down.shape[0]
    chunk = half
    return pl.pallas_call(
        functools.partial(first_kernel, near, groups, chunk),
        in_specs=[VMEM] * (near + groups + 2),
        out_specs=[VMEM] * 5,
        out_shape=[jax.ShapeDtypeStruct((total, units), jnp.float32)] * 3
        + [bf16(total, half)] * 2,
        compiler_params=params(24),
        cost_estimate=cost(6 * total * half * units, 6 * half * units),
        name="first_half",
    )(*near_rows, *far_rows, pair, down)


def second_kernel(homes, experts, near, groups, chunk, *refs):
    near_rows, far_rows = refs[:near], refs[near : near + groups]
    gate_sum, up_sum, hid_sum, pair, down = refs[near + groups : near + groups + 5]
    gate_out, up_out, hidden_out, tok_all, cot_all, parts_hbm = refs[
        near + groups + 5 : near + groups + 11
    ]
    parts, sems = refs[near + groups + 11 :]
    half, width = tok_all.shape[1], down.shape[1]
    there = slice(half, width)
    tok, cot = gather_columns(near_rows, far_rows, there, slice(0, half))
    tok_all[...] = tok
    cot_all[...] = cot
    pre_gate = gate_sum[...] + dot_nn(tok, pair[0, there, :])
    pre_up = up_sum[...] + dot_nn(tok, pair[1, there, :])
    hidden_grad = hid_sum[...] + dot_nt(cot, down[:, there])
    sigmoid_gate = jax.nn.sigmoid(pre_gate)
    activated = pre_gate * sigmoid_gate
    hidden_out[...] = (activated * pre_up).astype(jnp.bfloat16)
    gate_grad = (
        hidden_grad * pre_up * sigmoid_gate * (1.0 + pre_gate * (1.0 - sigmoid_gate))
    ).astype(jnp.bfloat16)
    up_grad = (hidden_grad * activated).astype(jnp.bfloat16)
    gate_out[...] = gate_grad
    up_out[...] = up_grad
    me, group = lax.axis_index("expert"), lax.axis_index("dp")
    rows = [
        lax.rem(group - back + groups, groups) * experts + (me ^ turn) for back, turn in homes
    ]
    copies = []
    for step in range(width // chunk):
        at = slice(step * chunk, (step + 1) * chunk)
        value = dot_nt(gate_grad, pair[0, at, :]) + dot_nt(up_grad, pair[1, at, :])
        value = value.astype(jnp.bfloat16)
        for block, row in enumerate(rows):
            parts[row, :, at] = value[block * CAP : (block + 1) * CAP]
        where = pl.ds(step * chunk, chunk)
        one = pltpu.make_async_copy(
            parts.at[:, :, where], parts_hbm.at[:, :, where], sems.at[step]
        )
        one.start()
        copies.append(one)
    for one in copies:
        one.wait()


def second_half(near_rows, far_rows, sums, pair, down, homes, experts):
    near, groups = len(near_rows), len(far_rows)
    total, units = sums[0].shape
    half, width = far_rows[0].shape[1], down.shape[1]
    chunk = min(512, half)
    blocks = total // CAP
    return pl.pallas_call(
        functools.partial(second_kernel, homes, experts, near, groups, chunk),
        in_specs=[VMEM] * (near + groups + 5),
        out_specs=[VMEM] * 5 + [HBM],
        out_shape=[bf16(total, units)] * 3
        + [bf16(total, half)] * 2
        + [pltpu.HBM((blocks, CAP, width), jnp.bfloat16)],
        scratch_shapes=[
            pltpu.VMEM((blocks, CAP, width), jnp.bfloat16),
            pltpu.SemaphoreType.DMA((width // chunk,)),
        ],
        compiler_params=params(24),
        cost_estimate=cost(7 * total * width * units, 6 * width * units),
        name="second_half",
    )(*near_rows, *far_rows, *sums, pair, down)


def pair_grad_kernel(blocks, chunk, *refs):
    toks, gate_ref, up_ref = refs[:blocks], refs[blocks], refs[blocks + 1]
    half = toks[0].shape[1]
    out_hbm, buffer, sems = refs[blocks + 2 :]
    copies = []
    for step in range(blocks * half // chunk):
        at = slice(step * chunk, (step + 1) * chunk)
        tok = toks[step * chunk // half][:, step * chunk % half : step * chunk % half + chunk]
        for side, ref in enumerate((gate_ref, up_ref)):
            buffer[side, at, :] = dot_tn(tok, ref[...]).astype(jnp.bfloat16)
        where = pl.ds(step * chunk, chunk)
        one = pltpu.make_async_copy(
            buffer.at[:, where, :], out_hbm.at[0, :, where, :], sems.at[step]
        )
        one.start()
        copies.append(one)
    for one in copies:
        one.wait()


def pair_grad(toks, gate_grad, up_grad):
    blocks = len(toks)
    width = blocks * toks[0].shape[1]
    total, units = gate_grad.shape
    chunk = min(512, width // blocks)
    return pl.pallas_call(
        functools.partial(pair_grad_kernel, blocks, chunk),
        in_specs=[VMEM] * (blocks + 2),
        out_specs=HBM,
        out_shape=bf16(1, 2, width, units),
        scratch_shapes=[
            pltpu.VMEM((2, width, units), jnp.bfloat16),
            pltpu.SemaphoreType.DMA((width // chunk,)),
        ],
        compiler_params=params(32),
        cost_estimate=cost(4 * total * width * units, 4 * width * units),
        name="pair_grad",
    )(*toks, gate_grad, up_grad)


def down_grad_kernel(blocks, chunk, *refs):
    cots, hidden_ref, out_hbm = refs[:blocks], refs[blocks], refs[blocks + 1]
    buffer, sems = refs[blocks + 2 :]
    half = cots[0].shape[1]
    copies = []
    for step in range(blocks * half // chunk):
        at = slice(step * chunk, (step + 1) * chunk)
        cot = cots[step * chunk // half][:, step * chunk % half : step * chunk % half + chunk]
        buffer[:, at] = dot_tn(hidden_ref[...], cot).astype(jnp.bfloat16)
        where = pl.ds(step * chunk, chunk)
        one = pltpu.make_async_copy(buffer.at[:, where], out_hbm.at[0, :, where], sems.at[step])
        one.start()
        copies.append(one)
    for one in copies:
        one.wait()


def down_grad(cots, hidden):
    blocks = len(cots)
    width = blocks * cots[0].shape[1]
    total, units = hidden.shape
    chunk = min(1024, width // blocks)
    return pl.pallas_call(
        functools.partial(down_grad_kernel, blocks, chunk),
        in_specs=[VMEM] * (blocks + 1),
        out_specs=HBM,
        out_shape=bf16(1, units, width),
        scratch_shapes=[
            pltpu.VMEM((units, width), jnp.bfloat16),
            pltpu.SemaphoreType.DMA((width // chunk,)),
        ],
        compiler_params=params(24),
        cost_estimate=cost(2 * total * width * units, 2 * width * units),
        name="down_grad",
    )(*cots, hidden)


def spread_kernel(chunk, rows_ref, place_ref, out_hbm, buffer, sems):
    blocks, _, width = rows_ref.shape
    place = jnp.concatenate([place_ref[...]] * (blocks * CAP // place_ref.shape[0]), axis=0)
    copies = []
    for step in range(width // chunk):
        at = slice(step * chunk, (step + 1) * chunk)
        rows = jnp.concatenate([rows_ref[block, :, at] for block in range(blocks)], axis=0)
        buffer[:, at] = dot_tn(place, rows).astype(jnp.bfloat16)
        where = pl.ds(step * chunk, chunk)
        one = pltpu.make_async_copy(buffer.at[:, where], out_hbm.at[:, where], sems.at[step])
        one.start()
        copies.append(one)
    for one in copies:
        one.wait()


def spread(rows, place):
    width = rows.shape[2]
    slots, tokens = place.shape
    chunk = min(1024, width)
    return pl.pallas_call(
        functools.partial(spread_kernel, chunk),
        in_specs=[VMEM] * 2,
        out_specs=HBM,
        out_shape=bf16(tokens, width),
        scratch_shapes=[
            pltpu.VMEM((tokens, width), jnp.bfloat16),
            pltpu.SemaphoreType.DMA((width // chunk,)),
        ],
        compiler_params=params(16),
        cost_estimate=cost(2 * slots * tokens * width, 2 * tokens * width),
        name="spread_rows",
    )(rows, place)


def per_device(activations, cotangent, expert_ids, gate_probs, gate_up, down_proj):
    experts = lax.axis_size("expert")
    groups = lax.axis_size("dp")
    tokens = activations.shape[0]
    far, near = factors(experts)

    def send(value, by_group, by_expert):
        if by_group == 0 and by_expert == 0:
            return value
        pairs = []
        for group in range(groups):
            to = (group + by_group) % groups
            for i in range(experts):
                pairs.append((group * experts + i, to * experts + (i ^ by_expert)))
        return lax.ppermute(value, ("dp", "expert"), pairs)

    pieces, place = route(
        expert_ids.reshape(1, tokens),
        gate_probs.reshape(1, tokens),
        activations,
        cotangent,
        experts,
    )
    pair, down = load(gate_up[0], down_proj[0], place)
    arrived = [send(pieces[high], 0, high * near) for high in range(far)]
    early, late = range(far // 2), range(far // 2, far)
    first = [send(pieces[high], group, high * near) for group in range(1, groups) for high in early]
    first = merge([arrived[high] for high in early] + first)
    loaded = pltpu.with_memory_space_constraint(down, pltpu.VMEM)
    second = merge([arrived[high] for high in late], (loaded,))
    order = [0] + list(range(near - 1, 0, -1))
    mine = [send(second[low], 0, low) for low in order]
    halves = stack(mine)
    near_rows = [send(first[low], 0, low) for low in order]
    far_rows = [[send(half, group, 0) for group in range(groups)] for half in halves]
    homes = [
        (group, high * near + low)
        for low in order
        for group in range(groups)
        for high in early
    ]
    homes += [
        (group, high * near + low)
        for group in range(groups)
        for low in order
        for high in late
    ]
    pair = pltpu.with_memory_space_constraint(pair, pltpu.VMEM)
    *sums, tok_first, cot_first = first_half(near_rows, far_rows[0], pair, loaded)
    gate_grad, up_grad, hidden, tok_second, cot_second, parts = second_half(
        near_rows, far_rows[1], sums, pair, loaded, homes, experts
    )
    returned = lax.all_to_all(parts, ("dp", "expert"), split_axis=0, concat_axis=0, tiled=True)
    down_total = down_grad([cot_first, cot_second], hidden)
    pair_total = pair_grad([tok_first, tok_second], gate_grad, up_grad)
    input_grad = spread(returned, place)
    return input_grad, pair_total, down_total


def solution(mesh):
    rows = P(("dp", "expert"), None)
    pair, down = P("expert", None, None, "dp"), P("expert", "dp", None)
    return jax.shard_map(
        per_device,
        mesh=mesh,
        in_specs=(rows, rows, rows, rows, pair, down),
        out_specs=(rows, pair, down),
        check_vma=False,
    )
```

```python
import functools

import jax
import jax.numpy as jnp
from jax import lax
from jax.experimental import pallas as pl
from jax.experimental.pallas import tpu as pltpu
from jax.sharding import PartitionSpec as P

CAP = 2
HALVES = 2
MIB = 1024 * 1024
VMEM = pl.BlockSpec(memory_space=pltpu.VMEM)
HBM = pl.BlockSpec(memory_space=pltpu.HBM)


def dot_nn(a, b):
    return lax.dot_general(a, b, (((1,), (0,)), ((), ())), preferred_element_type=jnp.float32)


def dot_nt(a, b):
    return lax.dot_general(a, b, (((1,), (1,)), ((), ())), preferred_element_type=jnp.float32)


def dot_tn(a, b):
    return lax.dot_general(a, b, (((0,), (0,)), ((), ())), preferred_element_type=jnp.float32)


def cost(flops, moved):
    return pl.CostEstimate(flops=int(flops), bytes_accessed=int(moved), transcendentals=0)


def params(mib):
    return pltpu.CompilerParams(vmem_limit_bytes=mib * MIB)


def in_hbm(value):
    return pltpu.with_memory_space_constraint(value, pltpu.HBM)


def bf16(*shape):
    return jax.ShapeDtypeStruct(shape, jnp.bfloat16)


def factors(experts):
    far = 1
    while 4 * far * far <= experts:
        far *= 2
    return far, experts // far


def route_kernel(experts, chunk, ids_hbm, probs_hbm, act_hbm, cot_hbm, *refs):
    far, near = factors(experts)
    sends, place_ref = refs[:far], refs[far]
    ids_ref, probs_ref, act, cot, sems = refs[far + 1 :]
    tokens, width = act.shape
    steps = width // chunk
    small = (
        pltpu.make_async_copy(ids_hbm, ids_ref, sems.at[2 * steps]),
        pltpu.make_async_copy(probs_hbm, probs_ref, sems.at[2 * steps + 1]),
    )
    large = []
    for step in range(steps):
        at = pl.ds(step * chunk, chunk)
        large.append(
            (
                pltpu.make_async_copy(act_hbm.at[:, at], act.at[:, at], sems.at[2 * step]),
                pltpu.make_async_copy(cot_hbm.at[:, at], cot.at[:, at], sems.at[2 * step + 1]),
            )
        )
    for one in small:
        one.start()
    for pair in large:
        for one in pair:
            one.start()
    for one in small:
        one.wait()

    me = lax.axis_index("expert")
    ids = ids_ref[...]
    inside = ids < experts
    units = lax.broadcasted_iota(jnp.int32, (experts, tokens), 0)
    onehot = jnp.where(units == ids, 1.0, 0.0)
    earlier = lax.broadcasted_iota(jnp.int32, (tokens, tokens), 0) < lax.broadcasted_iota(
        jnp.int32, (tokens, tokens), 1
    )
    before = dot_nn(onehot.astype(jnp.bfloat16), jnp.where(earlier, 1.0, 0.0).astype(jnp.bfloat16))
    rank = jnp.sum(before * onehot, axis=0, keepdims=True).astype(jnp.int32)
    slots = lax.broadcasted_iota(jnp.int32, (experts * CAP, tokens), 0)
    slot = jnp.where(inside, ids * CAP + rank, -1)
    place_ref[...] = jnp.where(slots == slot, 1.0, 0.0).astype(jnp.bfloat16)
    turned = jnp.where(inside, (ids ^ me) * CAP + rank, -1)
    pick = jnp.where(slots == turned, 1.0, 0.0)
    weight = jnp.sum(pick * probs_ref[...], axis=1, keepdims=True)
    pick = pick.astype(jnp.bfloat16)
    for step in range(steps):
        at = slice(step * chunk, (step + 1) * chunk)
        for one in large[step]:
            one.wait()
        rows_tok = dot_nn(pick, act[:, at]).astype(jnp.bfloat16)
        rows_cot = (weight * dot_nn(pick, cot[:, at])).astype(jnp.bfloat16)
        for unit in range(experts):
            rows = slice(unit * CAP, (unit + 1) * CAP)
            sends[unit // near][unit % near, :CAP, at] = rows_tok[rows]
            sends[unit // near][unit % near, CAP:, at] = rows_cot[rows]


def route(ids, probs, act, cot, experts):
    tokens, width = act.shape
    chunk = min(1024, width)
    far, near = factors(experts)
    out = pl.pallas_call(
        functools.partial(route_kernel, experts, chunk),
        in_specs=[HBM] * 4,
        out_specs=[VMEM] * (far + 1),
        out_shape=[bf16(near, 2 * CAP, width)] * far + [bf16(experts * CAP, tokens)],
        scratch_shapes=[
            pltpu.VMEM((1, tokens), jnp.int32),
            pltpu.VMEM((1, tokens), jnp.float32),
            pltpu.VMEM((tokens, width), jnp.bfloat16),
            pltpu.VMEM((tokens, width), jnp.bfloat16),
            pltpu.SemaphoreType.DMA((2 * (width // chunk) + 2,)),
        ],
        compiler_params=params(16),
        cost_estimate=cost(4 * experts * CAP * tokens * width, 4 * tokens * width),
        name="route_rows",
    )(in_hbm(ids), in_hbm(probs), in_hbm(act), in_hbm(cot))
    return out[:far], out[far]


def merge_kernel(far, *refs):
    pieces, outs = refs[:far], refs[len(refs) - refs[0].shape[0] :]
    for index, out in enumerate(outs):
        rows = [piece[index, :CAP, :] for piece in pieces]
        rows += [piece[index, CAP:, :] for piece in pieces]
        out[...] = jnp.concatenate(rows, axis=0)


def merge(pieces, after=()):
    far = len(pieces)
    near, _, width = pieces[0].shape
    return pl.pallas_call(
        functools.partial(merge_kernel, far),
        in_specs=[VMEM] * far + [pl.BlockSpec(memory_space=pl.ANY)] * len(after),
        out_specs=[VMEM] * near,
        out_shape=[bf16(2 * CAP * far, width)] * near,
        compiler_params=params(16),
        cost_estimate=cost(0, 8 * near * CAP * far * width),
        name="merge_rows",
    )(*pieces, *after)


def stack_kernel(number, *refs):
    pieces, outs = refs[:number], refs[number:]
    rows, width = pieces[0].shape[0] // 2, outs[0].shape[1]
    for half, out in enumerate(outs):
        at = slice(half * width, (half + 1) * width)
        picked = [piece[:rows, at] for piece in pieces] + [piece[rows:, at] for piece in pieces]
        out[...] = jnp.concatenate(picked, axis=0)


def stack(pieces):
    number = len(pieces)
    rows, width = pieces[0].shape
    return pl.pallas_call(
        functools.partial(stack_kernel, number),
        in_specs=[VMEM] * number,
        out_specs=[VMEM] * HALVES,
        out_shape=[bf16(number * rows, width // HALVES)] * HALVES,
        compiler_params=params(16),
        cost_estimate=cost(0, 4 * number * rows * width),
        name="stack_rows",
    )(*pieces)


def load_kernel(chunk, pair_hbm, down_hbm, after, pair, down, sems):
    del after
    width = down.shape[1]
    copies = []
    for step in range(width // chunk):
        at = pl.ds(step * chunk, chunk)
        copies += [
            pltpu.make_async_copy(pair_hbm.at[:, at, :], pair.at[:, at, :], sems.at[0, step]),
            pltpu.make_async_copy(down_hbm.at[:, at], down.at[:, at], sems.at[1, step]),
        ]
    for one in copies:
        one.start()
    for one in copies:
        one.wait()


def load(pair, down, after):
    units, width = down.shape
    chunk = min(1024, width)
    return pl.pallas_call(
        functools.partial(load_kernel, chunk),
        in_specs=[HBM] * 2 + [pl.BlockSpec(memory_space=pl.ANY)],
        out_specs=[VMEM] * 2,
        out_shape=[pltpu.VMEM(pair.shape, jnp.bfloat16), pltpu.VMEM(down.shape, jnp.bfloat16)],
        scratch_shapes=[pltpu.SemaphoreType.DMA((2, width // chunk))],
        compiler_params=params(28),
        cost_estimate=cost(0, 6 * width * units),
        name="load_weights",
    )(in_hbm(pair), in_hbm(down), after)


def gather_columns(near_rows, far_rows, near_at, far_at):
    pieces = [(ref, near_at) for ref in near_rows] + [(ref, far_at) for ref in far_rows]
    tok = [ref[: ref.shape[0] // 2, at] for ref, at in pieces]
    cot = [ref[ref.shape[0] // 2 :, at] for ref, at in pieces]
    return jnp.concatenate(tok, axis=0), jnp.concatenate(cot, axis=0)


def first_kernel(near, groups, chunk, *refs):
    near_rows, far_rows = refs[:near], refs[near : near + groups]
    pair, down, gate, up, hid, tok_all, cot_all = refs[near + groups :]
    for step in range(tok_all.shape[1] // chunk):
        at = slice(step * chunk, (step + 1) * chunk)
        tok, cot = gather_columns(near_rows, far_rows, at, at)
        tok_all[:, at] = tok
        cot_all[:, at] = cot
        part_gate = dot_nn(tok, pair[0, at, :])
        part_up = dot_nn(tok, pair[1, at, :])
        part_hid = dot_nt(cot, down[:, at])
        if step == 0:
            gate[...], up[...], hid[...] = part_gate, part_up, part_hid
        else:
            gate[...] += part_gate
            up[...] += part_up
            hid[...] += part_hid


def first_half(near_rows, far_rows, pair, down):
    near, groups = len(near_rows), len(far_rows)
    total = (near * near_rows[0].shape[0] + groups * far_rows[0].shape[0]) // 2
    half = far_rows[0].shape[1]
    units = down.shape[0]
    chunk = half
    return pl.pallas_call(
        functools.partial(first_kernel, near, groups, chunk),
        in_specs=[VMEM] * (near + groups + 2),
        out_specs=[VMEM] * 5,
        out_shape=[jax.ShapeDtypeStruct((total, units), jnp.float32)] * 3
        + [bf16(total, half)] * 2,
        compiler_params=params(24),
        cost_estimate=cost(6 * total * half * units, 6 * half * units),
        name="first_half",
    )(*near_rows, *far_rows, pair, down)


def second_kernel(homes, experts, near, groups, chunk, *refs):
    near_rows, far_rows = refs[:near], refs[near : near + groups]
    gate_sum, up_sum, hid_sum, pair, down = refs[near + groups : near + groups + 5]
    gate_out, up_out, hidden_out, tok_all, cot_all, parts_hbm = refs[
        near + groups + 5 : near + groups + 11
    ]
    parts, sems = refs[near + groups + 11 :]
    half, width = tok_all.shape[1], down.shape[1]
    there = slice(half, width)
    tok, cot = gather_columns(near_rows, far_rows, there, slice(0, half))
    tok_all[...] = tok
    cot_all[...] = cot
    units = down.shape[0]
    tile = 256 if units % 256 == 0 else units
    for start in range(0, units, tile):
        unit = slice(start, start + tile)
        pre_gate = gate_sum[:, unit] + dot_nn(tok, pair[0, there, unit])
        pre_up = up_sum[:, unit] + dot_nn(tok, pair[1, there, unit])
        hidden_grad = hid_sum[:, unit] + dot_nt(cot, down[unit, there])
        sigmoid_gate = jax.nn.sigmoid(pre_gate)
        activated = pre_gate * sigmoid_gate
        hidden_out[:, unit] = (activated * pre_up).astype(jnp.bfloat16)
        gate_out[:, unit] = (
            hidden_grad * pre_up * sigmoid_gate * (1.0 + pre_gate * (1.0 - sigmoid_gate))
        ).astype(jnp.bfloat16)
        up_out[:, unit] = (hidden_grad * activated).astype(jnp.bfloat16)
    gate_grad, up_grad = gate_out[...], up_out[...]
    me, group = lax.axis_index("expert"), lax.axis_index("dp")
    rows = [
        lax.rem(group - back + groups, groups) * experts + (me ^ turn) for back, turn in homes
    ]
    copies = []
    for step in range(width // chunk):
        at = slice(step * chunk, (step + 1) * chunk)
        value = dot_nt(gate_grad, pair[0, at, :]) + dot_nt(up_grad, pair[1, at, :])
        value = value.astype(jnp.bfloat16)
        for block, row in enumerate(rows):
            parts[row, :, at] = value[block * CAP : (block + 1) * CAP]
        where = pl.ds(step * chunk, chunk)
        one = pltpu.make_async_copy(
            parts.at[:, :, where], parts_hbm.at[:, :, where], sems.at[step]
        )
        one.start()
        copies.append(one)
    for one in copies:
        one.wait()


def second_half(near_rows, far_rows, sums, pair, down, homes, experts):
    near, groups = len(near_rows), len(far_rows)
    total, units = sums[0].shape
    half, width = far_rows[0].shape[1], down.shape[1]
    chunk = min(512, half)
    blocks = total // CAP
    return pl.pallas_call(
        functools.partial(second_kernel, homes, experts, near, groups, chunk),
        in_specs=[VMEM] * (near + groups + 5),
        out_specs=[VMEM] * 5 + [HBM],
        out_shape=[bf16(total, units)] * 3
        + [bf16(total, half)] * 2
        + [pltpu.HBM((blocks, CAP, width), jnp.bfloat16)],
        scratch_shapes=[
            pltpu.VMEM((blocks, CAP, width), jnp.bfloat16),
            pltpu.SemaphoreType.DMA((width // chunk,)),
        ],
        compiler_params=params(24),
        cost_estimate=cost(7 * total * width * units, 6 * width * units),
        name="second_half",
    )(*near_rows, *far_rows, *sums, pair, down)


def pair_grad_kernel(blocks, chunk, *refs):
    toks, gate_ref, up_ref = refs[:blocks], refs[blocks], refs[blocks + 1]
    half = toks[0].shape[1]
    out_hbm, buffer, sems = refs[blocks + 2 :]
    copies = []
    for step in range(blocks * half // chunk):
        at = slice(step * chunk, (step + 1) * chunk)
        tok = toks[step * chunk // half][:, step * chunk % half : step * chunk % half + chunk]
        for side, ref in enumerate((gate_ref, up_ref)):
            buffer[side, at, :] = dot_tn(tok, ref[...]).astype(jnp.bfloat16)
        where = pl.ds(step * chunk, chunk)
        one = pltpu.make_async_copy(
            buffer.at[:, where, :], out_hbm.at[0, :, where, :], sems.at[step]
        )
        one.start()
        copies.append(one)
    for one in copies:
        one.wait()


def pair_grad(toks, gate_grad, up_grad):
    blocks = len(toks)
    width = blocks * toks[0].shape[1]
    total, units = gate_grad.shape
    chunk = min(512, width // blocks)
    return pl.pallas_call(
        functools.partial(pair_grad_kernel, blocks, chunk),
        in_specs=[VMEM] * (blocks + 2),
        out_specs=HBM,
        out_shape=bf16(1, 2, width, units),
        scratch_shapes=[
            pltpu.VMEM((2, width, units), jnp.bfloat16),
            pltpu.SemaphoreType.DMA((width // chunk,)),
        ],
        compiler_params=params(32),
        cost_estimate=cost(4 * total * width * units, 4 * width * units),
        name="pair_grad",
    )(*toks, gate_grad, up_grad)


def down_grad_kernel(blocks, chunk, *refs):
    cots, hidden_ref, out_hbm = refs[:blocks], refs[blocks], refs[blocks + 1]
    buffer, sems = refs[blocks + 2 :]
    half = cots[0].shape[1]
    copies = []
    for step in range(blocks * half // chunk):
        at = slice(step * chunk, (step + 1) * chunk)
        cot = cots[step * chunk // half][:, step * chunk % half : step * chunk % half + chunk]
        buffer[:, at] = dot_tn(hidden_ref[...], cot).astype(jnp.bfloat16)
        where = pl.ds(step * chunk, chunk)
        one = pltpu.make_async_copy(buffer.at[:, where], out_hbm.at[0, :, where], sems.at[step])
        one.start()
        copies.append(one)
    for one in copies:
        one.wait()


def down_grad(cots, hidden):
    blocks = len(cots)
    width = blocks * cots[0].shape[1]
    total, units = hidden.shape
    chunk = min(1024, width // blocks)
    return pl.pallas_call(
        functools.partial(down_grad_kernel, blocks, chunk),
        in_specs=[VMEM] * (blocks + 1),
        out_specs=HBM,
        out_shape=bf16(1, units, width),
        scratch_shapes=[
            pltpu.VMEM((units, width), jnp.bfloat16),
            pltpu.SemaphoreType.DMA((width // chunk,)),
        ],
        compiler_params=params(24),
        cost_estimate=cost(2 * total * width * units, 2 * width * units),
        name="down_grad",
    )(*cots, hidden)


def spread_kernel(chunk, rows_ref, place_ref, out_hbm, buffer, sems):
    blocks, _, width = rows_ref.shape
    place = jnp.concatenate([place_ref[...]] * (blocks * CAP // place_ref.shape[0]), axis=0)
    copies = []
    for step in range(width // chunk):
        at = slice(step * chunk, (step + 1) * chunk)
        rows = jnp.concatenate([rows_ref[block, :, at] for block in range(blocks)], axis=0)
        buffer[:, at] = dot_tn(place, rows).astype(jnp.bfloat16)
        where = pl.ds(step * chunk, chunk)
        one = pltpu.make_async_copy(buffer.at[:, where], out_hbm.at[:, where], sems.at[step])
        one.start()
        copies.append(one)
    for one in copies:
        one.wait()


def spread(rows, place):
    width = rows.shape[2]
    slots, tokens = place.shape
    chunk = min(1024, width)
    return pl.pallas_call(
        functools.partial(spread_kernel, chunk),
        in_specs=[VMEM] * 2,
        out_specs=HBM,
        out_shape=bf16(tokens, width),
        scratch_shapes=[
            pltpu.VMEM((tokens, width), jnp.bfloat16),
            pltpu.SemaphoreType.DMA((width // chunk,)),
        ],
        compiler_params=params(16),
        cost_estimate=cost(2 * slots * tokens * width, 2 * tokens * width),
        name="spread_rows",
    )(rows, place)


def per_device(activations, cotangent, expert_ids, gate_probs, gate_up, down_proj):
    experts = lax.axis_size("expert")
    groups = lax.axis_size("dp")
    tokens = activations.shape[0]
    far, near = factors(experts)

    def send(value, by_group, by_expert):
        if by_group == 0 and by_expert == 0:
            return value
        pairs = []
        for group in range(groups):
            to = (group + by_group) % groups
            for i in range(experts):
                pairs.append((group * experts + i, to * experts + (i ^ by_expert)))
        return lax.ppermute(value, ("dp", "expert"), pairs)

    pieces, place = route(
        expert_ids.reshape(1, tokens),
        gate_probs.reshape(1, tokens),
        activations,
        cotangent,
        experts,
    )
    pair, down = load(gate_up[0], down_proj[0], place)
    arrived = [send(pieces[high], 0, high * near) for high in range(far)]
    early, late = range(far // 2), range(far // 2, far)
    first = [send(pieces[high], group, high * near) for group in range(1, groups) for high in early]
    first = merge([arrived[high] for high in early] + first)
    loaded = pltpu.with_memory_space_constraint(down, pltpu.VMEM)
    second = merge([arrived[high] for high in late], (loaded,))
    mine = [send(second[low], 0, low) for low in range(near)]
    halves = stack(mine)
    near_rows = [send(first[low], 0, low) for low in range(near)]
    far_rows = [[send(half, group, 0) for group in range(groups)] for half in halves]
    homes = [
        (group, high * near + low)
        for low in range(near)
        for group in range(groups)
        for high in early
    ]
    homes += [
        (group, high * near + low)
        for group in range(groups)
        for low in range(near)
        for high in late
    ]
    pair = pltpu.with_memory_space_constraint(pair, pltpu.VMEM)
    *sums, tok_first, cot_first = first_half(near_rows, far_rows[0], pair, loaded)
    gate_grad, up_grad, hidden, tok_second, cot_second, parts = second_half(
        near_rows, far_rows[1], sums, pair, loaded, homes, experts
    )
    returned = lax.all_to_all(parts, ("dp", "expert"), split_axis=0, concat_axis=0, tiled=True)
    down_total = down_grad([cot_first, cot_second], hidden)
    pair_total = pair_grad([tok_first, tok_second], gate_grad, up_grad)
    input_grad = spread(returned, place)
    return input_grad, pair_total, down_total


def solution(mesh):
    rows = P(("dp", "expert"), None)
    pair, down = P("expert", None, None, "dp"), P("expert", "dp", None)
    return jax.shard_map(
        per_device,
        mesh=mesh,
        in_specs=(rows, rows, rows, rows, pair, down),
        out_specs=(rows, pair, down),
        check_vma=False,
    )
```

```python
import functools

import jax
import jax.numpy as jnp
from jax import lax
from jax.experimental import pallas as pl
from jax.experimental.pallas import tpu as pltpu
from jax.sharding import PartitionSpec as P

CAP = 2
HALVES = 2
MIB = 1024 * 1024
VMEM = pl.BlockSpec(memory_space=pltpu.VMEM)
HBM = pl.BlockSpec(memory_space=pltpu.HBM)


def dot_nn(a, b):
    return lax.dot_general(a, b, (((1,), (0,)), ((), ())), preferred_element_type=jnp.float32)


def dot_nt(a, b):
    return lax.dot_general(a, b, (((1,), (1,)), ((), ())), preferred_element_type=jnp.float32)


def dot_tn(a, b):
    return lax.dot_general(a, b, (((0,), (0,)), ((), ())), preferred_element_type=jnp.float32)


def cost(flops, moved):
    return pl.CostEstimate(flops=int(flops), bytes_accessed=int(moved), transcendentals=0)


def params(mib):
    return pltpu.CompilerParams(vmem_limit_bytes=mib * MIB)


def in_hbm(value):
    return pltpu.with_memory_space_constraint(value, pltpu.HBM)


def bf16(*shape):
    return jax.ShapeDtypeStruct(shape, jnp.bfloat16)


def factors(experts):
    far = 1
    while 4 * far * far <= experts:
        far *= 2
    return far, experts // far


def route_kernel(experts, chunk, ids_hbm, probs_hbm, act_hbm, cot_hbm, *refs):
    far, near = factors(experts)
    sends, place_ref = refs[:far], refs[far]
    ids_ref, probs_ref, act, cot, sems = refs[far + 1 :]
    tokens, width = act.shape
    steps = width // chunk
    small = (
        pltpu.make_async_copy(ids_hbm, ids_ref, sems.at[2 * steps]),
        pltpu.make_async_copy(probs_hbm, probs_ref, sems.at[2 * steps + 1]),
    )
    large = []
    for step in range(steps):
        at = pl.ds(step * chunk, chunk)
        large.append(
            (
                pltpu.make_async_copy(act_hbm.at[:, at], act.at[:, at], sems.at[2 * step]),
                pltpu.make_async_copy(cot_hbm.at[:, at], cot.at[:, at], sems.at[2 * step + 1]),
            )
        )
    for one in small:
        one.start()
    for pair in large:
        for one in pair:
            one.start()
    for one in small:
        one.wait()

    me = lax.axis_index("expert")
    ids = ids_ref[...]
    inside = ids < experts
    units = lax.broadcasted_iota(jnp.int32, (experts, tokens), 0)
    onehot = jnp.where(units == ids, 1.0, 0.0)
    earlier = lax.broadcasted_iota(jnp.int32, (tokens, tokens), 0) < lax.broadcasted_iota(
        jnp.int32, (tokens, tokens), 1
    )
    before = dot_nn(onehot.astype(jnp.bfloat16), jnp.where(earlier, 1.0, 0.0).astype(jnp.bfloat16))
    rank = jnp.sum(before * onehot, axis=0, keepdims=True).astype(jnp.int32)
    slots = lax.broadcasted_iota(jnp.int32, (experts * CAP, tokens), 0)
    slot = jnp.where(inside, ids * CAP + rank, -1)
    place_ref[...] = jnp.where(slots == slot, 1.0, 0.0).astype(jnp.bfloat16)
    turned = jnp.where(inside, (ids ^ me) * CAP + rank, -1)
    pick = jnp.where(slots == turned, 1.0, 0.0)
    weight = jnp.sum(pick * probs_ref[...], axis=1, keepdims=True)
    pick = pick.astype(jnp.bfloat16)
    for step in range(steps):
        at = slice(step * chunk, (step + 1) * chunk)
        for one in large[step]:
            one.wait()
        rows_tok = dot_nn(pick, act[:, at]).astype(jnp.bfloat16)
        rows_cot = (weight * dot_nn(pick, cot[:, at])).astype(jnp.bfloat16)
        for unit in range(experts):
            rows = slice(unit * CAP, (unit + 1) * CAP)
            sends[unit // near][unit % near, :CAP, at] = rows_tok[rows]
            sends[unit // near][unit % near, CAP:, at] = rows_cot[rows]


def route(ids, probs, act, cot, experts):
    tokens, width = act.shape
    chunk = min(1024, width)
    far, near = factors(experts)
    out = pl.pallas_call(
        functools.partial(route_kernel, experts, chunk),
        in_specs=[HBM] * 4,
        out_specs=[VMEM] * (far + 1),
        out_shape=[bf16(near, 2 * CAP, width)] * far + [bf16(experts * CAP, tokens)],
        scratch_shapes=[
            pltpu.VMEM((1, tokens), jnp.int32),
            pltpu.VMEM((1, tokens), jnp.float32),
            pltpu.VMEM((tokens, width), jnp.bfloat16),
            pltpu.VMEM((tokens, width), jnp.bfloat16),
            pltpu.SemaphoreType.DMA((2 * (width // chunk) + 2,)),
        ],
        compiler_params=params(16),
        cost_estimate=cost(4 * experts * CAP * tokens * width, 4 * tokens * width),
        name="route_rows",
    )(in_hbm(ids), in_hbm(probs), in_hbm(act), in_hbm(cot))
    return out[:far], out[far]


def merge_kernel(far, *refs):
    pieces, outs = refs[:far], refs[len(refs) - refs[0].shape[0] :]
    for index, out in enumerate(outs):
        rows = [piece[index, :CAP, :] for piece in pieces]
        rows += [piece[index, CAP:, :] for piece in pieces]
        out[...] = jnp.concatenate(rows, axis=0)


def merge(pieces, after=()):
    far = len(pieces)
    near, _, width = pieces[0].shape
    return pl.pallas_call(
        functools.partial(merge_kernel, far),
        in_specs=[VMEM] * far + [pl.BlockSpec(memory_space=pl.ANY)] * len(after),
        out_specs=[VMEM] * near,
        out_shape=[bf16(2 * CAP * far, width)] * near,
        compiler_params=params(16),
        cost_estimate=cost(0, 8 * near * CAP * far * width),
        name="merge_rows",
    )(*pieces, *after)


def stack_kernel(number, *refs):
    pieces, outs = refs[:number], refs[number:]
    rows, width = pieces[0].shape[0] // 2, outs[0].shape[1]
    for half, out in enumerate(outs):
        at = slice(half * width, (half + 1) * width)
        picked = [piece[:rows, at] for piece in pieces] + [piece[rows:, at] for piece in pieces]
        out[...] = jnp.concatenate(picked, axis=0)


def stack(pieces):
    number = len(pieces)
    rows, width = pieces[0].shape
    return pl.pallas_call(
        functools.partial(stack_kernel, number),
        in_specs=[VMEM] * number,
        out_specs=[VMEM] * HALVES,
        out_shape=[bf16(number * rows, width // HALVES)] * HALVES,
        compiler_params=params(16),
        cost_estimate=cost(0, 4 * number * rows * width),
        name="stack_rows",
    )(*pieces)


def load_kernel(chunk, pair_hbm, down_hbm, after, pair, down, sems):
    del after
    width = down.shape[1]
    copies = []
    for step in range(width // chunk):
        at = pl.ds(step * chunk, chunk)
        copies += [
            pltpu.make_async_copy(pair_hbm.at[:, at, :], pair.at[:, at, :], sems.at[0, step]),
            pltpu.make_async_copy(down_hbm.at[:, at], down.at[:, at], sems.at[1, step]),
        ]
    for one in copies:
        one.start()
    for one in copies:
        one.wait()


def load(pair, down, after):
    units, width = down.shape
    chunk = min(1024, width)
    return pl.pallas_call(
        functools.partial(load_kernel, chunk),
        in_specs=[HBM] * 2 + [pl.BlockSpec(memory_space=pl.ANY)],
        out_specs=[VMEM] * 2,
        out_shape=[pltpu.VMEM(pair.shape, jnp.bfloat16), pltpu.VMEM(down.shape, jnp.bfloat16)],
        scratch_shapes=[pltpu.SemaphoreType.DMA((2, width // chunk))],
        compiler_params=params(28),
        cost_estimate=cost(0, 6 * width * units),
        name="load_weights",
    )(in_hbm(pair), in_hbm(down), after)


def gather_columns(near_rows, far_rows, near_at, far_at):
    pieces = [(ref, near_at) for ref in near_rows] + [(ref, far_at) for ref in far_rows]
    tok = [ref[: ref.shape[0] // 2, at] for ref, at in pieces]
    cot = [ref[ref.shape[0] // 2 :, at] for ref, at in pieces]
    return jnp.concatenate(tok, axis=0), jnp.concatenate(cot, axis=0)


def first_kernel(near, groups, chunk, *refs):
    near_rows, far_rows = refs[:near], refs[near : near + groups]
    pair, down, gate, up, hid, tok_all, cot_all = refs[near + groups :]
    for step in range(tok_all.shape[1] // chunk):
        at = slice(step * chunk, (step + 1) * chunk)
        tok, cot = gather_columns(near_rows, far_rows, at, at)
        tok_all[:, at] = tok
        cot_all[:, at] = cot
        part_gate = dot_nn(tok, pair[0, at, :])
        part_up = dot_nn(tok, pair[1, at, :])
        part_hid = dot_nt(cot, down[:, at])
        if step == 0:
            gate[...], up[...], hid[...] = part_gate, part_up, part_hid
        else:
            gate[...] += part_gate
            up[...] += part_up
            hid[...] += part_hid


def first_half(near_rows, far_rows, pair, down):
    near, groups = len(near_rows), len(far_rows)
    total = (near * near_rows[0].shape[0] + groups * far_rows[0].shape[0]) // 2
    half = far_rows[0].shape[1]
    units = down.shape[0]
    chunk = half
    return pl.pallas_call(
        functools.partial(first_kernel, near, groups, chunk),
        in_specs=[VMEM] * (near + groups + 2),
        out_specs=[VMEM] * 5,
        out_shape=[jax.ShapeDtypeStruct((total, units), jnp.float32)] * 3
        + [bf16(total, half)] * 2,
        compiler_params=params(24),
        cost_estimate=cost(6 * total * half * units, 6 * half * units),
        name="first_half",
    )(*near_rows, *far_rows, pair, down)


def second_kernel(homes, experts, near, groups, chunk, *refs):
    near_rows, far_rows = refs[:near], refs[near : near + groups]
    gate_sum, up_sum, hid_sum, pair, down = refs[near + groups : near + groups + 5]
    gate_out, up_out, hidden_out, tok_all, cot_all, parts_hbm = refs[
        near + groups + 5 : near + groups + 11
    ]
    parts, sems = refs[near + groups + 11 :]
    half, width = tok_all.shape[1], down.shape[1]
    there = slice(half, width)
    tok, cot = gather_columns(near_rows, far_rows, there, slice(0, half))
    tok_all[...] = tok
    cot_all[...] = cot
    pre_gate = gate_sum[...] + dot_nn(tok, pair[0, there, :])
    pre_up = up_sum[...] + dot_nn(tok, pair[1, there, :])
    hidden_grad = hid_sum[...] + dot_nt(cot, down[:, there])
    sigmoid_gate = jax.nn.sigmoid(pre_gate)
    activated = pre_gate * sigmoid_gate
    hidden_out[...] = (activated * pre_up).astype(jnp.bfloat16)
    gate_grad = (
        hidden_grad * pre_up * sigmoid_gate * (1.0 + pre_gate * (1.0 - sigmoid_gate))
    ).astype(jnp.bfloat16)
    up_grad = (hidden_grad * activated).astype(jnp.bfloat16)
    gate_out[...] = gate_grad
    up_out[...] = up_grad
    me, group = lax.axis_index("expert"), lax.axis_index("dp")
    rows = [
        lax.rem(group - back + groups, groups) * experts + (me ^ turn) for back, turn in homes
    ]
    copies = []
    for side in range(HALVES):
        for step in range(side * half // chunk, (side + 1) * half // chunk):
            at = slice(step * chunk, (step + 1) * chunk)
            value = dot_nt(gate_grad, pair[0, at, :]) + dot_nt(up_grad, pair[1, at, :])
            value = value.astype(jnp.bfloat16)
            for block, row in enumerate(rows):
                parts[row, :, at] = value[block * CAP : (block + 1) * CAP]
        where = pl.ds(side * half, half)
        one = pltpu.make_async_copy(
            parts.at[:, :, where], parts_hbm.at[:, :, where], sems.at[side]
        )
        one.start()
        copies.append(one)
    for one in copies:
        one.wait()


def second_half(near_rows, far_rows, sums, pair, down, homes, experts):
    near, groups = len(near_rows), len(far_rows)
    total, units = sums[0].shape
    half, width = far_rows[0].shape[1], down.shape[1]
    chunk = min(512, half)
    blocks = total // CAP
    return pl.pallas_call(
        functools.partial(second_kernel, homes, experts, near, groups, chunk),
        in_specs=[VMEM] * (near + groups + 5),
        out_specs=[VMEM] * 5 + [HBM],
        out_shape=[bf16(total, units)] * 3
        + [bf16(total, half)] * 2
        + [pltpu.HBM((blocks, CAP, width), jnp.bfloat16)],
        scratch_shapes=[
            pltpu.VMEM((blocks, CAP, width), jnp.bfloat16),
            pltpu.SemaphoreType.DMA((HALVES,)),
        ],
        compiler_params=params(24),
        cost_estimate=cost(7 * total * width * units, 6 * width * units),
        name="second_half",
    )(*near_rows, *far_rows, *sums, pair, down)


def pair_grad_kernel(blocks, chunk, *refs):
    toks, gate_ref, up_ref = refs[:blocks], refs[blocks], refs[blocks + 1]
    half = toks[0].shape[1]
    out_hbm, buffer, sems = refs[blocks + 2 :]
    copies = []
    for step in range(blocks * half // chunk):
        at = slice(step * chunk, (step + 1) * chunk)
        tok = toks[step * chunk // half][:, step * chunk % half : step * chunk % half + chunk]
        for side, ref in enumerate((gate_ref, up_ref)):
            buffer[side, at, :] = dot_tn(tok, ref[...]).astype(jnp.bfloat16)
        where = pl.ds(step * chunk, chunk)
        one = pltpu.make_async_copy(
            buffer.at[:, where, :], out_hbm.at[0, :, where, :], sems.at[step]
        )
        one.start()
        copies.append(one)
    for one in copies:
        one.wait()


def pair_grad(toks, gate_grad, up_grad):
    blocks = len(toks)
    width = blocks * toks[0].shape[1]
    total, units = gate_grad.shape
    chunk = min(512, width // blocks)
    return pl.pallas_call(
        functools.partial(pair_grad_kernel, blocks, chunk),
        in_specs=[VMEM] * (blocks + 2),
        out_specs=HBM,
        out_shape=bf16(1, 2, width, units),
        scratch_shapes=[
            pltpu.VMEM((2, width, units), jnp.bfloat16),
            pltpu.SemaphoreType.DMA((width // chunk,)),
        ],
        compiler_params=params(32),
        cost_estimate=cost(4 * total * width * units, 4 * width * units),
        name="pair_grad",
    )(*toks, gate_grad, up_grad)


def down_grad_kernel(blocks, chunk, *refs):
    cots, hidden_ref, out_hbm = refs[:blocks], refs[blocks], refs[blocks + 1]
    buffer, sems = refs[blocks + 2 :]
    half = cots[0].shape[1]
    copies = []
    for step in range(blocks * half // chunk):
        at = slice(step * chunk, (step + 1) * chunk)
        cot = cots[step * chunk // half][:, step * chunk % half : step * chunk % half + chunk]
        buffer[:, at] = dot_tn(hidden_ref[...], cot).astype(jnp.bfloat16)
        where = pl.ds(step * chunk, chunk)
        one = pltpu.make_async_copy(buffer.at[:, where], out_hbm.at[0, :, where], sems.at[step])
        one.start()
        copies.append(one)
    for one in copies:
        one.wait()


def down_grad(cots, hidden):
    blocks = len(cots)
    width = blocks * cots[0].shape[1]
    total, units = hidden.shape
    chunk = min(1024, width // blocks)
    return pl.pallas_call(
        functools.partial(down_grad_kernel, blocks, chunk),
        in_specs=[VMEM] * (blocks + 1),
        out_specs=HBM,
        out_shape=bf16(1, units, width),
        scratch_shapes=[
            pltpu.VMEM((units, width), jnp.bfloat16),
            pltpu.SemaphoreType.DMA((width // chunk,)),
        ],
        compiler_params=params(24),
        cost_estimate=cost(2 * total * width * units, 2 * width * units),
        name="down_grad",
    )(*cots, hidden)


def spread_kernel(chunk, rows_ref, place_ref, out_hbm, buffer, sems):
    blocks, _, width = rows_ref.shape
    place = jnp.concatenate([place_ref[...]] * (blocks * CAP // place_ref.shape[0]), axis=0)
    copies = []
    for step in range(width // chunk):
        at = slice(step * chunk, (step + 1) * chunk)
        rows = jnp.concatenate([rows_ref[block, :, at] for block in range(blocks)], axis=0)
        buffer[:, at] = dot_tn(place, rows).astype(jnp.bfloat16)
        where = pl.ds(step * chunk, chunk)
        one = pltpu.make_async_copy(buffer.at[:, where], out_hbm.at[:, where], sems.at[step])
        one.start()
        copies.append(one)
    for one in copies:
        one.wait()


def spread(rows, place):
    width = rows.shape[2]
    slots, tokens = place.shape
    chunk = width // HALVES
    return pl.pallas_call(
        functools.partial(spread_kernel, chunk),
        in_specs=[VMEM] * 2,
        out_specs=HBM,
        out_shape=bf16(tokens, width),
        scratch_shapes=[
            pltpu.VMEM((tokens, width), jnp.bfloat16),
            pltpu.SemaphoreType.DMA((width // chunk,)),
        ],
        compiler_params=params(16),
        cost_estimate=cost(2 * slots * tokens * width, 2 * tokens * width),
        name="spread_rows",
    )(rows, place)


def per_device(activations, cotangent, expert_ids, gate_probs, gate_up, down_proj):
    experts = lax.axis_size("expert")
    groups = lax.axis_size("dp")
    tokens = activations.shape[0]
    far, near = factors(experts)

    def send(value, by_group, by_expert):
        if by_group == 0 and by_expert == 0:
            return value
        pairs = []
        for group in range(groups):
            to = (group + by_group) % groups
            for i in range(experts):
                pairs.append((group * experts + i, to * experts + (i ^ by_expert)))
        return lax.ppermute(value, ("dp", "expert"), pairs)

    pieces, place = route(
        expert_ids.reshape(1, tokens),
        gate_probs.reshape(1, tokens),
        activations,
        cotangent,
        experts,
    )
    pair, down = load(gate_up[0], down_proj[0], place)
    arrived = [send(pieces[high], 0, high * near) for high in range(far)]
    early, late = range(far // 2), range(far // 2, far)
    first = [send(pieces[high], group, high * near) for group in range(1, groups) for high in early]
    first = merge([arrived[high] for high in early] + first)
    loaded = pltpu.with_memory_space_constraint(down, pltpu.VMEM)
    second = merge([arrived[high] for high in late], (loaded,))
    mine = [send(second[low], 0, low) for low in range(near)]
    halves = stack(mine)
    near_rows = [send(first[low], 0, low) for low in range(near)]
    far_rows = [[send(half, group, 0) for group in range(groups)] for half in halves]
    homes = [
        (group, high * near + low)
        for low in range(near)
        for group in range(groups)
        for high in early
    ]
    homes += [
        (group, high * near + low)
        for group in range(groups)
        for low in range(near)
        for high in late
    ]
    pair = pltpu.with_memory_space_constraint(pair, pltpu.VMEM)
    *sums, tok_first, cot_first = first_half(near_rows, far_rows[0], pair, loaded)
    gate_grad, up_grad, hidden, tok_second, cot_second, parts = second_half(
        near_rows, far_rows[1], sums, pair, loaded, homes, experts
    )
    returned = lax.all_to_all(parts, ("dp", "expert"), split_axis=0, concat_axis=0, tiled=True)
    down_total = down_grad([cot_first, cot_second], hidden)
    pair_total = pair_grad([tok_first, tok_second], gate_grad, up_grad)
    input_grad = spread(returned, place)
    return input_grad, pair_total, down_total


def solution(mesh):
    rows = P(("dp", "expert"), None)
    pair, down = P("expert", None, None, "dp"), P("expert", "dp", None)
    return jax.shard_map(
        per_device,
        mesh=mesh,
        in_specs=(rows, rows, rows, rows, pair, down),
        out_specs=(rows, pair, down),
        check_vma=False,
    )
```
